32 devices in a mesh: dp: 8 (over y, x, core), mp: 4 (over z).
Axes of the slice: x: 2, y: 2, z: 4, core: 2. Of those that a mesh axis runs over, the one named last changes fastest.
Arguments:
- samples: bfloat16 [64, 55, 128], P('dp'), may hold values from -6 to 6
- targets: bfloat16 [64, 53, 128], P('dp'), may hold values from -6 to 6
- counts: int32 [8], P('dp'), may hold values from 1 to 7, as said below
- weight_in: float32 [55, 2048], P(None, ('mp', 'dp')), may hold values from -0.875 to 0.875
- weight_mid: float32 [2048, 2048], P('mp', 'dp'), may hold values from -0.125 to 0.125
- weight_top: float32 [2048, 2048], P('dp', 'mp'), may hold values from -0.125 to 0.125
- weight_out: float32 [2048, 53], P(('mp', 'dp')), may hold values from -0.125 to 0.125
- moment_in: float32 [55, 2048], P(None, ('mp', 'dp')), may hold values from -0.15625 to 0.15625
- moment_mid: float32 [2048, 2048], P('mp', 'dp'), may hold values from -0.15625 to 0.15625
- moment_top: float32 [2048, 2048], P('dp', 'mp'), may hold values from -0.15625 to 0.15625
- moment_out: float32 [2048, 53], P(('mp', 'dp')), may hold values from -0.15625 to 0.15625
Outputs:
- new_in: float32 [55, 2048], P(None, ('mp', 'dp'))
- new_mid: float32 [2048, 2048], P('mp', 'dp')
- new_top: float32 [2048, 2048], P('dp', 'mp')
- new_out: float32 [2048, 53], P(('mp', 'dp'))
- mom_in: float32 [55, 2048], P(None, ('mp', 'dp'))
- mom_mid: float32 [2048, 2048], P('mp', 'dp')
- mom_top: float32 [2048, 2048], P('dp', 'mp')
- mom_out: float32 [2048, 53], P(('mp', 'dp'))
The draws below stay inside these ranges and needn't reach their ends.
Inputs may be any that keep to these rules, and one draw needn't show every extreme that they name: Partition p and partition (p + 4) mod 8 form a matched pair whose counts sum to at most 8; some partition has 7.
All inputs are finite; a program needn't handle non-finite values.
Results may differ from the reference program's by a relative error of at most 0.011.
Values may be sent and summed in bfloat16 or wider, within the bound.
No kernel may reach another device: no remote copies, remote signals or barrier semaphores. Data moves between devices by JAX's collectives and lax.ppermute only.
A program may use at most 64 MiB of HBM per device.

```python
import math
import jax
import jax.numpy as jnp
from jax import lax

IN = 55
OUT = 53
H = 2048
BLOCK = 128
BLK_DEV = 8
CAP = 4
NBLK = 64
N_DP = 8
N_MP = 4


def draw_counts(key, part):
    pairs = N_DP // 2
    totals = jax.random.randint(jax.random.fold_in(key, 12), (pairs,), 2, 2 * CAP + 1)
    totals = totals.at[0].set(2 * CAP)
    spread = totals // 2
    lower = (totals + 1) // 2
    picks = jax.random.randint(jax.random.fold_in(key, 13), (pairs,), 0, 1 << 20)
    heavy = lower + picks % spread
    heavy = heavy.at[0].set(2 * CAP - 1)
    light = totals - heavy
    flips = jax.random.randint(jax.random.fold_in(key, 14), (pairs,), 0, 2)
    low_half = jnp.where(flips == 1, heavy, light)
    high_half = jnp.where(flips == 1, light, heavy)
    return jnp.concatenate([low_half, high_half]).astype(jnp.int32)


def steps_of(rng, shape, split, smallest, largest):
    level = 1.0
    for axis_at, shards_of in split:
        draws = jax.random.uniform(jax.random.fold_in(jax.random.fold_in(rng, 6), axis_at), (shards_of,), jnp.float32, smallest / len(split), largest / len(split))
        level = level * jnp.repeat(jnp.exp(draws), shape[axis_at] // shards_of).reshape((-1,) + (1,) * (len(shape) - 1 - axis_at))
    return level


def scatter_about(rng, dims, scale, bound, pieces=(), kind=jnp.bfloat16):
    result = jax.random.normal(rng, dims, jnp.float32) * scale
    if len(pieces) > 0:
        result = steps_of(rng, dims, pieces, -0.22, 0.18) * result
    return jnp.clip(result, min=-bound, max=bound).astype(kind)


def setup_inputs(seed: int = 0) -> dict:
    splits = jax.random.split(jax.random.key(seed), 12)
    return {
        "samples": scatter_about(splits[0], (NBLK, IN, BLOCK), 1.0, 6.0, ((0, 8),)),
        "targets": scatter_about(splits[1], (NBLK, OUT, BLOCK), 1.0, 6.0, ((0, 8),)),
        "counts": draw_counts(jax.random.fold_in(splits[11], 71), 0),
        "weight_in": scatter_about(splits[3], (IN, H), IN ** -0.5, 0.875, ((1, 32),), jnp.float32),
        "weight_mid": scatter_about(splits[4], (H, H), H ** -0.5, 0.125, ((0, 4), (1, 8)), jnp.float32),
        "weight_top": scatter_about(splits[5], (H, H), H ** -0.5, 0.125, ((0, 8), (1, 4)), jnp.float32),
        "weight_out": scatter_about(splits[6], (H, OUT), H ** -0.5, 0.125, ((0, 32),), jnp.float32),
        "moment_in": scatter_about(splits[7], (IN, H), 0.01, 0.15625, ((1, 32),), jnp.float32),
        "moment_mid": scatter_about(splits[8], (H, H), 0.01, 0.15625, ((0, 4), (1, 8)), jnp.float32),
        "moment_top": scatter_about(splits[9], (H, H), 0.01, 0.15625, ((0, 8), (1, 4)), jnp.float32),
        "moment_out": scatter_about(splits[10], (H, OUT), 0.01, 0.15625, ((0, 32),), jnp.float32),
    }


momentum_decay = 0.9
learn_rate = 0.05

def gelu_act(value):
    return 0.5 * value * (1.0 + jax.scipy.special.erf(value / math.sqrt(2.0)))

def gelu_slope(value):
    return 0.5 * (1.0 + jax.scipy.special.erf(value / math.sqrt(2.0))) + value * jnp.exp(-0.5 * value * value) / math.sqrt(2.0 * math.pi)

def split_sum(left, right):
    width = left.shape[1] // N_MP
    summed = jnp.zeros((left.shape[0], right.shape[1]), jnp.float32)
    for group in range(N_MP):
        part = jnp.dot(left[:, group * width:(group + 1) * width], right[group * width:(group + 1) * width], preferred_element_type=jnp.float32)
        rounded = lax.optimization_barrier(part.astype(jnp.bfloat16))
        summed = summed + rounded.astype(jnp.float32)
    return summed

def reference(samples, targets, counts, weight_in, weight_mid, weight_top, weight_out, moment_in, moment_mid, moment_top, moment_out):
    inputs = jnp.transpose(samples, (0, 2, 1)).reshape(-1, IN)
    wanted = jnp.transpose(targets, (0, 2, 1)).reshape(-1, OUT).astype(jnp.float32)
    slots = jnp.arange(NBLK, dtype=jnp.int32)
    live = (slots % BLK_DEV < jnp.repeat(counts, BLK_DEV)).astype(jnp.float32)
    row_live = jnp.repeat(live, BLOCK)
    total = jnp.sum(counts).astype(jnp.float32) * BLOCK
    first = weight_in.astype(jnp.bfloat16)
    second = weight_mid.astype(jnp.bfloat16)
    third = weight_top.astype(jnp.bfloat16)
    fourth = weight_out.astype(jnp.bfloat16)
    pre_one = jnp.dot(inputs, first, preferred_element_type=jnp.float32)
    act_one = gelu_act(pre_one).astype(jnp.bfloat16)
    pre_two = split_sum(act_one, second)
    act_two = gelu_act(pre_two).astype(jnp.bfloat16)
    pre_three = jnp.dot(act_two, third, preferred_element_type=jnp.float32)
    act_three = gelu_act(pre_three).astype(jnp.bfloat16)
    predicted = split_sum(act_three, fourth)
    grad_pred = (2.0 / total * (predicted - wanted) * row_live[:, None]).astype(jnp.bfloat16)
    grad_four = jnp.dot(act_three.T, grad_pred, preferred_element_type=jnp.float32)
    delta_three = (jnp.dot(grad_pred, fourth.T, preferred_element_type=jnp.float32) * gelu_slope(pre_three)).astype(jnp.bfloat16)
    grad_three = jnp.dot(act_two.T, delta_three, preferred_element_type=jnp.float32)
    delta_two = (split_sum(delta_three, third.T) * gelu_slope(pre_two)).astype(jnp.bfloat16)
    grad_two = jnp.dot(act_one.T, delta_two, preferred_element_type=jnp.float32)
    delta_one = (jnp.dot(delta_two, second.T, preferred_element_type=jnp.float32) * gelu_slope(pre_one)).astype(jnp.bfloat16)
    grad_one = jnp.dot(inputs.T, delta_one, preferred_element_type=jnp.float32)
    mom_in = momentum_decay * moment_in + grad_one
    mom_mid = momentum_decay * moment_mid + grad_two
    mom_top = momentum_decay * moment_top + grad_three
    mom_out = momentum_decay * moment_out + grad_four
    return (weight_in - learn_rate * mom_in, weight_mid - learn_rate * mom_mid, weight_top - learn_rate * mom_top, weight_out - learn_rate * mom_out, mom_in, mom_mid, mom_top, mom_out)
```

```python
import math

import jax
import jax.numpy as jnp
from jax import lax
from jax.sharding import PartitionSpec as P

momentum_decay = 0.9
learn_rate = 0.05
bf16 = jnp.bfloat16
f32 = jnp.float32


def swap(value, axis, step):
    count = lax.axis_size(axis)
    return lax.ppermute(value, axis, [(at, at ^ step) for at in range(count)])


def gelu_act(value):
    return 0.5 * value * (1.0 + jax.scipy.special.erf(value / math.sqrt(2.0)))


def gelu_slope(value):
    return 0.5 * (1.0 + jax.scipy.special.erf(value / math.sqrt(2.0))) + value * jnp.exp(
        -0.5 * value * value
    ) / math.sqrt(2.0 * math.pi)


def dot(left, right, contract):
    return lax.dot_general(left, right, (contract, ((), ())), preferred_element_type=f32)


def fit(value, lanes):
    return jnp.pad(value, ((0, 0), (0, lanes - value.shape[1])))


def on_device(
    samples,
    targets,
    counts,
    weight_in,
    weight_mid,
    weight_top,
    weight_out,
    moment_in,
    moment_mid,
    moment_top,
    moment_out,
):
    slots, n_in, block = samples.shape
    n_out = targets.shape[1]
    n_dp, n_mp = lax.axis_size("dp"), lax.axis_size("mp")
    dp_at, mp_at = lax.axis_index("dp"), lax.axis_index("mp")
    half = n_dp // 2
    per = slots // n_mp
    rows = per * block // 2
    wide = weight_in.shape[1]
    lanes = max(rows, 2 * wide)
    high = dp_at >= half
    planes = range(n_mp)

    n_small = n_in + 1
    piece = jnp.concatenate(
        [
            jnp.pad(weight_in.astype(bf16), ((0, n_small - n_in), (0, 0))),
            jnp.pad(weight_out.astype(bf16).T, ((0, n_small - n_out), (0, 0))),
        ],
        1,
    )
    pieces = [piece] + [swap(piece, "mp", k) for k in planes[1:]]
    mid = weight_mid.astype(bf16)
    top = weight_top.astype(bf16)
    second = [mid] + [swap(mid, "mp", k) for k in planes[1:]]

    own = []
    for j in range(per):
        at = per * mp_at + j
        slot = jnp.where(high, slots - 1 - at, at)
        keep = slot < counts[0]
        x = lax.dynamic_index_in_dim(samples, slot, 0, False)
        y = lax.dynamic_index_in_dim(targets, slot, 0, False)
        number = jnp.broadcast_to(counts[0].astype(bf16), (1, block))
        lit = jnp.broadcast_to(keep.astype(bf16), (1, block))
        x = jnp.where(keep, x, jnp.zeros_like(x))
        y = jnp.where(keep, y, jnp.zeros_like(y))
        own.append(jnp.concatenate([x, number, y, lit], 0))
    mine = jnp.concatenate(own, 1)
    n_rows = mine.shape[0]
    mine = mine.reshape(n_rows, 2, rows)
    mine = jnp.concatenate([mine[:, 0], mine[:, 1]], 0)
    n_piece = n_mp * n_small
    sent = jnp.concatenate([fit(mine, lanes)] + [fit(p, lanes) for p in pieces], 0)
    got = swap(sent, "dp", half)
    pair = sent[: 2 * n_rows, :rows] + got[: 2 * n_rows, :rows]
    first_half, second_half = pair[:n_rows], pair[n_rows:]
    at_home = jnp.where(high, second_half, first_half)
    away = jnp.where(high, first_half, second_half)
    wanted = at_home[n_small : n_small + n_out]
    live = at_home[n_small + n_out :].astype(f32)

    def both(bit, held, other):
        return [jnp.where(bit, other, held), jnp.where(bit, held, other)]

    held_x = {0: at_home[:n_small], half: away[:n_small]}
    held_p = both(high, sent[2 * n_rows :, : 2 * wide], got[2 * n_rows :, : 2 * wide])
    step = 1
    while step < half:
        keys = list(held_x)
        sent = jnp.concatenate(
            [fit(held_x[k], lanes) for k in keys] + [fit(p, lanes) for p in held_p], 0
        )
        got = swap(sent, "dp", step)
        got_x = got[: len(keys) * n_small, :rows]
        for i, k in enumerate(keys):
            held_x[k | step] = got_x[i * n_small : (i + 1) * n_small]
        got_p = got[len(keys) * n_small :, : 2 * wide]
        bit = (dp_at & step) != 0
        others = [got_p[i * n_piece : (i + 1) * n_piece] for i in range(len(held_p))]
        pairs = [both(bit, a, b) for a, b in zip(held_p, others)]
        held_p = [p[0] for p in pairs] + [p[1] for p in pairs]
        step *= 2
    order = []
    for at in range(n_dp):
        low = at & (half - 1)
        order.append(low * 2 + (at >= half))
    first, fourth = [], []
    for k in planes:
        cut = [held_p[o][k * n_small : (k + 1) * n_small] for o in order]
        first.append(jnp.concatenate([c[:n_in, :wide] for c in cut], 1))
        fourth.append(jnp.concatenate([c[:n_out, wide:] for c in cut], 1))
    fourth = jnp.concatenate(fourth, 1)

    blocks = [k for k in range(n_dp) if k % 2 == 0] + [k for k in range(n_dp) if k % 2 == 1]
    inputs = jnp.concatenate([held_x[k][:n_in] for k in blocks], 1)
    pair_counts = jnp.concatenate([held_x[k][n_in:, :1] for k in range(half)], 0)
    total = jnp.sum(pair_counts.astype(f32)) * block

    pre_one = [dot(inputs, b, ((0,), (0,))) for b in first]
    act_one = [gelu_act(a).astype(bf16) for a in pre_one]
    pre_two = sum(dot(a, b, ((1,), (0,))) for a, b in zip(act_one, second))
    act_two = gelu_act(pre_two).astype(bf16)
    third = [top] + [swap(top, "mp", k) for k in planes[1:]]
    third = jnp.concatenate(third, 1)

    kept = half * rows
    away_sum = dot(act_two[kept:], third, ((1,), (0,))).astype(bf16)
    home_sum = dot(act_two[:kept], third, ((1,), (0,)))
    core_sum = home_sum + swap(away_sum, "dp", 1).astype(f32)
    pre_three = core_sum[:rows]
    core_sum = core_sum.astype(bf16)
    for i in range(1, half):
        pre_three = pre_three + swap(core_sum[i * rows : (i + 1) * rows], "dp", 2 * i).astype(f32)
    act_three = gelu_act(pre_three).astype(bf16)
    predicted = dot(fourth, act_three, ((1,), (1,)))
    grad_pred = (2.0 / total * (predicted - wanted.astype(f32)) * live).astype(bf16)
    grad_four = dot(grad_pred, act_three, ((1,), (0,)))
    delta_three = (dot(grad_pred, fourth, ((0,), (0,))) * gelu_slope(pre_three)).astype(bf16)
    deltas = [delta_three] + [swap(delta_three, "dp", 2 * i) for i in range(1, half)]
    deltas = jnp.concatenate(deltas, 0)
    deltas = jnp.concatenate([deltas, swap(deltas, "dp", 1)], 0)

    n_top = top.shape[1]
    sum_two = dot(deltas, third, ((1,), (1,)))
    delta_two = (sum_two * gelu_slope(pre_two)).astype(bf16)
    grad_three = dot(act_two, deltas, ((0,), (0,)))
    sum_three = grad_three[:, :n_top]
    for k in planes[1:]:
        sent = grad_three[:, k * n_top : (k + 1) * n_top].astype(bf16)
        sum_three = sum_three + swap(sent, "mp", k).astype(f32)
    sum_mid = None
    small = None
    for k in planes:
        grad_two = dot(act_one[k], delta_two, ((0,), (0,)))
        delta_one = (dot(delta_two, second[k], ((1,), (1,))) * gelu_slope(pre_one[k])).astype(bf16)
        grad_one = dot(inputs, delta_one, ((1,), (0,)))
        both_small = jnp.concatenate([grad_one, grad_four[:, k * n_top : (k + 1) * n_top]], 0)
        if k == 0:
            sum_mid, small = grad_two, both_small
        else:
            sum_mid = sum_mid + swap(grad_two.astype(bf16), "mp", k).astype(f32)
            small = small + swap(both_small.astype(bf16), "mp", k).astype(f32)
    small = small.astype(bf16).reshape(n_in + n_out, n_dp, wide).transpose(1, 0, 2)
    small = jnp.sum(lax.all_to_all(small, "dp", 0, 0, tiled=True).astype(f32), 0)

    mom_in = momentum_decay * moment_in + small[:n_in]
    mom_mid = momentum_decay * moment_mid + sum_mid
    mom_top = momentum_decay * moment_top + sum_three
    mom_out = momentum_decay * moment_out + small[n_in:].T
    return (
        weight_in - learn_rate * mom_in,
        weight_mid - learn_rate * mom_mid,
        weight_top - learn_rate * mom_top,
        weight_out - learn_rate * mom_out,
        mom_in,
        mom_mid,
        mom_top,
        mom_out,
    )


def solution(mesh):
    in_specs = (
        P("dp", None, None),
        P("dp", None, None),
        P("dp"),
        P(None, ("mp", "dp")),
        P("mp", "dp"),
        P("dp", "mp"),
        P(("mp", "dp"), None),
        P(None, ("mp", "dp")),
        P("mp", "dp"),
        P("dp", "mp"),
        P(("mp", "dp"), None),
    )
    out_specs = (
        P(None, ("mp", "dp")),
        P("mp", "dp"),
        P("dp", "mp"),
        P(("mp", "dp"), None),
        P(None, ("mp", "dp")),
        P("mp", "dp"),
        P("dp", "mp"),
        P(("mp", "dp"), None),
    )
    return jax.shard_map(
        on_device, mesh=mesh, in_specs=in_specs, out_specs=out_specs, check_vma=False
    )
```

```python
import functools
import math

import jax
import jax.numpy as jnp
from jax import lax
from jax.experimental import pallas as pl
from jax.experimental.pallas import tpu as pltpu
from jax.sharding import PartitionSpec as P

momentum_decay = 0.9
learn_rate = 0.05
bf16 = jnp.bfloat16
f32 = jnp.float32
VMEM_BYTES = 24 << 20


def swap(value, axis, step):
    count = lax.axis_size(axis)
    return lax.ppermute(value, axis, [(at, at ^ step) for at in range(count)])


def parent(k):
    return k & (k - 1)


def low_bit(k):
    return k & -k


def up_to(value, unit):
    return -(-value // unit) * unit


def gelu_act(value):
    return 0.5 * value * (1.0 + lax.erf(value * math.sqrt(0.5)))


def gelu_slope(value):
    return 0.5 * (1.0 + lax.erf(value * math.sqrt(0.5))) + value * jnp.exp(
        -0.5 * value * value
    ) * (1.0 / math.sqrt(2.0 * math.pi))


def dot(left, right, at_left, at_right):
    dims = (((at_left,), (at_right,)), ((), ()))
    return lax.dot_general(left, right, dims, preferred_element_type=f32)


def shaped(dims, kind):
    return jax.ShapeDtypeStruct(dims, kind)


def on_core(body, outs, args, name, flops=0, scratch=(), scalars=()):
    at = pl.BlockSpec(memory_space=pltpu.VMEM)
    return pl.pallas_call(
        body,
        out_shape=outs,
        in_specs=[pl.BlockSpec(memory_space=pltpu.SMEM)] * len(scalars) + [at] * len(args),
        out_specs=jax.tree.map(lambda _: at, outs),
        scratch_shapes=list(scratch),
        compiler_params=pltpu.CompilerParams(vmem_limit_bytes=VMEM_BYTES),
        cost_estimate=pl.CostEstimate(flops=flops, bytes_accessed=0, transcendentals=0),
        name=name,
    )(*scalars, *args)


def pack_small(w_in, w_out, out, *, tall):
    n_in, wide = w_in.shape
    n_out = w_out.shape[0]
    left = jnp.concatenate([w_in[...], jnp.zeros((tall - n_in, wide), f32)], 0)
    right = jnp.concatenate([w_out[...], jnp.zeros((tall - n_out, wide), f32)], 0)
    parts = [left, right]
    spare = out.shape[1] - 2 * wide
    if spare:
        parts.append(jnp.zeros((tall, spare), f32))
    out[...] = jnp.concatenate(parts, 1).astype(bf16)


def pack_rows(count, samples, targets, *refs, tall, rows, per):
    pieces, out = refs[:-1], refs[-1]
    slots, n_in, block = samples.shape
    n_out = targets.shape[1]
    half = lax.axis_size("dp") // 2
    high = lax.axis_index("dp") >= half
    mine = []
    for j in range(per):
        at = per * lax.axis_index("mp") + j
        slot = jnp.where(high, slots - 1 - at, at)
        keep = slot < count[0]
        x = samples[slot].astype(f32)
        y = targets[slot].astype(f32)
        x = jnp.where(keep, x, jnp.zeros_like(x))
        y = jnp.where(keep, y, jnp.zeros_like(y))
        number = jnp.full((1, block), count[0].astype(f32))
        lit = jnp.where(keep, jnp.ones((1, block), f32), jnp.zeros((1, block), f32))
        parts = [x, number]
        if tall > n_in + 1:
            parts.append(jnp.zeros((tall - n_in - 1, block), f32))
        parts += [y, lit]
        if tall > n_out + 1:
            parts.append(jnp.zeros((tall - n_out - 1, block), f32))
        mine.append(jnp.concatenate(parts, 0).astype(bf16))
    if per > 1:
        mine = jnp.concatenate(mine, 1)
    else:
        mine = mine[0]
    spare = out.shape[1] - rows
    for t in range(2):
        half_rows = mine[:, t * rows : (t + 1) * rows]
        if spare:
            half_rows = jnp.concatenate([half_rows, jnp.zeros((2 * tall, spare), bf16)], 1)
        out[2 * tall * t : 2 * tall * (t + 1)] = half_rows
    for i, piece in enumerate(pieces):
        out[4 * tall + i * tall : 4 * tall + (i + 1) * tall] = piece[...]


def in_order(bit, own, got, out, base):
    span = own.shape[0]
    out[base : base + span] = jnp.where(bit, got, own)
    out[base + span : base + 2 * span] = jnp.where(bit, own, got)


def first_step(own, got, out, wanted, *, tall):
    half = lax.axis_size("dp") // 2
    high = lax.axis_index("dp") >= half
    front = own[: 2 * tall] + got[: 2 * tall]
    back = own[2 * tall : 4 * tall] + got[2 * tall : 4 * tall]
    home = jnp.where(high, back, front)
    away = jnp.where(high, front, back)
    out[:tall] = home[:tall]
    out[tall : 2 * tall] = away[:tall]
    wanted[...] = home[tall:, : wanted.shape[1]]
    in_order(high, own[4 * tall :], got[4 * tall :], out, 2 * tall)


def next_step(own, got, out, *, step, span):
    bit = (lax.axis_index("dp") & step) != 0
    out[:span] = own[:span]
    out[span : 2 * span] = got[:span]
    in_order(bit, own[span:], got[span:], out, 2 * span)


def place_small(own, got, inputs, first, fourth, *, step, span, tall, rows, wide, order):
    n_dp, n_mp = lax.axis_size("dp"), lax.axis_size("mp")
    bit = (lax.axis_index("dp") & step) != 0
    count = span // tall
    for place, at in enumerate(order):
        source = own if at < count else got
        row = (at % count) * tall
        inputs[:, place * rows : (place + 1) * rows] = source[row : row + tall, :rows]
    own_p, got_p = own[span:], got[span:]
    low_p = jnp.where(bit, got_p, own_p).reshape(-1, tall, own.shape[1])
    high_p = jnp.where(bit, own_p, got_p).reshape(-1, tall, own.shape[1])
    half = n_dp // 2
    n_low = half // 2 * 2
    for k in range(n_mp):
        ones, fours = [], []
        for at in range(n_dp):
            low = at & (half - 1)
            where = low * 2 + (at >= half)
            if where < n_low:
                piece = low_p[where * n_mp + k]
            else:
                piece = high_p[(where - n_low) * n_mp + k]
            ones.append(piece[:, :wide])
            fours.append(piece[:, wide : 2 * wide])
        hidden = n_dp * wide
        first[:, k * hidden : (k + 1) * hidden] = jnp.concatenate(ones, 1)
        fourth[:, k * hidden : (k + 1) * hidden] = jnp.concatenate(fours, 1)


def one_forward(inputs, first, out, *, tile):
    n_rows = inputs.shape[1]
    cut = min(256, n_rows)

    def step(i, _):
        at = pl.ds(pl.multiple_of(i * tile, tile), tile)
        weights = first[:, at].T
        for c in range(0, n_rows, cut):
            pre = dot(weights, inputs[:, c : c + cut], 1, 0)
            out[at, c : c + cut] = gelu_act(pre).astype(bf16)
        return 0

    lax.fori_loop(0, first.shape[1] // tile, step, 0)


def one_slope(inputs, first, out, *, tile):
    n_rows = inputs.shape[1]
    cut = min(256, n_rows)

    def step(i, _):
        at = pl.ds(pl.multiple_of(i * tile, tile), tile)
        weights = first[:, at].T
        for c in range(0, n_rows, cut):
            pre = dot(weights, inputs[:, c : c + cut], 1, 0)
            out[at, c : c + cut] = gelu_slope(pre).astype(bf16)
        return 0

    lax.fori_loop(0, first.shape[1] // tile, step, 0)


def two_forward(act_one, *refs):
    seconds, (act, act_t, slope) = refs[:-3], refs[-3:]
    n_rows = act_one.shape[1]
    cut = min(256, n_rows)
    span = seconds[0].shape[0]
    turned = [s[...].T for s in seconds]
    for c in range(0, n_rows, cut):
        at = slice(c, c + cut)
        pre = dot(turned[0], act_one[:span, at], 1, 0)
        for k in range(1, len(seconds)):
            pre = pre + dot(turned[k], act_one[k * span : (k + 1) * span, at], 1, 0)
        value = gelu_act(pre)
        act_t[:, at] = value.astype(bf16)
        act[at] = value.T.astype(bf16)
        slope[:, at] = gelu_slope(pre)


def three_away(act, *refs, kept):
    thirds, out = refs[:-1], refs[-1]
    span = thirds[0].shape[1]
    for k, third in enumerate(thirds):
        out[:, k * span : (k + 1) * span] = dot(act[kept:], third[...], 1, 0).astype(bf16)


def three_home(act, got, *refs, kept, rows):
    half = kept // rows
    thirds, own, sends = refs[:-half], refs[-half], refs[len(refs) - half + 1 :]
    span = thirds[0].shape[1]
    for k, third in enumerate(thirds):
        at = slice(k * span, (k + 1) * span)
        total = dot(act[:kept], third[...], 1, 0) + got[:, at].astype(f32)
        own[:, at] = total[:rows]
        for i, send in enumerate(sends):
            send[:, at] = total[(i + 1) * rows : (i + 2) * rows].astype(bf16)


def error_step(inputs, wanted, fourth, *refs, groups, half, per, n_in, n_out):
    terms = refs[: groups * half]
    act, pre = refs[-2:]
    deltas, grad_four = refs[groups * half : groups * half + groups], refs[-3]
    width = pre.shape[1] // groups
    for g in range(groups):
        at = slice(g * width, (g + 1) * width)
        own, others = terms[g * half], terms[g * half + 1 : (g + 1) * half]
        total = own[...]
        for other in others:
            total = total + other[...].astype(f32)
        pre[:, at] = total
        act[:, at] = gelu_act(total).astype(bf16)
    predicted = dot(fourth[...], act[...], 1, 1)
    number = jnp.sum(inputs[n_in : n_in + 1, :].astype(f32), axis=1, keepdims=True) / per
    live = wanted[n_out : n_out + 1, :].astype(f32)
    error = (2.0 / number * (predicted - wanted[...].astype(f32)) * live).astype(bf16)
    row = lax.broadcasted_iota(jnp.int32, error.shape, 0)
    error = jnp.where(row < n_out, error, jnp.zeros_like(error))
    grad_four[...] = dot(error, act[...], 1, 0)
    turned = error.astype(f32).T.astype(bf16)
    for g in range(groups):
        at = slice(g * width, (g + 1) * width)
        delta = dot(turned, fourth[:, at], 1, 0) * gelu_slope(pre[:, at])
        deltas[g][...] = delta.astype(bf16)


def three_back(act_t, *refs, n_blocks, ks, carried):
    blocks = refs[:n_blocks]
    thirds = refs[n_blocks : n_blocks + len(ks)]
    refs = refs[n_blocks + len(ks) :]
    before = refs[0] if carried else None
    refs = refs[carried:]
    sum_two, grads, whole = refs[0], refs[1 : 1 + len(ks)], refs[-1]
    rows = blocks[0].shape[0]
    span = thirds[0].shape[1]
    for i, block in enumerate(blocks):
        whole[i * rows : (i + 1) * rows] = block[...]
    for i in range(len(ks)):
        at = slice(i * span, (i + 1) * span)
        grads[i][...] = dot(act_t[...], whole[:, at], 1, 0).astype(grads[i].dtype)
    total = before[...] if carried else None
    for i, third in enumerate(thirds):
        term = dot(third[...], whole[:, i * span : (i + 1) * span], 1, 1)
        total = term if total is None else total + term
    sum_two[...] = total


def two_back(sum_two, slope, act_one, delta, *grads):
    value = (sum_two[...] * slope[...]).astype(bf16)
    delta[...] = value
    span = act_one.shape[0] // len(grads)
    for k, grad in enumerate(grads):
        grad[...] = dot(act_one[k * span : (k + 1) * span], value, 1, 1).astype(grad.dtype)


def one_back(inputs, delta, slope, grad_four, *refs, n_mp):
    seconds, outs = refs[:n_mp], refs[n_mp:]
    tall = inputs.shape[0]
    span = seconds[0].shape[0]
    for k in range(n_mp):
        value = dot(seconds[k][...], delta[...], 1, 0)
        value = (value * slope[k * span : (k + 1) * span].astype(f32)).astype(bf16)
        outs[k][:tall] = dot(inputs[...], value, 1, 1).astype(outs[k].dtype)
        outs[k][tall:] = grad_four[:, k * span : (k + 1) * span].astype(outs[k].dtype)


def add_up(own, got, out):
    out[...] = (own[...].astype(f32) + got[...].astype(f32)).astype(out.dtype)


def spread_small(own, *refs):
    gots, out = refs[:-1], refs[-1]
    total = own[...].astype(f32)
    for got in gots:
        total = total + got[...].astype(f32)
    wide = out.shape[2]
    for d in range(out.shape[0]):
        out[d] = total[:, d * wide : (d + 1) * wide].astype(bf16)


def update_small(got, w_in, w_out, m_in, m_out, nw_in, nw_out, nm_in, nm_out):
    tall = got.shape[1] // 2
    total = jnp.sum(got[...].astype(f32), axis=0)
    n_in, n_out = w_in.shape[0], w_out.shape[0]
    mom = momentum_decay * m_in[...] + total[:n_in]
    nm_in[...] = mom
    nw_in[...] = w_in[...] - learn_rate * mom
    mom = momentum_decay * m_out[...] + total[tall : tall + n_out]
    nm_out[...] = mom
    nw_out[...] = w_out[...] - learn_rate * mom


def update_big(weight, moment, own, *refs):
    gots, (new_weight, new_moment) = refs[:-2], refs[-2:]
    total = own[...]
    for got in gots:
        total = total + got[...].astype(f32)
    mom = momentum_decay * moment[...] + total
    new_moment[...] = mom
    new_weight[...] = weight[...] - learn_rate * mom


def gathered(own, n_mp):
    held = {0: own}
    tops = [k for k in range(1, n_mp) if parent(k) == 0][::-1]
    rest = [k for k in range(1, n_mp) if parent(k) != 0]
    for k in tops + sorted(rest, key=lambda k: -low_bit(k)):
        held[k] = swap(held[parent(k)], "mp", low_bit(k))
    return held


def summed(held, n_mp, shape):
    gots = []
    for k in sorted(range(1, n_mp), key=lambda k: (low_bit(k), -k)):
        got = swap(held[k], "mp", low_bit(k))
        to = parent(k)
        if to:
            held[to] = on_core(add_up, shaped(shape, bf16), [held[to], got], "add_up")
        else:
            gots.append(got)
    return gots


def on_device(
    samples,
    targets,
    counts,
    weight_in,
    weight_mid,
    weight_top,
    weight_out,
    moment_in,
    moment_mid,
    moment_top,
    moment_out,
):
    slots, n_in, block = samples.shape
    n_out = targets.shape[1]
    n_dp, n_mp = lax.axis_size("dp"), lax.axis_size("mp")
    half = n_dp // 2
    per = slots // n_mp
    rows = per * block // 2
    n_rows = n_dp * rows
    wide = weight_in.shape[1]
    lanes = max(rows, 2 * wide)
    tall = up_to(max(n_in, n_out) + 1, 16)
    hidden = wide * n_dp
    width = hidden * n_mp
    n_mid, n_top = weight_mid.shape[1], weight_top.shape[1]
    planes = range(n_mp)
    part = functools.partial

    second = gathered(weight_mid.astype(bf16), n_mp)
    piece = on_core(
        part(pack_small, tall=tall), shaped((tall, lanes), bf16), [weight_in, weight_out.T], "pack_small"
    )
    pieces = [piece] + [swap(piece, "mp", k) for k in planes[1:]]
    third = gathered(weight_top.astype(bf16), n_mp)

    own = on_core(
        part(pack_rows, tall=tall, rows=rows, per=per),
        shaped(((4 + n_mp) * tall, lanes), bf16),
        [samples, targets, *pieces],
        "pack_rows",
        scalars=[counts],
    )
    got = swap(own, "dp", half)
    n_piece = n_mp * tall
    own, wanted = on_core(
        part(first_step, tall=tall),
        [shaped((2 * tall + 2 * n_piece, lanes), bf16), shaped((tall, rows), bf16)],
        [own, got],
        "first_step",
    )
    span, keys, step = 2 * tall, [0, half], 1
    while step * 2 < half:
        got = swap(own, "dp", step)
        own = on_core(
            part(next_step, step=step, span=span),
            shaped((2 * own.shape[0], lanes), bf16),
            [own, got],
            "next_step",
        )
        keys = keys + [k | step for k in keys]
        span, step = 2 * span, 2 * step
    got = swap(own, "dp", step)
    keys = keys + [k | step for k in keys]
    order = [keys.index(k) for k in list(range(0, n_dp, 2)) + list(range(1, n_dp, 2))]
    inputs, first, fourth = on_core(
        part(place_small, step=step, span=span, tall=tall, rows=rows, wide=wide, order=order),
        [shaped((tall, n_rows), bf16), shaped((tall, width), bf16), shaped((tall, width), bf16)],
        [own, got],
        "place_small",
    )

    act_one = on_core(
        part(one_forward, tile=128), shaped((width, n_rows), bf16), [inputs, first], "one_forward"
    )
    act_two, act_two_t, slope_two = on_core(
        two_forward,
        [shaped((n_rows, n_mid), bf16), shaped((n_mid, n_rows), bf16), shaped((n_mid, n_rows), f32)],
        [act_one] + [second[k] for k in planes],
        "two_forward",
    )
    groups = [list(planes[: n_mp // 2]), list(planes[n_mp // 2 :])]
    kept = half * rows
    terms = []
    for ks in groups:
        cols = len(ks) * n_top
        weights = [third[k] for k in ks]
        away = on_core(
            part(three_away, kept=kept), shaped((kept, cols), bf16), [act_two, *weights], "three_away"
        )
        own, *sends = on_core(
            part(three_home, kept=kept, rows=rows),
            [shaped((rows, cols), f32)] + [shaped((rows, cols), bf16)] * (half - 1),
            [act_two, swap(away, "dp", 1), *weights],
            "three_home",
        )
        terms += [own] + [swap(send, "dp", 2 * (i + 1)) for i, send in enumerate(sends)]
    slope_one = on_core(
        part(one_slope, tile=128), shaped((width, n_rows), bf16), [inputs, first], "one_slope",
        flops=12_000_000_000,
    )
    *deltas, grad_four = on_core(
        part(error_step, groups=len(groups), half=half, per=per, n_in=n_in, n_out=n_out),
        [shaped((rows, len(ks) * n_top), bf16) for ks in groups] + [shaped((tall, width), f32)],
        [inputs, wanted, fourth, *terms],
        "error_step",
        scratch=[pltpu.VMEM((rows, width), bf16), pltpu.VMEM((rows, width), f32)],
    )

    sum_two = None
    grad_three = {}
    gots_three = None
    for g in reversed(range(len(groups))):
        ks = groups[g]
        home = [deltas[g]] + [swap(deltas[g], "dp", 2 * i) for i in range(1, half)]
        away = [swap(value, "dp", 1) for value in home]
        carried = sum_two is not None
        sum_two, *grads = on_core(
            part(three_back, n_blocks=n_dp, ks=ks, carried=carried),
            [shaped((n_mid, n_rows), f32)]
            + [shaped((n_mid, n_top), bf16 if k else f32) for k in ks],
            [act_two_t, *home, *away] + [third[k] for k in ks] + ([sum_two] if carried else []),
            "three_back",
            scratch=[pltpu.VMEM((n_rows, len(ks) * n_top), bf16)],
        )
        grad_three.update(zip(ks, grads))
    gots_three = summed(grad_three, n_mp, (n_mid, n_top))
    grad_two = {}
    delta_two, *grads = on_core(
        two_back,
        [shaped((n_mid, n_rows), bf16)] + [shaped((hidden, n_mid), bf16 if k else f32) for k in planes],
        [sum_two, slope_two, act_one],
        "two_back",
    )
    grad_two = dict(zip(planes, grads))
    gots_two = summed(grad_two, n_mp, (hidden, n_mid))
    small = on_core(
        part(one_back, n_mp=n_mp),
        [shaped((2 * tall, hidden), bf16 if k else f32) for k in planes],
        [inputs, delta_two, slope_one, grad_four] + [second[k] for k in planes],
        "one_back",
    )
    small = on_core(
        spread_small,
        shaped((n_dp, 2 * tall, wide), bf16),
        [small[0]] + [swap(small[k], "mp", k) for k in planes[1:]],
        "spread_small",
    )
    small = lax.all_to_all(small, "dp", 0, 0, tiled=True)

    like = lambda value: shaped(value.shape, f32)
    flat = (weight_in, weight_out.T, moment_in, moment_out.T)
    new_in, new_out, mom_in, mom_out = on_core(
        update_small, [like(value) for value in flat], [small, *flat], "update_small"
    )
    new_top, mom_top = on_core(
        update_big, [like(weight_top)] * 2, [weight_top, moment_top, grad_three[0], *gots_three], "update_top"
    )
    new_mid, mom_mid = on_core(
        update_big, [like(weight_mid)] * 2, [weight_mid, moment_mid, grad_two[0], *gots_two], "update_mid"
    )
    return (new_in, new_mid, new_top, new_out.T, mom_in, mom_mid, mom_top, mom_out.T)


def solution(mesh):
    in_specs = (
        P("dp", None, None),
        P("dp", None, None),
        P("dp"),
        P(None, ("mp", "dp")),
        P("mp", "dp"),
        P("dp", "mp"),
        P(("mp", "dp"), None),
        P(None, ("mp", "dp")),
        P("mp", "dp"),
        P("dp", "mp"),
        P(("mp", "dp"), None),
    )
    out_specs = (
        P(None, ("mp", "dp")),
        P("mp", "dp"),
        P("dp", "mp"),
        P(("mp", "dp"), None),
        P(None, ("mp", "dp")),
        P("mp", "dp"),
        P("dp", "mp"),
        P(("mp", "dp"), None),
    )
    return jax.shard_map(
        on_device, mesh=mesh, in_specs=in_specs, out_specs=out_specs, check_vma=False
    )
```

```python
import functools
import math

import jax
import jax.numpy as jnp
from jax import lax
from jax.experimental import pallas as pl
from jax.experimental.pallas import tpu as pltpu
from jax.sharding import PartitionSpec as P

momentum_decay = 0.9
learn_rate = 0.05
bf16 = jnp.bfloat16
f32 = jnp.float32
VMEM_BYTES = 24 << 20
LONG = 100_000_000_000


def swap(value, axis, step):
    count = lax.axis_size(axis)
    return lax.ppermute(value, axis, [(at, at ^ step) for at in range(count)])


def parent(k):
    return k & (k - 1)


def low_bit(k):
    return k & -k


def up_to(value, unit):
    return -(-value // unit) * unit


def gelu_act(value):
    return 0.5 * value * (1.0 + lax.erf(value * math.sqrt(0.5)))


def gelu_slope(value):
    return 0.5 * (1.0 + lax.erf(value * math.sqrt(0.5))) + value * jnp.exp(
        -0.5 * value * value
    ) * (1.0 / math.sqrt(2.0 * math.pi))


def dot(left, right, at_left, at_right):
    dims = (((at_left,), (at_right,)), ((), ()))
    return lax.dot_general(left, right, dims, preferred_element_type=f32)


def shaped(dims, kind):
    return jax.ShapeDtypeStruct(dims, kind)


def on_core(body, outs, args, name, flops=0, scratch=(), scalars=()):
    at = pl.BlockSpec(memory_space=pltpu.VMEM)
    return pl.pallas_call(
        body,
        out_shape=outs,
        in_specs=[pl.BlockSpec(memory_space=pltpu.SMEM)] * len(scalars) + [at] * len(args),
        out_specs=jax.tree.map(lambda _: at, outs),
        scratch_shapes=list(scratch),
        compiler_params=pltpu.CompilerParams(vmem_limit_bytes=VMEM_BYTES),
        cost_estimate=pl.CostEstimate(flops=flops, bytes_accessed=0, transcendentals=0),
        name=name,
    )(*scalars, *args)


def pack_small(w_in, w_out, out, *, tall):
    n_in, wide = w_in.shape
    n_out = w_out.shape[0]
    left = jnp.concatenate([w_in[...], jnp.zeros((tall - n_in, wide), f32)], 0)
    right = jnp.concatenate([w_out[...], jnp.zeros((tall - n_out, wide), f32)], 0)
    parts = [left, right]
    spare = out.shape[1] - 2 * wide
    if spare:
        parts.append(jnp.zeros((tall, spare), f32))
    out[...] = jnp.concatenate(parts, 1).astype(bf16)


def pick_rows(count, samples, targets, out, wanted, *, tall, rows, per):
    slots, n_in, block = samples.shape
    n_out = targets.shape[1]
    half = lax.axis_size("dp") // 2
    high = lax.axis_index("dp") >= half
    xs, ys = [], []
    for j in range(per):
        at = per * lax.axis_index("mp") + j
        slot = jnp.where(high, slots - 1 - at, at)
        keep = slot < count[0]
        for source, last, all_of in (
            (samples, jnp.full((1, block), count[0].astype(f32)), xs),
            (targets, jnp.full((1, block), keep.astype(f32)), ys),
        ):
            value = source[slot].astype(f32)
            parts = [jnp.where(keep, value, jnp.zeros_like(value)), last]
            spare = tall - value.shape[0] - 1
            if spare:
                parts.append(jnp.zeros((spare, block), f32))
            all_of.append(jnp.concatenate(parts, 0).astype(bf16))
    x = jnp.concatenate(xs, 1) if per > 1 else xs[0]
    y = jnp.concatenate(ys, 1) if per > 1 else ys[0]
    spare = out.shape[1] - rows
    for t in range(2):
        at = slice(t * rows, (t + 1) * rows)
        half_x = x[:, at]
        if spare:
            half_x = jnp.concatenate([half_x, jnp.zeros((tall, spare), bf16)], 1)
        out[tall * t : tall * (t + 1)] = half_x
        wanted[t] = y[:, at]


def pack_all(*refs):
    out, at = refs[-1], 0
    for part in refs[:-1]:
        out[at : at + part.shape[0]] = part[...]
        at += part.shape[0]


def place_small(held, inputs, first, fourth, *, tall, rows, wide, places):
    n_dp, n_mp = lax.axis_size("dp"), lax.axis_size("mp")
    half = n_dp // 2
    blocks = list(range(0, n_dp, 2)) + list(range(1, n_dp, 2))
    for place, k in enumerate(blocks):
        at = lax.axis_index("dp") ^ k
        high = at >= half
        pair = jnp.where(high, at - half, at)
        both = held[pair, : 2 * tall] + held[pair + half, : 2 * tall]
        value = jnp.where(high, both[tall:], both[:tall])
        inputs[:, place * rows : (place + 1) * rows] = value[:, :rows]
    hidden = n_dp * wide
    for k in range(n_mp):
        row = slice((2 + k) * tall, (3 + k) * tall)
        pieces = [held[d, row] for d in range(n_dp)]
        at = slice(k * hidden, (k + 1) * hidden)
        first[:, at] = jnp.concatenate([piece[:, :wide] for piece in pieces], 1)
        at = slice(places.index(k) * hidden, (places.index(k) + 1) * hidden)
        fourth[:, at] = jnp.concatenate([piece[:, wide : 2 * wide] for piece in pieces], 1)


def one_forward(inputs, first, out, *, tile):
    n_rows = inputs.shape[1]
    cut = min(256, n_rows)

    def step(i, _):
        at = pl.ds(pl.multiple_of(i * tile, tile), tile)
        weights = first[:, at].T
        for c in range(0, n_rows, cut):
            pre = dot(weights, inputs[:, c : c + cut], 1, 0)
            out[at, c : c + cut] = gelu_act(pre).astype(bf16)
        return 0

    lax.fori_loop(0, first.shape[1] // tile, step, 0)


def one_slope(inputs, first, out, *, tile):
    n_rows = inputs.shape[1]
    cut = min(256, n_rows)

    def step(i, _):
        at = pl.ds(pl.multiple_of(i * tile, tile), tile)
        weights = first[:, at].T
        for c in range(0, n_rows, cut):
            pre = dot(weights, inputs[:, c : c + cut], 1, 0)
            out[at, c : c + cut] = gelu_slope(pre).astype(bf16)
        return 0

    lax.fori_loop(0, first.shape[1] // tile, step, 0)


def two_forward(act_one, *refs):
    seconds, (act, act_t, slope) = refs[:-3], refs[-3:]
    n_rows = act_one.shape[1]
    cut = min(256, n_rows)
    span = seconds[0].shape[0]
    turned = [s[...].T for s in seconds]
    for c in range(0, n_rows, cut):
        at = slice(c, c + cut)
        pre = dot(turned[0], act_one[:span, at], 1, 0)
        for k in range(1, len(seconds)):
            pre = pre + dot(turned[k], act_one[k * span : (k + 1) * span, at], 1, 0)
        value = gelu_act(pre)
        act_t[:, at] = value.astype(bf16)
        act[at] = value.T.astype(bf16)
        slope[:, at] = gelu_slope(pre)


def three_away(act, *refs, kept):
    thirds, out = refs[:-1], refs[-1]
    span = thirds[0].shape[1]
    for k, third in enumerate(thirds):
        out[:, k * span : (k + 1) * span] = dot(act[kept:], third[...], 1, 0).astype(bf16)


def three_home(act, got, *refs, kept, rows):
    half = kept // rows
    thirds, own, sends = refs[:-half], refs[-half], refs[len(refs) - half + 1 :]
    span = thirds[0].shape[1]
    for k, third in enumerate(thirds):
        at = slice(k * span, (k + 1) * span)
        total = dot(act[:kept], third[...], 1, 0) + got[:, at].astype(f32)
        own[:, at] = total[:rows]
        for i, send in enumerate(sends):
            send[:, at] = total[(i + 1) * rows : (i + 2) * rows].astype(bf16)


def error_step(inputs, wanted, wanted_too, fourth, *refs, groups, half, per, n_in, n_out):
    terms = refs[: groups * half]
    act, pre = refs[-2:]
    deltas, grad_four = refs[groups * half : groups * half + groups], refs[-3]
    width = pre.shape[1] // groups
    for g in range(groups):
        at = slice(g * width, (g + 1) * width)
        own, others = terms[g * half], terms[g * half + 1 : (g + 1) * half]
        total = own[...]
        for other in others:
            total = total + other[...].astype(f32)
        pre[:, at] = total
        act[:, at] = gelu_act(total).astype(bf16)
    predicted = dot(fourth[...], act[...], 1, 1)
    number = jnp.sum(inputs[n_in : n_in + 1, :].astype(f32), axis=1, keepdims=True) / per
    mine = jnp.where(lax.axis_index("dp") >= half, 1, 0)
    wanted = wanted[mine] + wanted_too[mine]
    live = wanted[n_out : n_out + 1, :].astype(f32)
    error = (2.0 / number * (predicted - wanted.astype(f32)) * live).astype(bf16)
    row = lax.broadcasted_iota(jnp.int32, error.shape, 0)
    error = jnp.where(row < n_out, error, jnp.zeros_like(error))
    grad_four[...] = dot(error, act[...], 1, 0)
    turned = error.astype(f32).T.astype(bf16)
    for g in range(groups):
        at = slice(g * width, (g + 1) * width)
        delta = dot(turned, fourth[:, at], 1, 0) * gelu_slope(pre[:, at])
        deltas[g][: delta.shape[0]] = delta.astype(bf16)


def join(*refs):
    rows = refs[-1].shape[0] // (len(refs) - 1)
    for i, part in enumerate(refs[:-1]):
        refs[-1][i * rows : (i + 1) * rows] = part[:rows]


def three_back(act_t, home, away, *refs, ks, carried):
    thirds = refs[: len(ks)]
    refs = refs[len(ks) :]
    before = refs[0] if carried else None
    refs = refs[carried:]
    sum_two, grads, whole = refs[0], refs[1 : 1 + len(ks)], refs[-1]
    rows = home.shape[0]
    span = thirds[0].shape[1]
    whole[:rows] = home[...]
    whole[rows:] = away[...]
    for i in range(len(ks)):
        at = slice(i * span, (i + 1) * span)
        grads[i][...] = dot(act_t[...], whole[:, at], 1, 0).astype(grads[i].dtype)
    total = before[...] if carried else None
    for i, third in enumerate(thirds):
        term = dot(third[...], whole[:, i * span : (i + 1) * span], 1, 1)
        total = term if total is None else total + term
    sum_two[...] = total


def two_back(sum_two, slope, act_one, delta, *grads):
    value = (sum_two[...] * slope[...]).astype(bf16)
    delta[...] = value
    span = act_one.shape[0] // len(grads)
    for k, grad in enumerate(grads):
        grad[...] = dot(act_one[k * span : (k + 1) * span], value, 1, 1).astype(grad.dtype)


def split_dp(parts, step, keep, send):
    bit = (lax.axis_index("dp") & step) != 0
    for i in range(len(parts) // 2):
        even, odd = parts[2 * i], parts[2 * i + 1]
        keep[i] = jnp.where(bit, odd, even)
        send[i] = jnp.where(bit, even, odd).astype(bf16)


def one_back(inputs, delta, slope, grad_four, *refs, n_mp, n_dp, places):
    seconds, (keep, send) = refs[:n_mp], refs[n_mp:]
    span = seconds[0].shape[0]
    wide = span // n_dp
    whole = []
    for k in range(n_mp):
        value = dot(seconds[k][...], delta[...], 1, 0)
        value = (value * slope[k * span : (k + 1) * span].astype(f32)).astype(bf16)
        grad_one = dot(inputs[...], value, 1, 1)
        at = places.index(k) * span
        whole.append(jnp.concatenate([grad_one, grad_four[:, at : at + span]], 0))
    parts = [
        jnp.concatenate([value[:, d * wide : (d + 1) * wide] for value in whole], 1)
        for d in range(n_dp)
    ]
    split_dp(parts, 1, keep, send)


def halve(own, got, keep, send, *, step):
    split_dp([own[i] + got[i].astype(f32) for i in range(own.shape[0])], step, keep, send)


def last_half(own, got, keep, send):
    total = own[0] + got[0].astype(f32)
    wide = keep.shape[1]
    keep[...] = total[:, :wide]
    send[...] = total[:, wide:].astype(bf16)


def last_half_mp(own, got, keep, send):
    total = own[...] + got[...].astype(f32)
    wide = keep.shape[1]
    keep[...] = total[:, :wide]
    send[...] = total[:, wide:].astype(bf16)


def add_up(own, got, out):
    out[...] = (own[...].astype(f32) + got[...].astype(f32)).astype(out.dtype)


def update_small(own, *refs):
    gots, (w_in, w_out, m_in, m_out), outs = refs[:-8], refs[-8:-4], refs[-4:]
    nw_in, nw_out, nm_in, nm_out = outs
    tall = own.shape[0] // 2
    total = own[...]
    for got in gots:
        total = total + got[...].astype(f32)
    n_in, n_out = w_in.shape[0], w_out.shape[0]
    mom = momentum_decay * m_in[...] + total[:n_in]
    nm_in[...] = mom
    nw_in[...] = w_in[...] - learn_rate * mom
    mom = momentum_decay * m_out[...] + total[tall : tall + n_out]
    nm_out[...] = mom
    nw_out[...] = w_out[...] - learn_rate * mom


def update_big(weight, moment, own, *refs):
    gots, (new_weight, new_moment) = refs[:-2], refs[-2:]
    total = own[...]
    for got in gots:
        total = total + got[...].astype(f32)
    mom = momentum_decay * moment[...] + total
    new_moment[...] = mom
    new_weight[...] = weight[...] - learn_rate * mom


def after(first, *values):
    return lax.optimization_barrier((first, *values))[1:]


def gathered(own, n_mp):
    held = {0: own}
    for k in [k for k in range(1, n_mp) if parent(k) == 0][::-1]:
        held[k] = swap(own, "mp", k)
    return held


def passed_on(held, n_mp, ready):
    for k in sorted((k for k in range(1, n_mp) if parent(k)), key=lambda k: -low_bit(k)):
        held[k] = swap(after(ready, held[parent(k)])[0], "mp", low_bit(k))


def summed(held, ks, sent):
    gots = []
    for k in sorted((k for k in ks if k), key=lambda k: (low_bit(k), -k)):
        got = sent[k] if k in sent else swap(held[k], "mp", low_bit(k))
        to = parent(k)
        if to:
            held[to] = on_core(add_up, shaped(got.shape, bf16), [held[to], got], "add_up")
        else:
            gots.append(got)
    return gots


def on_device(
    samples,
    targets,
    counts,
    weight_in,
    weight_mid,
    weight_top,
    weight_out,
    moment_in,
    moment_mid,
    moment_top,
    moment_out,
):
    slots, n_in, block = samples.shape
    n_out = targets.shape[1]
    n_dp, n_mp = lax.axis_size("dp"), lax.axis_size("mp")
    half = n_dp // 2
    per = slots // n_mp
    rows = per * block // 2
    n_rows = n_dp * rows
    wide = weight_in.shape[1]
    lanes = max(rows, 2 * wide)
    tall = up_to(max(n_in, n_out) + 1, 16)
    hidden = wide * n_dp
    width = hidden * n_mp
    n_mid, n_top = weight_mid.shape[1], weight_top.shape[1]
    planes = range(n_mp)
    groups = [list(planes[::2]), list(planes[1::2])]
    places = [k for ks in groups for k in ks]
    part = functools.partial

    piece = on_core(
        part(pack_small, tall=tall), shaped((tall, lanes), bf16), [weight_in, weight_out.T], "pack_small"
    )
    second = gathered(weight_mid.astype(bf16), n_mp)
    picked, wanted = on_core(
        part(pick_rows, tall=tall, rows=rows, per=per),
        [shaped((2 * tall, lanes), bf16), shaped((2, tall, rows), bf16)],
        [samples, targets],
        "pick_rows",
        scalars=[counts],
    )
    pieces = [piece] + [swap(piece, "mp", k) for k in planes[1:]]
    top = after((picked, pieces), weight_top.astype(bf16))[0]
    third = gathered(top, n_mp)
    passed_on(second, n_mp, (picked, pieces))

    early = [second[k] for k in planes if k and not parent(k)]
    packed = on_core(
        pack_all,
        shaped(((2 + n_mp) * tall, lanes), bf16),
        [picked, *after(early, *pieces)],
        "pack_all",
    )
    wanted = [wanted, swap(wanted, "dp", half)]
    held = lax.all_gather(packed, "dp")
    inputs, first, fourth = on_core(
        part(place_small, tall=tall, rows=rows, wide=wide, places=places),
        [shaped((tall, n_rows), bf16), shaped((tall, width), bf16), shaped((tall, width), bf16)],
        [held],
        "place_small",
    )

    act_one = on_core(
        part(one_forward, tile=128), shaped((width, n_rows), bf16), [inputs, first], "one_forward"
    )
    act_two, act_two_t, slope_two = on_core(
        two_forward,
        [shaped((n_rows, n_mid), bf16), shaped((n_mid, n_rows), bf16), shaped((n_mid, n_rows), f32)],
        [act_one] + [second[k] for k in planes],
        "two_forward",
    )
    passed_on(third, n_mp, act_one)
    kept = half * rows
    terms = []
    ahead = [third[k] for k in planes if k and not parent(k)]
    for ks in groups:
        cols = len(ks) * n_top
        weights = after(ahead, *[third[k] for k in ks])
        away = on_core(
            part(three_away, kept=kept), shaped((kept, cols), bf16), [act_two, *weights], "three_away"
        )
        own, *sends = on_core(
            part(three_home, kept=kept, rows=rows),
            [shaped((rows, cols), f32)] + [shaped((rows, cols), bf16)] * (half - 1),
            [act_two, swap(away, "dp", 1), *weights],
            "three_home",
        )
        ahead = [swap(send, "dp", 2 * (i + 1)) for i, send in enumerate(sends)]
        terms += [own, *ahead]
    slope_one = on_core(
        part(one_slope, tile=128), shaped((width, n_rows), bf16), [inputs, first], "one_slope",
        flops=12_000_000_000,
    )
    *deltas, grad_four = on_core(
        part(error_step, groups=len(groups), half=half, per=per, n_in=n_in, n_out=n_out),
        [shaped((rows + 16 * (g == 0), len(ks) * n_top), bf16) for g, ks in enumerate(groups)] + [shaped((tall, width), f32)],
        [inputs, *wanted, fourth, *after(slope_one, *terms)],
        "error_step",
        scratch=[pltpu.VMEM((rows, width), bf16), pltpu.VMEM((rows, width), f32)],
    )

    sum_two, grad_three, sent = None, {}, []
    for g in reversed(range(len(groups))):
        ks = groups[g]
        home = [deltas[g]] + [swap(deltas[g], "dp", 2 * i) for i in range(1, half)]
        if sent:
            home = after((sum_two, sent), *home)
        home = on_core(join, shaped((kept, deltas[g].shape[1]), bf16), home, "join")
        away = swap(home, "dp", 1)
        carry = [sum_two] if sent else []
        sum_two, *grads = on_core(
            part(three_back, ks=ks, carried=len(carry)),
            [shaped((n_mid, n_rows), f32)]
            + [shaped((n_mid, n_top), bf16 if k else f32) for k in ks],
            [act_two_t, home, away] + [third[k] for k in ks] + carry,
            "three_back",
            scratch=[pltpu.VMEM((n_rows, len(ks) * n_top), bf16)],
        )
        grad_three.update(zip(ks, grads))
        if not sent:
            sent = [swap(grad_three[k], "mp", 1) for k in ks]
    gots_three = summed(grad_three, planes, dict(zip(groups[1], sent)))
    grad_two = {}
    delta_two, *grads = on_core(
        two_back,
        [shaped((n_mid, n_rows), bf16)] + [shaped((hidden, n_mid), bf16 if k else f32) for k in planes],
        [sum_two, slope_two, act_one],
        "two_back",
        flops=LONG,
    )
    grad_two = dict(zip(planes, grads))
    farthest = swap(grad_two[n_mp - 1], "mp", 1)
    grad_two[1] = after(farthest, grad_two[1])[0]
    gots_two = summed(grad_two, planes, {n_mp - 1: farthest})
    shape = (half, 2 * tall, n_mp * wide)
    keep, send = on_core(
        part(one_back, n_mp=n_mp, n_dp=n_dp, places=places),
        [shaped(shape, f32), shaped(shape, bf16)],
        [inputs, delta_two, slope_one, grad_four] + [second[k] for k in planes],
        "one_back",
        flops=LONG,
    )
    step = 1
    while step < half:
        got = swap(send, "dp", step)
        step *= 2
        shape = (shape[0] // 2, *shape[1:])
        keep, send = on_core(
            part(halve, step=step), [shaped(shape, f32), shaped(shape, bf16)], [keep, got], "halve"
        )
    got = swap(send, "dp", step)
    half_mp = n_mp // 2 * wide
    keep, send = on_core(
        last_half,
        [shaped((2 * tall, half_mp), f32), shaped((2 * tall, half_mp), bf16)],
        [keep, got],
        "last_half",
    )
    step = n_mp // 2
    while step:
        got = swap(send, "mp", step)
        step //= 2
        if step:
            got = after((gots_two, gots_three), got)[0]
        if step:
            half_mp = step * wide
            keep, send = on_core(
                last_half_mp,
                [shaped((2 * tall, half_mp), f32), shaped((2 * tall, half_mp), bf16)],
                [keep, got],
                "last_half_mp",
            )
    gots_small = [got]

    like = lambda value: shaped(value.shape, f32)
    flat = (weight_in, weight_out.T, moment_in, moment_out.T)
    new_in, new_out, mom_in, mom_out = on_core(
        update_small, [like(value) for value in flat], [keep, *gots_small, *flat], "update_small"
    )
    new_top, mom_top = on_core(
        update_big, [like(weight_top)] * 2, [weight_top, moment_top, grad_three[0], *gots_three], "update_top",
        flops=2_000_000_000,
    )
    new_mid, mom_mid = on_core(
        update_big, [like(weight_mid)] * 2, [weight_mid, moment_mid, grad_two[0], *gots_two], "update_mid"
    )
    return (new_in, new_mid, new_top, new_out.T, mom_in, mom_mid, mom_top, mom_out.T)


def solution(mesh):
    in_specs = (
        P("dp", None, None),
        P("dp", None, None),
        P("dp"),
        P(None, ("mp", "dp")),
        P("mp", "dp"),
        P("dp", "mp"),
        P(("mp", "dp"), None),
        P(None, ("mp", "dp")),
        P("mp", "dp"),
        P("dp", "mp"),
        P(("mp", "dp"), None),
    )
    out_specs = (
        P(None, ("mp", "dp")),
        P("mp", "dp"),
        P("dp", "mp"),
        P(("mp", "dp"), None),
        P(None, ("mp", "dp")),
        P("mp", "dp"),
        P("dp", "mp"),
        P(("mp", "dp"), None),
    )
    return jax.shard_map(
        on_device, mesh=mesh, in_specs=in_specs, out_specs=out_specs, check_vma=False
    )
```

```python
import functools
import math

import jax
import jax.numpy as jnp
from jax import lax
from jax.experimental import pallas as pl
from jax.experimental.pallas import tpu as pltpu
from jax.sharding import PartitionSpec as P

momentum_decay = 0.9
learn_rate = 0.05
bf16 = jnp.bfloat16
f32 = jnp.float32
VMEM_BYTES = 24 << 20
LONG = 100_000_000_000


def swap(value, axis, step):
    count = lax.axis_size(axis)
    return lax.ppermute(value, axis, [(at, at ^ step) for at in range(count)])


def parent(k):
    return k & (k - 1)


def low_bit(k):
    return k & -k


def up_to(value, unit):
    return -(-value // unit) * unit


def gelu_act(value):
    return 0.5 * value * (1.0 + lax.erf(value * math.sqrt(0.5)))


def gelu_slope(value):
    return 0.5 * (1.0 + lax.erf(value * math.sqrt(0.5))) + value * jnp.exp(
        -0.5 * value * value
    ) * (1.0 / math.sqrt(2.0 * math.pi))


def dot(left, right, at_left, at_right):
    dims = (((at_left,), (at_right,)), ((), ()))
    return lax.dot_general(left, right, dims, preferred_element_type=f32)


def shaped(dims, kind):
    return jax.ShapeDtypeStruct(dims, kind)


def on_core(body, outs, args, name, flops=0, scratch=(), scalars=()):
    at = pl.BlockSpec(memory_space=pltpu.VMEM)
    return pl.pallas_call(
        body,
        out_shape=outs,
        in_specs=[pl.BlockSpec(memory_space=pltpu.SMEM)] * len(scalars) + [at] * len(args),
        out_specs=jax.tree.map(lambda _: at, outs),
        scratch_shapes=list(scratch),
        compiler_params=pltpu.CompilerParams(vmem_limit_bytes=VMEM_BYTES),
        cost_estimate=pl.CostEstimate(flops=flops, bytes_accessed=0, transcendentals=0),
        name=name,
    )(*scalars, *args)


def pack_small(w_in, w_out, out, *, tall):
    n_in, wide = w_in.shape
    n_out = w_out.shape[0]
    left = jnp.concatenate([w_in[...], jnp.zeros((tall - n_in, wide), f32)], 0)
    right = jnp.concatenate([w_out[...], jnp.zeros((tall - n_out, wide), f32)], 0)
    parts = [left, right]
    spare = out.shape[1] - 2 * wide
    if spare:
        parts.append(jnp.zeros((tall, spare), f32))
    out[...] = jnp.concatenate(parts, 1).astype(bf16)


def pick_rows(count, samples, targets, out, wanted, *, tall, rows, per):
    slots, n_in, block = samples.shape
    n_out = targets.shape[1]
    half = lax.axis_size("dp") // 2
    high = lax.axis_index("dp") >= half
    xs, ys = [], []
    for j in range(per):
        at = per * lax.axis_index("mp") + j
        slot = jnp.where(high, slots - 1 - at, at)
        keep = slot < count[0]
        for source, last, all_of in (
            (samples, jnp.full((1, block), count[0].astype(f32)), xs),
            (targets, jnp.full((1, block), keep.astype(f32)), ys),
        ):
            value = source[slot].astype(f32)
            parts = [jnp.where(keep, value, jnp.zeros_like(value)), last]
            spare = tall - value.shape[0] - 1
            if spare:
                parts.append(jnp.zeros((spare, block), f32))
            all_of.append(jnp.concatenate(parts, 0).astype(bf16))
    x = jnp.concatenate(xs, 1) if per > 1 else xs[0]
    y = jnp.concatenate(ys, 1) if per > 1 else ys[0]
    spare = out.shape[1] - rows
    for t in range(2):
        at = slice(t * rows, (t + 1) * rows)
        half_x = x[:, at]
        if spare:
            half_x = jnp.concatenate([half_x, jnp.zeros((tall, spare), bf16)], 1)
        out[tall * t : tall * (t + 1)] = half_x
        wanted[t] = y[:, at]


def pack_all(*refs):
    out, at = refs[-1], 0
    for part in refs[:-1]:
        out[at : at + part.shape[0]] = part[...]
        at += part.shape[0]


def place_small(held, inputs, first, fourth, *, tall, rows, wide, places):
    n_dp, n_mp = lax.axis_size("dp"), lax.axis_size("mp")
    half = n_dp // 2
    blocks = list(range(0, n_dp, 2)) + list(range(1, n_dp, 2))
    for place, k in enumerate(blocks):
        at = lax.axis_index("dp") ^ k
        high = at >= half
        pair = jnp.where(high, at - half, at)
        both = held[pair, : 2 * tall] + held[pair + half, : 2 * tall]
        value = jnp.where(high, both[tall:], both[:tall])
        inputs[:, place * rows : (place + 1) * rows] = value[:, :rows]
    hidden = n_dp * wide
    for k in range(n_mp):
        row = slice((2 + k) * tall, (3 + k) * tall)
        pieces = [held[d, row] for d in range(n_dp)]
        at = slice(k * hidden, (k + 1) * hidden)
        first[:, at] = jnp.concatenate([piece[:, :wide] for piece in pieces], 1)
        at = slice(places.index(k) * hidden, (places.index(k) + 1) * hidden)
        fourth[:, at] = jnp.concatenate([piece[:, wide : 2 * wide] for piece in pieces], 1)


def one_forward(inputs, first, out, *, tile):
    n_rows = inputs.shape[1]
    cut = min(256, n_rows)

    def step(i, _):
        at = pl.ds(pl.multiple_of(i * tile, tile), tile)
        weights = first[:, at].T
        for c in range(0, n_rows, cut):
            pre = dot(weights, inputs[:, c : c + cut], 1, 0)
            out[at, c : c + cut] = gelu_act(pre).astype(bf16)
        return 0

    lax.fori_loop(0, first.shape[1] // tile, step, 0)


def one_slope(inputs, first, out, *, tile):
    n_rows = inputs.shape[1]
    cut = min(256, n_rows)

    def step(i, _):
        at = pl.ds(pl.multiple_of(i * tile, tile), tile)
        weights = first[:, at].T
        for c in range(0, n_rows, cut):
            pre = dot(weights, inputs[:, c : c + cut], 1, 0)
            out[at, c : c + cut] = gelu_slope(pre).astype(bf16)
        return 0

    lax.fori_loop(0, first.shape[1] // tile, step, 0)


def two_forward(act_one, *refs):
    seconds, (act, act_t, slope) = refs[:-3], refs[-3:]
    n_rows = act_one.shape[1]
    cut = min(256, n_rows)
    span = seconds[0].shape[0]
    turned = [s[...].T for s in seconds]
    for c in range(0, n_rows, cut):
        at = slice(c, c + cut)
        pre = dot(turned[0], act_one[:span, at], 1, 0)
        for k in range(1, len(seconds)):
            pre = pre + dot(turned[k], act_one[k * span : (k + 1) * span, at], 1, 0)
        value = gelu_act(pre)
        act_t[:, at] = value.astype(bf16)
        act[at] = value.T.astype(bf16)
        slope[:, at] = gelu_slope(pre)


def three_away(act, *refs, kept):
    thirds, out = refs[:-1], refs[-1]
    span = thirds[0].shape[1]
    for k, third in enumerate(thirds):
        out[:, k * span : (k + 1) * span] = dot(act[kept:], third[...], 1, 0).astype(bf16)


def divided(kept, bit):
    return [k for k in kept if not k & bit]


def three_home(act, got, *refs, n_third, orders, kept):
    thirds, own, outs = refs[:n_third], refs[n_third], refs[n_third + 1 :]
    rows = own.shape[0]
    span = thirds[0].shape[1]
    count = len(kept) * rows
    blocks = {k: slice(i * rows, (i + 1) * rows) for i, k in enumerate(kept)}
    half = own.shape[1] // 2
    step = min(span, half)
    for at in range(0, own.shape[1], step):
        third = thirds[at // span]
        total = dot(act[:count], third[:, at % span : at % span + step], 1, 0)
        total = total + got[:, at : at + step].astype(f32)
        own[:, at : at + step] = total[blocks[0]]
        part = at // half
        keep, send = outs[2 * part], outs[2 * part + 1]
        put = slice(at - part * half, at - part * half + step)
        bit = orders[part][0]
        for i, k in enumerate(divided(kept, bit)):
            if k:
                keep[(i - 1) * rows : i * rows, put] = total[blocks[k]]
            send[i * rows : (i + 1) * rows, put] = total[blocks[k | bit]].astype(bf16)


def three_pass(own, *refs, stage, orders, kept):
    ins, new_own, outs = refs[:4], refs[4], refs[5:]
    rows = own.shape[0]
    half = own.shape[1] // 2
    for part, order in enumerate(orders):
        here = list(kept)
        for bit in order[:stage]:
            here = divided(here, bit)
        keep, got = ins[2 * part], ins[2 * part + 1]
        at = slice(part * half, (part + 1) * half)
        total = {}
        for i, k in enumerate(here):
            value = own[:, at] if k == 0 else keep[(i - 1) * rows : i * rows]
            total[k] = value + got[i * rows : (i + 1) * rows].astype(f32)
        new_own[:, at] = total[0]
        bit = order[stage]
        send = outs[2 * part + 1] if len(outs) == 4 else outs[part]
        for i, k in enumerate(divided(here, bit)):
            if k:
                outs[2 * part][(i - 1) * rows : i * rows] = total[k]
            send[i * rows : (i + 1) * rows] = total[k | bit].astype(bf16)


def error_step(inputs, wanted, wanted_too, fourth, *refs, groups, half, per, n_in, n_out):
    terms = refs[: 3 * groups]
    act, pre = refs[-2:]
    deltas, grad_four = refs[3 * groups : 5 * groups], refs[-3]
    width = pre.shape[1] // groups // 2
    for g in range(groups):
        for part in range(2):
            at = slice((2 * g + part) * width, (2 * g + part + 1) * width)
            total = terms[3 * g][:, part * width : (part + 1) * width]
            total = total + terms[3 * g + 1 + part][...].astype(f32)
            pre[:, at] = total
            act[:, at] = gelu_act(total).astype(bf16)
    predicted = dot(fourth[...], act[...], 1, 1)
    number = jnp.sum(inputs[n_in : n_in + 1, :].astype(f32), axis=1, keepdims=True) / per
    mine = jnp.where(lax.axis_index("dp") >= half, 1, 0)
    wanted = wanted[mine] + wanted_too[mine]
    live = wanted[n_out : n_out + 1, :].astype(f32)
    error = (2.0 / number * (predicted - wanted.astype(f32)) * live).astype(bf16)
    row = lax.broadcasted_iota(jnp.int32, error.shape, 0)
    error = jnp.where(row < n_out, error, jnp.zeros_like(error))
    grad_four[...] = dot(error, act[...], 1, 0)
    turned = error.astype(f32).T.astype(bf16)
    for i, delta in enumerate(deltas):
        at = slice(i * width, (i + 1) * width)
        value = dot(turned, fourth[:, at], 1, 0) * gelu_slope(pre[:, at])
        delta[...] = value.astype(bf16)


def join(own, got, out):
    rows = own.shape[0]
    out[:rows] = own[...]
    filled = rows + got.shape[0]
    out[rows:filled] = got[...]
    if filled < out.shape[0]:
        out[filled:] = jnp.zeros((out.shape[0] - filled, out.shape[1]), out.dtype)


def join_all(*refs, held, evens, rows):
    out = refs[-1]
    half = out.shape[1] // 2
    for i, blocks in enumerate(held):
        for j, k in enumerate(blocks):
            to = evens.index(k) * rows
            at = slice(i // 2 * half, (i // 2 + 1) * half)
            out[to : to + rows, at] = refs[i][j * rows : (j + 1) * rows]


def three_first(act_t, home, away, grad, *, column):
    rows = home.shape[0]
    at = slice(column, column + grad.shape[1])
    total = dot(act_t[:, :rows], home[:, at], 1, 0) + dot(act_t[:, rows:], away[:, at], 1, 0)
    grad[...] = total.astype(grad.dtype)


def three_back(act_t, home, away, *refs, ks, carried, ready):
    thirds = refs[: len(ks)]
    refs = refs[len(ks) :]
    before = refs[0] if carried else None
    refs = refs[carried:]
    sum_two, grads, whole = refs[0], refs[1 : 1 + len(ks) - ready], refs[-1]
    rows = home.shape[0]
    span = thirds[0].shape[1]
    whole[:rows] = home[...]
    whole[rows:] = away[...]
    for i in range(len(grads)):
        at = slice(i * span, (i + 1) * span)
        grads[i][...] = dot(act_t[...], whole[:, at], 1, 0).astype(grads[i].dtype)
    total = before[...] if carried else None
    for i, third in enumerate(thirds):
        term = dot(third[...], whole[:, i * span : (i + 1) * span], 1, 1)
        total = term if total is None else total + term
    sum_two[...] = total


def two_first(sum_two, slope, act_one, delta, grad):
    value = (sum_two[...] * slope[...]).astype(bf16)
    delta[...] = value
    grad[...] = dot(act_one[act_one.shape[0] - grad.shape[0] :], value, 1, 1).astype(grad.dtype)


def two_back(delta, act_one, *grads):
    span = grads[0].shape[0]
    for k, grad in enumerate(grads):
        part = act_one[k * span : (k + 1) * span]
        grad[...] = dot(part, delta[...], 1, 1).astype(grad.dtype)


def split_dp(parts, step, keep, send):
    bit = (lax.axis_index("dp") & step) != 0
    for i in range(len(parts) // 2):
        even, odd = parts[2 * i], parts[2 * i + 1]
        keep[i] = jnp.where(bit, odd, even)
        send[i] = jnp.where(bit, even, odd).astype(bf16)


def one_back(inputs, delta, slope, grad_four, *refs, n_mp, n_dp, places, n_in, n_out):
    seconds, (keep, send) = refs[:n_mp], refs[n_mp:]
    span = seconds[0].shape[0]
    wide = span // n_dp
    whole = []
    for k in range(n_mp):
        value = dot(seconds[k][...], delta[...], 1, 0)
        value = (value * slope[k * span : (k + 1) * span].astype(f32)).astype(bf16)
        grad_one = dot(inputs[...], value, 1, 1)
        at = places.index(k) * span
        pieces = [grad_one[:n_in], grad_four[:n_out, at : at + span]]
        spare = keep.shape[1] - n_in - n_out
        if spare:
            pieces.append(jnp.zeros((spare, span), f32))
        whole.append(jnp.concatenate(pieces, 0))
    parts = [
        jnp.concatenate([value[:, d * wide : (d + 1) * wide] for value in whole], 1)
        for d in range(n_dp)
    ]
    split_dp(parts, 1, keep, send)


def halve(own, got, keep, send, *, step):
    split_dp([own[i] + got[i].astype(f32) for i in range(own.shape[0])], step, keep, send)


def last_half(own, got, keep, send):
    total = own[0] + got[0].astype(f32)
    wide = keep.shape[1]
    keep[...] = total[:, :wide]
    send[...] = total[:, wide:].astype(bf16)


def last_half_mp(own, got, keep, send):
    total = own[...] + got[...].astype(f32)
    wide = keep.shape[1]
    keep[...] = total[:, :wide]
    send[...] = total[:, wide:].astype(bf16)


def add_up(own, got, out):
    out[...] = (own[...].astype(f32) + got[...].astype(f32)).astype(out.dtype)


def update_small(own, *refs):
    gots, (w_in, w_out, m_in, m_out), outs = refs[:-8], refs[-8:-4], refs[-4:]
    nw_in, nw_out, nm_in, nm_out = outs
    total = own[...]
    for got in gots:
        total = total + got[...].astype(f32)
    n_in, n_out = w_in.shape[0], w_out.shape[0]
    mom = momentum_decay * m_in[...] + total[:n_in]
    nm_in[...] = mom
    nw_in[...] = w_in[...] - learn_rate * mom
    mom = momentum_decay * m_out[...] + total[n_in : n_in + n_out]
    nm_out[...] = mom
    nw_out[...] = w_out[...] - learn_rate * mom


def update_big(weight, moment, own, *refs):
    gots, (new_weight, new_moment) = refs[:-2], refs[-2:]
    total = own[...]
    for got in gots:
        total = total + got[...].astype(f32)
    mom = momentum_decay * moment[...] + total
    new_moment[...] = mom
    new_weight[...] = weight[...] - learn_rate * mom


def after(first, *values):
    return lax.optimization_barrier((first, *values))[1:]


def gathered(own, n_mp):
    held = {0: own}
    for k in [k for k in range(1, n_mp) if parent(k) == 0][::-1]:
        held[k] = swap(own, "mp", k)
    return held


def passed_on(held, n_mp, ready):
    for k in sorted((k for k in range(1, n_mp) if parent(k)), key=lambda k: -low_bit(k)):
        held[k] = swap(after(ready, held[parent(k)])[0], "mp", low_bit(k))


def summed(held, ks, firsts=None):
    gots = []
    for k in sorted((k for k in ks if k), key=lambda k: (low_bit(k), -k)):
        got = swap(held[k], "mp", low_bit(k))
        to = parent(k)
        if firsts is not None:
            firsts.append(got)
        if to:
            held[to] = on_core(add_up, shaped(got.shape, bf16), [held[to], got], "add_up")
        else:
            gots.append(got)
    return gots


def on_device(
    samples,
    targets,
    counts,
    weight_in,
    weight_mid,
    weight_top,
    weight_out,
    moment_in,
    moment_mid,
    moment_top,
    moment_out,
):
    slots, n_in, block = samples.shape
    n_out = targets.shape[1]
    n_dp, n_mp = lax.axis_size("dp"), lax.axis_size("mp")
    half = n_dp // 2
    per = slots // n_mp
    rows = per * block // 2
    n_rows = n_dp * rows
    wide = weight_in.shape[1]
    lanes = max(rows, 2 * wide)
    tall = up_to(max(n_in, n_out) + 1, 16)
    hidden = wide * n_dp
    width = hidden * n_mp
    n_mid, n_top = weight_mid.shape[1], weight_top.shape[1]
    planes = range(n_mp)
    groups = [list(planes[: n_mp // 2]), list(planes[n_mp // 2 :])]
    places = [k for ks in groups for k in ks]
    part = functools.partial

    piece = on_core(
        part(pack_small, tall=tall), shaped((tall, lanes), bf16), [weight_in, weight_out.T], "pack_small"
    )
    pieces = [piece] + [swap(piece, "mp", k) for k in planes[1:]]
    second = gathered(weight_mid.astype(bf16), n_mp)
    picked, wanted = on_core(
        part(pick_rows, tall=tall, rows=rows, per=per),
        [shaped((2 * tall, lanes), bf16), shaped((2, tall, rows), bf16)],
        [samples, targets],
        "pick_rows",
        scalars=after(pieces, counts),
        flops=LONG,
    )
    top = after((picked, pieces), weight_top.astype(bf16))[0]
    third = gathered(top, n_mp)

    packed = on_core(
        pack_all,
        shaped(((2 + n_mp) * tall, lanes), bf16),
        [picked, *pieces],
        "pack_all",
    )
    wanted = [wanted, swap(wanted, "dp", half)]
    held = lax.all_gather(packed, "dp")
    passed_on(second, n_mp, held)
    inputs, first, fourth = on_core(
        part(place_small, tall=tall, rows=rows, wide=wide, places=places),
        [shaped((tall, n_rows), bf16), shaped((tall, width), bf16), shaped((tall, width), bf16)],
        [held],
        "place_small",
    )

    act_one = on_core(
        part(one_forward, tile=128), shaped((width, n_rows), bf16), [inputs, first], "one_forward"
    )
    act_two, act_two_t, slope_two = on_core(
        two_forward,
        [shaped((n_rows, n_mid), bf16), shaped((n_mid, n_rows), bf16), shaped((n_mid, n_rows), f32)],
        [act_one] + [second[k] for k in planes],
        "two_forward",
    )
    passed_on(third, n_mp, act_one)
    evens = list(range(0, n_dp, 2))
    bits = [1 << i for i in range(1, n_dp.bit_length() - 1)]
    orders = [bits, bits[::-1]]
    kept = half * rows
    slope_one = on_core(
        part(one_slope, tile=128), shaped((width, n_rows), bf16), [inputs, first], "one_slope",
        flops=12_000_000_000,
    )
    terms = []
    ahead = [wanted[1]] + [third[k] for k in planes if k and not parent(k)]
    for ks in groups:
        cols = len(ks) * n_top
        weights = after(ahead, *[third[k] for k in ks])
        away = on_core(
            part(three_away, kept=kept), shaped((kept, cols), bf16), [act_two, *weights], "three_away"
        )
        left = half // 2
        kinds = [shaped(((left - 1) * rows, cols // 2), f32), shaped((left * rows, cols // 2), bf16)]
        own, *halves = on_core(
            part(three_home, n_third=len(ks), orders=orders, kept=evens),
            [shaped((rows, cols), f32)] + kinds * 2,
            [act_two, swap(away, "dp", 1), *weights],
            "three_home",
        )
        ahead = []
        for stage in range(len(bits)):
            sends = halves[1::2] if len(halves) == 4 else halves
            gots = [swap(send, "dp", order[stage]) for send, order in zip(sends, orders)]
            ahead = ahead or [slope_one, *gots]
            if stage + 1 == len(bits):
                break
            keeps, left = halves[::2], left // 2
            kinds = [shaped((left * rows, cols // 2), bf16)]
            if left > 1:
                kinds = [shaped(((left - 1) * rows, cols // 2), f32)] + kinds
            own, *halves = on_core(
                part(three_pass, stage=stage + 1, orders=orders, kept=evens),
                [shaped((rows, cols), f32)] + kinds * 2,
                [own, keeps[0], gots[0], keeps[1], gots[1]],
                "three_pass",
            )
        terms += [own, *gots]
    *deltas, grad_four = on_core(
        part(error_step, groups=len(groups), half=half, per=per, n_in=n_in, n_out=n_out),
        [shaped((rows, len(ks) * n_top // 2), bf16) for ks in groups for _ in range(2)]
        + [shaped((tall, width), f32)],
        [inputs, *wanted, fourth, *terms],
        "error_step",
        scratch=[pltpu.VMEM((rows, width), bf16), pltpu.VMEM((rows, width), f32)],
    )

    sum_two, grad_three = None, {}
    gathers = {}
    for g in reversed(range(len(groups))):
        held, kinds = [[0], [0]], []
        arrays = list(deltas[2 * g : 2 * g + 2])
        cols = arrays[0].shape[1]
        for stage in range(len(bits)):
            last = stage + 1 == len(bits)
            gots = [swap(value, "dp", order[stage]) for value, order in zip(arrays, orders)]
            more = [[k | order[stage] for k in blocks] for blocks, order in zip(held, orders)]
            if last:
                break
            held = [a + b for a, b in zip(held, more)]
            spare = 16 * (g == 0 and stage + 2 == len(bits))
            arrays = [
                on_core(join, shaped((len(blocks) * rows + spare, cols), bf16), [own, got], "join")
                for blocks, own, got in zip(held, arrays, gots)
            ]
            gathers[g, stage] = gots
        gathers[g] = (arrays, gots, [held[0], more[0], held[1], more[1]])
    for g in reversed(range(len(groups))):
        ks, carried = groups[g], sum_two is not None
        arrays, gots, blocks = gathers[g]
        if carried:
            gots = after((sum_two, firsts[0]), *gots)
        elif (0, 0) in gathers:
            gots = after(gathers[0, 0], *gots)
        home = on_core(
            part(join_all, held=blocks, evens=evens, rows=rows),
            shaped((kept, len(ks) * n_top), bf16),
            [arrays[0], gots[0], arrays[1], gots[1]],
            "join_all",
        )
        away = swap(home, "dp", 1)
        carry = [sum_two] if carried else []
        if not carried:
            grad_three[ks[-1]] = on_core(
                part(three_first, column=(len(ks) - 1) * n_top),
                shaped((n_mid, n_top), bf16),
                [act_two_t, home, away],
                "three_first",
            )
        made = ks if carried else ks[:-1]
        sum_two, *grads = on_core(
            part(three_back, ks=ks, carried=len(carry), ready=len(ks) - len(made)),
            [shaped((n_mid, n_rows), f32)]
            + [shaped((n_mid, n_top), bf16 if k else f32) for k in made],
            [act_two_t, home, away] + [third[k] for k in ks] + carry,
            "three_back",
            scratch=[pltpu.VMEM((n_rows, len(ks) * n_top), bf16)],
        )
        grad_three.update(zip(made, grads))
        if not carried:
            firsts = []
            gots_three = summed(grad_three, ks, firsts)
    delta_two, farthest = on_core(
        two_first,
        [shaped((n_mid, n_rows), bf16), shaped((hidden, n_mid), bf16)],
        [sum_two, slope_two, act_one],
        "two_first",
        flops=LONG,
    )
    grads = on_core(
        two_back,
        [shaped((hidden, n_mid), bf16 if k else f32) for k in planes[:-1]],
        [delta_two, act_one],
        "two_back",
    )
    grad_two = dict(zip(planes, [*grads, farthest]))
    far = n_mp - 1
    got = swap(grad_two[far], "mp", 1)
    grad_two[far - 1] = on_core(add_up, shaped(got.shape, bf16), [grad_two[far - 1], got], "add_up")
    grad_two[1], grad_three[1] = after(grad_two[far - 1], grad_two[1], grad_three[1])
    gots_two = summed(grad_two, planes[: n_mp - 1])
    early_three = list(gots_three)
    gots_three += summed(grad_three, groups[0])
    like = lambda value: shaped(value.shape, f32)
    new_top, mom_top = on_core(
        update_big, [like(weight_top)] * 2, [weight_top, moment_top, grad_three[0], *gots_three], "update_top",
        flops=2_000_000_000,
    )
    n_small = up_to(n_in + n_out, 16)
    shape = (half, n_small, n_mp * wide)
    keep, send = on_core(
        part(one_back, n_mp=n_mp, n_dp=n_dp, places=places, n_in=n_in, n_out=n_out),
        [shaped(shape, f32), shaped(shape, bf16)],
        [inputs, delta_two, slope_one, grad_four] + [second[k] for k in planes],
        "one_back",
        flops=LONG,
    )
    step = 1
    while step < half:
        got = swap(send, "dp", step)
        if step == 1:
            got = after(early_three, got)[0]
        step *= 2
        shape = (shape[0] // 2, *shape[1:])
        keep, send = on_core(
            part(halve, step=step), [shaped(shape, f32), shaped(shape, bf16)], [keep, got], "halve"
        )
    got = swap(send, "dp", step)
    half_mp = n_mp // 2 * wide
    keep, send = on_core(
        last_half,
        [shaped((n_small, half_mp), f32), shaped((n_small, half_mp), bf16)],
        [keep, got],
        "last_half",
    )
    step = n_mp // 2
    while step:
        got = swap(send, "mp", step)
        step //= 2
        if step:
            got = after((gots_two, mom_top), got)[0]
        if step:
            half_mp = step * wide
            keep, send = on_core(
                last_half_mp,
                [shaped((n_small, half_mp), f32), shaped((n_small, half_mp), bf16)],
                [keep, got],
                "last_half_mp",
            )
    gots_small = [got]

    flat = (weight_in, weight_out.T, moment_in, moment_out.T)
    new_in, new_out, mom_in, mom_out = on_core(
        update_small, [like(value) for value in flat], [keep, *gots_small, *flat], "update_small"
    )
    new_mid, mom_mid = on_core(
        update_big, [like(weight_mid)] * 2, [weight_mid, moment_mid, grad_two[0], *gots_two], "update_mid"
    )
    return (new_in, new_mid, new_top, new_out.T, mom_in, mom_mid, mom_top, mom_out.T)


def solution(mesh):
    in_specs = (
        P("dp", None, None),
        P("dp", None, None),
        P("dp"),
        P(None, ("mp", "dp")),
        P("mp", "dp"),
        P("dp", "mp"),
        P(("mp", "dp"), None),
        P(None, ("mp", "dp")),
        P("mp", "dp"),
        P("dp", "mp"),
        P(("mp", "dp"), None),
    )
    out_specs = (
        P(None, ("mp", "dp")),
        P("mp", "dp"),
        P("dp", "mp"),
        P(("mp", "dp"), None),
        P(None, ("mp", "dp")),
        P("mp", "dp"),
        P("dp", "mp"),
        P(("mp", "dp"), None),
    )
    return jax.shard_map(
        on_device, mesh=mesh, in_specs=in_specs, out_specs=out_specs, check_vma=False
    )
```

```python
import functools
import math

import jax
import jax.numpy as jnp
from jax import lax
from jax.experimental import pallas as pl
from jax.experimental.pallas import tpu as pltpu
from jax.sharding import PartitionSpec as P

momentum_decay = 0.9
learn_rate = 0.05
bf16 = jnp.bfloat16
f32 = jnp.float32
VMEM_BYTES = 24 << 20
LONG = 100_000_000_000


def swap(value, axis, step):
    count = lax.axis_size(axis)
    return lax.ppermute(value, axis, [(at, at ^ step) for at in range(count)])


def parent(k):
    return k & (k - 1)


def low_bit(k):
    return k & -k


def up_to(value, unit):
    return -(-value // unit) * unit


def gelu_act(value):
    return 0.5 * value * (1.0 + lax.erf(value * math.sqrt(0.5)))


def gelu_slope(value):
    return 0.5 * (1.0 + lax.erf(value * math.sqrt(0.5))) + value * jnp.exp(
        -0.5 * value * value
    ) * (1.0 / math.sqrt(2.0 * math.pi))


def dot(left, right, at_left, at_right):
    dims = (((at_left,), (at_right,)), ((), ()))
    return lax.dot_general(left, right, dims, preferred_element_type=f32)


def shaped(dims, kind):
    return jax.ShapeDtypeStruct(dims, kind)


def on_core(body, outs, args, name, flops=0, scratch=(), scalars=()):
    at = pl.BlockSpec(memory_space=pltpu.VMEM)
    return pl.pallas_call(
        body,
        out_shape=outs,
        in_specs=[pl.BlockSpec(memory_space=pltpu.SMEM)] * len(scalars) + [at] * len(args),
        out_specs=jax.tree.map(lambda _: at, outs),
        scratch_shapes=list(scratch),
        compiler_params=pltpu.CompilerParams(vmem_limit_bytes=VMEM_BYTES),
        cost_estimate=pl.CostEstimate(flops=flops, bytes_accessed=0, transcendentals=0),
        name=name,
    )(*scalars, *args)


def pack_small(w_in, w_out, out, *, tall):
    n_in, wide = w_in.shape
    n_out = w_out.shape[0]
    left = jnp.concatenate([w_in[...], jnp.zeros((tall - n_in, wide), f32)], 0)
    right = jnp.concatenate([w_out[...], jnp.zeros((tall - n_out, wide), f32)], 0)
    parts = [left, right]
    spare = out.shape[1] - 2 * wide
    if spare:
        parts.append(jnp.zeros((tall, spare), f32))
    out[...] = jnp.concatenate(parts, 1).astype(bf16)


def pick_rows(count, samples, targets, out, wanted, *, tall, rows, per):
    slots, n_in, block = samples.shape
    n_out = targets.shape[1]
    half = lax.axis_size("dp") // 2
    high = lax.axis_index("dp") >= half
    xs, ys = [], []
    for j in range(per):
        at = per * lax.axis_index("mp") + j
        slot = jnp.where(high, slots - 1 - at, at)
        keep = slot < count[0]
        for source, last, all_of in (
            (samples, jnp.full((1, block), count[0].astype(f32)), xs),
            (targets, jnp.full((1, block), keep.astype(f32)), ys),
        ):
            value = source[slot].astype(f32)
            parts = [jnp.where(keep, value, jnp.zeros_like(value)), last]
            spare = tall - value.shape[0] - 1
            if spare:
                parts.append(jnp.zeros((spare, block), f32))
            all_of.append(jnp.concatenate(parts, 0).astype(bf16))
    x = jnp.concatenate(xs, 1) if per > 1 else xs[0]
    y = jnp.concatenate(ys, 1) if per > 1 else ys[0]
    spare = out.shape[1] - rows
    for t in range(2):
        at = slice(t * rows, (t + 1) * rows)
        half_x = x[:, at]
        if spare:
            half_x = jnp.concatenate([half_x, jnp.zeros((tall, spare), bf16)], 1)
        out[tall * t : tall * (t + 1)] = half_x
        wanted[t] = y[:, at]


def pack_all(*refs):
    out, at = refs[-1], 0
    for part in refs[:-1]:
        out[at : at + part.shape[0]] = part[...]
        at += part.shape[0]


def place_small(held, inputs, first, fourth, number, *, n_in, tall, rows, wide, places):
    n_dp, n_mp = lax.axis_size("dp"), lax.axis_size("mp")
    half = n_dp // 2
    total = held[0, n_in : n_in + 1].astype(f32)
    for d in range(1, n_dp):
        total = total + held[d, n_in : n_in + 1].astype(f32)
    number[...] = total
    for place, k in enumerate(range(0, n_dp, 2)):
        at = lax.axis_index("dp") ^ k
        high = at >= half
        pair = jnp.where(high, at - half, at)
        both = held[pair, : 2 * tall] + held[pair + half, : 2 * tall]
        value = jnp.where(high, both[tall:], both[:tall])
        inputs[:, place * rows : (place + 1) * rows] = value[:, :rows]
    hidden = n_dp * wide
    for k in range(n_mp):
        row = slice((2 + k) * tall, (3 + k) * tall)
        pieces = [held[d, row] for d in range(n_dp)]
        at = slice(k * hidden, (k + 1) * hidden)
        first[:, at] = jnp.concatenate([piece[:, :wide] for piece in pieces], 1)
        at = slice(places.index(k) * hidden, (places.index(k) + 1) * hidden)
        fourth[:, at] = jnp.concatenate([piece[:, wide : 2 * wide] for piece in pieces], 1)


def one_forward(inputs, first, out, *, tile):
    n_rows = inputs.shape[1]
    cut = min(256, n_rows)

    def step(i, _):
        at = pl.ds(pl.multiple_of(i * tile, tile), tile)
        weights = first[:, at].T
        for c in range(0, n_rows, cut):
            pre = dot(weights, inputs[:, c : c + cut], 1, 0)
            out[at, c : c + cut] = gelu_act(pre).astype(bf16)
        return 0

    lax.fori_loop(0, first.shape[1] // tile, step, 0)


def one_slope(inputs, first, out, *, tile):
    n_rows = inputs.shape[1]
    cut = min(256, n_rows)

    def step(i, _):
        at = pl.ds(pl.multiple_of(i * tile, tile), tile)
        weights = first[:, at].T
        for c in range(0, n_rows, cut):
            pre = dot(weights, inputs[:, c : c + cut], 1, 0)
            out[at, c : c + cut] = gelu_slope(pre).astype(bf16)
        return 0

    lax.fori_loop(0, first.shape[1] // tile, step, 0)


def two_forward(act_one, near, far, near_too, far_too, act, act_t, slope):
    n_rows = act_one.shape[1]
    cut = min(256, n_rows)
    first, cols = near.shape
    for side, (left, right) in enumerate(((near, far), (near_too, far_too))):
        to = slice(side * cols, (side + 1) * cols)
        left, right = left[...].T, right[...].T
        for c in range(0, n_rows, cut):
            at = slice(c, c + cut)
            pre = dot(left, act_one[:first, at], 1, 0) + dot(right, act_one[first:, at], 1, 0)
            value = gelu_act(pre)
            act_t[to, at] = value.astype(bf16)
            act[at, to] = value.T.astype(bf16)
            slope[to, at] = gelu_slope(pre)


def divided(kept, bit):
    return [k for k in kept if not k & bit]


def three_home(act, *refs, n_third, orders, kept):
    thirds, own, outs = refs[:n_third], refs[n_third], refs[n_third + 1 :]
    rows = own.shape[0]
    mid, span = thirds[0].shape
    blocks = {k: slice(i * rows, (i + 1) * rows) for i, k in enumerate(kept)}
    half = own.shape[1] // 2
    step = math.gcd(span, half)
    for at in range(0, own.shape[1], step):
        left, right = thirds[at // span], thirds[n_third // 2 + at // span]
        cut = slice(at % span, at % span + step)
        total = dot(act[:, :mid], left[:, cut], 1, 0) + dot(act[:, mid:], right[:, cut], 1, 0)
        own[:, at : at + step] = total[blocks[0]]
        part = at // half
        keep, send = outs[2 * part], outs[2 * part + 1]
        put = slice(at - part * half, at - part * half + step)
        bit = orders[part][0]
        for i, k in enumerate(divided(kept, bit)):
            if k:
                keep[(i - 1) * rows : i * rows, put] = total[blocks[k]]
            send[i * rows : (i + 1) * rows, put] = total[blocks[k | bit]].astype(bf16)


def three_pass(own, *refs, stage, orders, kept):
    ins, new_own, outs = refs[:4], refs[4], refs[5:]
    rows = own.shape[0]
    half = own.shape[1] // 2
    for part, order in enumerate(orders):
        here = list(kept)
        for bit in order[:stage]:
            here = divided(here, bit)
        keep, got = ins[2 * part], ins[2 * part + 1]
        at = slice(part * half, (part + 1) * half)
        total = {}
        for i, k in enumerate(here):
            value = own[:, at] if k == 0 else keep[(i - 1) * rows : i * rows]
            total[k] = value + got[i * rows : (i + 1) * rows].astype(f32)
        new_own[:, at] = total[0]
        bit = order[stage]
        send = outs[2 * part + 1] if len(outs) == 4 else outs[part]
        for i, k in enumerate(divided(here, bit)):
            if k:
                outs[2 * part][(i - 1) * rows : i * rows] = total[k]
            send[i * rows : (i + 1) * rows] = total[k | bit].astype(bf16)


def error_step(number, wanted, wanted_too, fourth, *refs, widths, half, block, n_out):
    groups = len(widths)
    terms = refs[: 3 * groups]
    act, pre = refs[-2:]
    deltas, grad_four = refs[3 * groups : 5 * groups], refs[-3]
    start = 0
    spots = []
    for g, width in enumerate(widths):
        for part in range(2):
            at = slice(start, start + width)
            start += width
            spots.append(at)
            total = terms[3 * g][:, part * width : (part + 1) * width]
            total = total + terms[3 * g + 1 + part][...].astype(f32)
            pre[:, at] = total
            act[:, at] = gelu_act(total).astype(bf16)
    predicted = dot(fourth[...], act[...], 1, 1)
    mine = jnp.where(lax.axis_index("dp") >= half, 1, 0)
    wanted = wanted[mine] + wanted_too[mine]
    live = wanted[n_out : n_out + 1, :].astype(f32)
    error = (2.0 / (number[:, :1] * block) * (predicted - wanted.astype(f32)) * live).astype(bf16)
    row = lax.broadcasted_iota(jnp.int32, error.shape, 0)
    error = jnp.where(row < n_out, error, jnp.zeros_like(error))
    grad_four[...] = dot(error, act[...], 1, 0)
    turned = error.astype(f32).T.astype(bf16)
    for at, delta in zip(spots, deltas):
        value = dot(turned, fourth[:, at], 1, 0) * gelu_slope(pre[:, at])
        delta[...] = value.astype(bf16)


def join(own, got, out):
    rows = own.shape[0]
    out[:rows] = own[...]
    filled = rows + got.shape[0]
    out[rows:filled] = got[...]
    if filled < out.shape[0]:
        out[filled:] = jnp.zeros((out.shape[0] - filled, out.shape[1]), out.dtype)


def lay(*refs, axis):
    out, at = refs[-1], 0
    for value in refs[:-1]:
        to = at + value.shape[axis]
        if axis:
            out[:, at:to] = value[...]
        else:
            out[at:to] = value[...]
        at = to


def join_all(*refs, held, evens, rows):
    out = refs[-1]
    half = out.shape[1] // 2
    for i, blocks in enumerate(held):
        for j, k in enumerate(blocks):
            to = evens.index(k) * rows
            at = slice(i // 2 * half, (i // 2 + 1) * half)
            out[to : to + rows, at] = refs[i][j * rows : (j + 1) * rows]


def three_away(act_t, whole, away):
    mid = act_t.shape[0] // 2
    away[...] = dot(act_t[mid:], whole[...], 1, 0).astype(bf16)


def three_own(act_t, whole, got, *grads):
    mid = act_t.shape[0] // 2
    span = grads[0].shape[1]
    for i, grad in enumerate(grads):
        at = slice(i * span, (i + 1) * span)
        value = dot(act_t[:mid], whole[:, at], 1, 0) + got[:, at].astype(f32)
        grad[...] = value.astype(grad.dtype)


def three_back(whole, *refs, n_third):
    thirds, before, sum_two = refs[:n_third], refs[n_third:-1], refs[-1]
    mid, span = thirds[0].shape
    for side in range(2):
        to = slice(side * mid, (side + 1) * mid)
        total = before[0][to] if before else None
        for i, third in enumerate(thirds[side * n_third // 2 : (side + 1) * n_third // 2]):
            term = dot(third[...], whole[:, i * span : (i + 1) * span], 1, 1)
            total = term if total is None else total + term
        sum_two[to] = total


def two_first(sum_two, slope, act_one, delta, away_far, away):
    value = (sum_two[...] * slope[...]).astype(bf16)
    delta[...] = value
    mid, near = delta.shape[0] // 2, away.shape[0]
    away_far[...] = dot(act_one[near:], value[mid:], 1, 1).astype(bf16)
    away[...] = dot(act_one[:near], value[mid:], 1, 1).astype(bf16)


def two_own(delta, act_one, got, *grads, start):
    mid, span = delta.shape[0] // 2, grads[0].shape[0]
    for i, grad in enumerate(grads):
        at = slice(i * span, (i + 1) * span)
        rows = slice(start + i * span, start + (i + 1) * span)
        value = dot(act_one[rows], delta[:mid], 1, 1) + got[at].astype(f32)
        grad[...] = value.astype(grad.dtype)


def split_dp(parts, step, keep, send):
    bit = (lax.axis_index("dp") & step) != 0
    for i in range(len(parts) // 2):
        even, odd = parts[2 * i], parts[2 * i + 1]
        keep[i] = jnp.where(bit, odd, even)
        send[i] = jnp.where(bit, even, odd).astype(bf16)


def one_back(
    inputs, delta, slope, grad_four, near, far, near_too, far_too, keep, send, *, n_dp, places, n_in, n_out
):
    span = far.shape[0]
    n_mp = near.shape[0] // span + 1
    wide = span // n_dp
    mid = delta.shape[0] // 2
    whole = []
    for k in range(n_mp):
        at = slice(k * span, (k + 1) * span)
        left, right = (near[at], near_too[at]) if k + 1 < n_mp else (far[...], far_too[...])
        value = dot(left, delta[:mid], 1, 0) + dot(right, delta[mid:], 1, 0)
        value = (value * slope[k * span : (k + 1) * span].astype(f32)).astype(bf16)
        grad_one = dot(inputs[...], value, 1, 1)
        at = places.index(k) * span
        pieces = [grad_one[:n_in], grad_four[:n_out, at : at + span]]
        spare = keep.shape[1] - n_in - n_out
        if spare:
            pieces.append(jnp.zeros((spare, span), f32))
        whole.append(jnp.concatenate(pieces, 0))
    parts = [
        jnp.concatenate([value[:, d * wide : (d + 1) * wide] for value in whole], 1)
        for d in range(n_dp)
    ]
    split_dp(parts, 1, keep, send)


def halve(own, got, keep, send, *, step):
    split_dp([own[i] + got[i].astype(f32) for i in range(own.shape[0])], step, keep, send)


def last_half(own, got, keep, send):
    total = own[0] + got[0].astype(f32)
    wide = keep.shape[1]
    keep[...] = total[:, :wide]
    send[...] = total[:, wide:].astype(bf16)


def last_half_mp(own, got, keep, send):
    total = own[...] + got[...].astype(f32)
    wide = keep.shape[1]
    keep[...] = total[:, :wide]
    send[...] = total[:, wide:].astype(bf16)


def add_up(own, got, out):
    out[...] = (own[...].astype(f32) + got[...].astype(f32)).astype(out.dtype)


def update_small(own, *refs):
    gots, (w_in, w_out, m_in, m_out), outs = refs[:-8], refs[-8:-4], refs[-4:]
    nw_in, nw_out, nm_in, nm_out = outs
    total = own[...]
    for got in gots:
        total = total + got[...].astype(f32)
    n_in, n_out = w_in.shape[0], w_out.shape[0]
    mom = momentum_decay * m_in[...] + total[:n_in]
    nm_in[...] = mom
    nw_in[...] = w_in[...] - learn_rate * mom
    mom = momentum_decay * m_out[...] + total[n_in : n_in + n_out]
    nm_out[...] = mom
    nw_out[...] = w_out[...] - learn_rate * mom


def update_big(weight, moment, own, *refs):
    gots, (new_weight, new_moment) = refs[:-2], refs[-2:]
    total = own[...]
    for got in gots:
        total = total + got[...].astype(f32)
    mom = momentum_decay * moment[...] + total
    new_moment[...] = mom
    new_weight[...] = weight[...] - learn_rate * mom


def after(first, *values):
    return lax.optimization_barrier((first, *values))[1:]


def laid(values, axis):
    shape = list(values[0].shape)
    shape[axis] *= len(values)
    return on_core(functools.partial(lay, axis=axis), shaped(tuple(shape), bf16), values, "lay")


def gathered(own, n_mp):
    held = {0: own}
    for k in [k for k in range(1, n_mp) if parent(k) == 0][::-1]:
        held[k] = swap(own, "mp", k)
    return held


def passed_on(held, n_mp, ready):
    for k in sorted((k for k in range(1, n_mp) if parent(k)), key=lambda k: -low_bit(k)):
        held[k] = swap(after(ready, held[parent(k)])[0], "mp", low_bit(k))


def summed(held, ks):
    gots = []
    for k in sorted((k for k in ks if k), key=lambda k: (low_bit(k), -k)):
        got = swap(held[k], "mp", low_bit(k))
        to = parent(k)
        if to:
            held[to] = on_core(add_up, shaped(got.shape, bf16), [held[to], got], "add_up")
        else:
            gots.append(got)
    return gots


def on_device(
    samples,
    targets,
    counts,
    weight_in,
    weight_mid,
    weight_top,
    weight_out,
    moment_in,
    moment_mid,
    moment_top,
    moment_out,
):
    slots, n_in, block = samples.shape
    n_out = targets.shape[1]
    n_dp, n_mp = lax.axis_size("dp"), lax.axis_size("mp")
    half = n_dp // 2
    per = slots // n_mp
    rows = per * block // 2
    n_rows = half * rows
    wide = weight_in.shape[1]
    lanes = max(rows, 2 * wide)
    tall = up_to(max(n_in, n_out) + 1, 16)
    hidden = wide * n_dp
    width = hidden * n_mp
    n_mid, n_top = weight_mid.shape[1], weight_top.shape[1]
    planes = range(n_mp)
    groups = [list(planes[:-1]), [n_mp - 1]]
    places = [k for ks in groups for k in ks]
    part = functools.partial

    piece = on_core(
        part(pack_small, tall=tall), shaped((tall, lanes), bf16), [weight_in, weight_out.T], "pack_small"
    )
    second = gathered(weight_mid.astype(bf16), n_mp)
    picked, wanted = on_core(
        part(pick_rows, tall=tall, rows=rows, per=per),
        [shaped((2 * tall, lanes), bf16), shaped((2, tall, rows), bf16)],
        [samples, targets],
        "pick_rows",
        scalars=[counts],
    )
    pieces = [piece] + [swap(piece, "mp", k) for k in planes[1:]]
    top = after((picked, pieces), weight_top.astype(bf16))[0]
    third = gathered(top, n_mp)
    early = [second[k] for k in planes if k and not parent(k)]
    passed_on(second, n_mp, (picked, pieces))

    packed = on_core(
        pack_all,
        shaped(((2 + n_mp) * tall, lanes), bf16),
        [picked, *after(early, *pieces)],
        "pack_all",
    )
    wanted = [wanted, swap(wanted, "dp", half)]
    held = lax.all_gather(packed, "dp")
    inputs, first, fourth, number = on_core(
        part(place_small, n_in=n_in, tall=tall, rows=rows, wide=wide, places=places),
        [
            shaped((tall, n_rows), bf16),
            shaped((tall, width), bf16),
            shaped((tall, width), bf16),
            shaped((1, lanes), f32),
        ],
        [held],
        "place_small",
    )

    act_one = on_core(
        part(one_forward, tile=256), shaped((width, n_rows), bf16), [inputs, first], "one_forward"
    )
    wide_mid = 2 * n_mid
    near = laid(after((picked, pieces), *[second[k] for k in planes[:-1]]), 0)
    third_early = [third[k] for k in planes if k and not parent(k)]
    far = after((act_one, third_early, wanted[1]), second[n_mp - 1])[0]
    second_all = [near, far, swap(near, "dp", 1), swap(far, "dp", 1)]
    act_two, act_two_t, slope_two = on_core(
        two_forward,
        [shaped((n_rows, wide_mid), bf16), shaped((wide_mid, n_rows), bf16), shaped((wide_mid, n_rows), f32)],
        [act_one, *second_all],
        "two_forward",
    )
    passed_on(third, n_mp, act_two)
    third_too = {k: swap(after(act_one, third[k])[0] if k else top, "dp", 1) for k in planes}
    third_all = [[third[k] for k in ks] + [third_too[k] for k in ks] for ks in groups]
    evens = list(range(0, n_dp, 2))
    bits = [1 << i for i in range(1, n_dp.bit_length() - 1)]
    orders = [bits, bits[::-1]]
    slope_one = on_core(
        part(one_slope, tile=256), shaped((width, n_rows), bf16), [inputs, first], "one_slope",
        flops=12_000_000_000,
    )
    terms = []
    ahead = [third[k] for k in planes if k and not parent(k)]
    for ks, weights in zip(groups, third_all):
        cols = len(ks) * n_top
        weights = after(ahead, *weights)
        left = half // 2
        kinds = [shaped(((left - 1) * rows, cols // 2), f32), shaped((left * rows, cols // 2), bf16)]
        own, *halves = on_core(
            part(three_home, n_third=len(weights), orders=orders, kept=evens),
            [shaped((rows, cols), f32)] + kinds * 2,
            [act_two, *weights],
            "three_home",
        )
        ahead = []
        for stage in range(len(bits)):
            sends = halves[1::2] if len(halves) == 4 else halves
            gots = [swap(send, "dp", order[stage]) for send, order in zip(sends, orders)]
            ahead = ahead or [slope_one, *gots]
            if stage + 1 == len(bits):
                break
            keeps, left = halves[::2], left // 2
            kinds = [shaped((left * rows, cols // 2), bf16)]
            if left > 1:
                kinds = [shaped(((left - 1) * rows, cols // 2), f32)] + kinds
            own, *halves = on_core(
                part(three_pass, stage=stage + 1, orders=orders, kept=evens),
                [shaped((rows, cols), f32)] + kinds * 2,
                [own, keeps[0], gots[0], keeps[1], gots[1]],
                "three_pass",
            )
        terms += [own, *gots]
    *deltas, grad_four = on_core(
        part(error_step, widths=[len(ks) * n_top // 2 for ks in groups], half=half, block=block, n_out=n_out),
        [shaped((rows, len(ks) * n_top // 2), bf16) for ks in groups for _ in range(2)]
        + [shaped((tall, width), f32)],
        [number, *wanted, fourth, *terms],
        "error_step",
        scratch=[pltpu.VMEM((rows, width), bf16), pltpu.VMEM((rows, width), f32)],
    )

    sum_two, grad_three = None, {}
    gathers = {}
    for g in reversed(range(len(groups))):
        held, kinds = [[0], [0]], []
        arrays = list(deltas[2 * g : 2 * g + 2])
        cols = arrays[0].shape[1]
        for stage in range(len(bits)):
            last = stage + 1 == len(bits)
            gots = [swap(value, "dp", order[stage]) for value, order in zip(arrays, orders)]
            more = [[k | order[stage] for k in blocks] for blocks, order in zip(held, orders)]
            if last:
                break
            held = [a + b for a, b in zip(held, more)]
            spare = 16 * (g == 0 and stage + 2 == len(bits))
            arrays = [
                on_core(join, shaped((len(blocks) * rows + spare, cols), bf16), [own, got], "join")
                for blocks, own, got in zip(held, arrays, gots)
            ]
            gathers[g, stage] = gots
        gathers[g] = (arrays, gots, [held[0], more[0], held[1], more[1]])
    for g in reversed(range(len(groups))):
        ks, carried = groups[g], sum_two is not None
        arrays, gots, blocks = gathers[g]
        if carried:
            gots = after((sum_two, got_far), *gots)
        elif (0, 0) in gathers:
            gots = after(gathers[0, 0], *gots)
        whole = on_core(
            part(join_all, held=blocks, evens=evens, rows=rows),
            shaped((n_rows, len(ks) * n_top), bf16),
            [arrays[0], gots[0], arrays[1], gots[1]],
            "join_all",
        )
        away = on_core(
            three_away, shaped((n_mid, len(ks) * n_top), bf16), [act_two_t, whole], "three_away"
        )
        away = swap(away, "dp", 1)
        sum_two = on_core(
            part(three_back, n_third=2 * len(ks)),
            shaped((wide_mid, n_rows), f32),
            [whole, *third_all[g]] + ([sum_two] if carried else []),
            "three_back",
        )
        grads = on_core(
            three_own,
            [shaped((n_mid, n_top), bf16 if k else f32) for k in ks],
            [act_two_t, whole, away],
            "three_own",
        )
        grad_three.update(zip(ks, grads))
        if not carried:
            got_far = swap(grads[0], "mp", 1)
    far = n_mp - 1
    grad_three[far - 1] = on_core(
        add_up, shaped(got_far.shape, bf16), [grad_three[far - 1], got_far], "add_up"
    )
    delta_two, away_far, away = on_core(
        two_first,
        [
            shaped((wide_mid, n_rows), bf16),
            shaped((hidden, n_mid), bf16),
            shaped((far * hidden, n_mid), bf16),
        ],
        [sum_two, slope_two, act_one],
        "two_first",
        flops=LONG,
    )
    (farthest,) = on_core(
        part(two_own, start=far * hidden),
        [shaped((hidden, n_mid), bf16)],
        [delta_two, act_one, swap(away_far, "dp", 1)],
        "two_own",
    )
    grads = on_core(
        part(two_own, start=0),
        [shaped((hidden, n_mid), bf16 if k else f32) for k in planes[:-1]],
        [delta_two, act_one, swap(away, "dp", 1)],
        "two_own",
    )
    grad_two = dict(zip(planes, [*grads, farthest]))
    got = swap(grad_two[far], "mp", 1)
    grad_two[far - 1] = on_core(add_up, shaped(got.shape, bf16), [grad_two[far - 1], got], "add_up")
    grad_two[1], grad_three[1] = after(grad_two[far - 1], grad_two[1], grad_three[1])
    gots_two = summed(grad_two, planes[:far])
    gots_three = summed(grad_three, planes[:far])[::-1]
    like = lambda value: shaped(value.shape, f32)
    new_top, mom_top = on_core(
        update_big, [like(weight_top)] * 2, [weight_top, moment_top, grad_three[0], *gots_three], "update_top",
        flops=2_000_000_000,
    )
    n_small = up_to(n_in + n_out, 16)
    shape = (half, n_small, n_mp * wide)
    keep, send = on_core(
        part(one_back, n_dp=n_dp, places=places, n_in=n_in, n_out=n_out),
        [shaped(shape, f32), shaped(shape, bf16)],
        [inputs, delta_two, slope_one, grad_four, *second_all],
        "one_back",
        flops=LONG,
    )
    step = 1
    while step < half:
        got = swap(send, "dp", step)
        if step == 1:
            got = after(gots_three[0], got)[0]
        step *= 2
        shape = (shape[0] // 2, *shape[1:])
        keep, send = on_core(
            part(halve, step=step), [shaped(shape, f32), shaped(shape, bf16)], [keep, got], "halve"
        )
    got = swap(send, "dp", step)
    half_mp = n_mp // 2 * wide
    keep, send = on_core(
        last_half,
        [shaped((n_small, half_mp), f32), shaped((n_small, half_mp), bf16)],
        [keep, got],
        "last_half",
    )
    step = n_mp // 2
    while step:
        got = swap(send, "mp", step)
        step //= 2
        if step:
            got = after((gots_two, mom_top), got)[0]
        if step:
            half_mp = step * wide
            keep, send = on_core(
                last_half_mp,
                [shaped((n_small, half_mp), f32), shaped((n_small, half_mp), bf16)],
                [keep, got],
                "last_half_mp",
            )
    gots_small = [got]

    flat = (weight_in, weight_out.T, moment_in, moment_out.T)
    new_in, new_out, mom_in, mom_out = on_core(
        update_small, [like(value) for value in flat], [keep, *gots_small, *flat], "update_small"
    )
    new_mid, mom_mid = on_core(
        update_big, [like(weight_mid)] * 2, [weight_mid, moment_mid, grad_two[0], *gots_two], "update_mid"
    )
    return (new_in, new_mid, new_top, new_out.T, mom_in, mom_mid, mom_top, mom_out.T)


def solution(mesh):
    in_specs = (
        P("dp", None, None),
        P("dp", None, None),
        P("dp"),
        P(None, ("mp", "dp")),
        P("mp", "dp"),
        P("dp", "mp"),
        P(("mp", "dp"), None),
        P(None, ("mp", "dp")),
        P("mp", "dp"),
        P("dp", "mp"),
        P(("mp", "dp"), None),
    )
    out_specs = (
        P(None, ("mp", "dp")),
        P("mp", "dp"),
        P("dp", "mp"),
        P(("mp", "dp"), None),
        P(None, ("mp", "dp")),
        P("mp", "dp"),
        P("dp", "mp"),
        P(("mp", "dp"), None),
    )
    return jax.shard_map(
        on_device, mesh=mesh, in_specs=in_specs, out_specs=out_specs, check_vma=False
    )
```

```python
import functools
import math

import jax
import jax.numpy as jnp
from jax import lax
from jax.experimental import pallas as pl
from jax.experimental.pallas import tpu as pltpu
from jax.sharding import PartitionSpec as P

momentum_decay = 0.9
learn_rate = 0.05
bf16 = jnp.bfloat16
f32 = jnp.float32
VMEM_BYTES = 24 << 20
LONG = 100_000_000_000


def swap(value, axis, step):
    count = lax.axis_size(axis)
    return lax.ppermute(value, axis, [(at, at ^ step) for at in range(count)])


def parent(k):
    return k & (k - 1)


def low_bit(k):
    return k & -k


def up_to(value, unit):
    return -(-value // unit) * unit


def gelu_act(value):
    return 0.5 * value * (1.0 + lax.erf(value * math.sqrt(0.5)))


def gelu_slope(value):
    return 0.5 * (1.0 + lax.erf(value * math.sqrt(0.5))) + value * jnp.exp(
        -0.5 * value * value
    ) * (1.0 / math.sqrt(2.0 * math.pi))


def dot(left, right, at_left, at_right):
    dims = (((at_left,), (at_right,)), ((), ()))
    return lax.dot_general(left, right, dims, preferred_element_type=f32)


def shaped(dims, kind):
    return jax.ShapeDtypeStruct(dims, kind)


def on_core(body, outs, args, name, flops=0, scratch=(), scalars=()):
    at = pl.BlockSpec(memory_space=pltpu.VMEM)
    return pl.pallas_call(
        body,
        out_shape=outs,
        in_specs=[pl.BlockSpec(memory_space=pltpu.SMEM)] * len(scalars) + [at] * len(args),
        out_specs=jax.tree.map(lambda _: at, outs),
        scratch_shapes=list(scratch),
        compiler_params=pltpu.CompilerParams(vmem_limit_bytes=VMEM_BYTES),
        cost_estimate=pl.CostEstimate(flops=flops, bytes_accessed=0, transcendentals=0),
        name=name,
    )(*scalars, *args)


def pack_small(w_in, w_out, out, *, tall):
    n_in, wide = w_in.shape
    n_out = w_out.shape[0]
    left = jnp.concatenate([w_in[...], jnp.zeros((tall - n_in, wide), f32)], 0)
    right = jnp.concatenate([w_out[...], jnp.zeros((tall - n_out, wide), f32)], 0)
    parts = [left, right]
    spare = out.shape[1] - 2 * wide
    if spare:
        parts.append(jnp.zeros((tall, spare), f32))
    out[...] = jnp.concatenate(parts, 1).astype(bf16)


def pick_rows(count, samples, targets, out, wanted, *, tall, rows, per):
    slots, n_in, block = samples.shape
    n_out = targets.shape[1]
    half = lax.axis_size("dp") // 2
    high = lax.axis_index("dp") >= half
    xs, ys = [], []
    for j in range(per):
        at = per * lax.axis_index("mp") + j
        slot = jnp.where(high, slots - 1 - at, at)
        keep = slot < count[0]
        for source, last, all_of in (
            (samples, jnp.full((1, block), count[0].astype(f32)), xs),
            (targets, jnp.full((1, block), keep.astype(f32)), ys),
        ):
            value = source[slot].astype(f32)
            parts = [jnp.where(keep, value, jnp.zeros_like(value)), last]
            spare = tall - value.shape[0] - 1
            if spare:
                parts.append(jnp.zeros((spare, block), f32))
            all_of.append(jnp.concatenate(parts, 0).astype(bf16))
    x = jnp.concatenate(xs, 1) if per > 1 else xs[0]
    y = jnp.concatenate(ys, 1) if per > 1 else ys[0]
    spare = out.shape[1] - rows
    for t in range(2):
        at = slice(t * rows, (t + 1) * rows)
        half_x = x[:, at]
        if spare:
            half_x = jnp.concatenate([half_x, jnp.zeros((tall, spare), bf16)], 1)
        out[tall * t : tall * (t + 1)] = half_x
        wanted[t] = y[:, at]


def pack_all(*refs):
    out, at = refs[-1], 0
    for part in refs[:-1]:
        out[at : at + part.shape[0]] = part[...]
        at += part.shape[0]


def place_small(held, inputs, first, fourth, number, *, n_in, tall, rows, wide, places):
    n_dp, n_mp = lax.axis_size("dp"), lax.axis_size("mp")
    half = n_dp // 2
    total = held[0, n_in : n_in + 1].astype(f32)
    for d in range(1, n_dp):
        total = total + held[d, n_in : n_in + 1].astype(f32)
    number[...] = total
    for place, k in enumerate(range(0, n_dp, 2)):
        at = lax.axis_index("dp") ^ k
        high = at >= half
        pair = jnp.where(high, at - half, at)
        both = held[pair, : 2 * tall] + held[pair + half, : 2 * tall]
        value = jnp.where(high, both[tall:], both[:tall])
        inputs[:, place * rows : (place + 1) * rows] = value[:, :rows]
    hidden = n_dp * wide
    for k in range(n_mp):
        row = slice((2 + k) * tall, (3 + k) * tall)
        pieces = [held[d, row] for d in range(n_dp)]
        at = slice(k * hidden, (k + 1) * hidden)
        first[:, at] = jnp.concatenate([piece[:, :wide] for piece in pieces], 1)
        at = slice(places.index(k) * hidden, (places.index(k) + 1) * hidden)
        fourth[:, at] = jnp.concatenate([piece[:, wide : 2 * wide] for piece in pieces], 1)


def one_forward(inputs, first, out, *, tile):
    n_rows = inputs.shape[1]
    cut = min(256, n_rows)

    def step(i, _):
        at = pl.ds(pl.multiple_of(i * tile, tile), tile)
        weights = first[:, at].T
        for c in range(0, n_rows, cut):
            pre = dot(weights, inputs[:, c : c + cut], 1, 0)
            out[at, c : c + cut] = gelu_act(pre).astype(bf16)
        return 0

    lax.fori_loop(0, first.shape[1] // tile, step, 0)


def one_slope(inputs, first, out, *, tile):
    n_rows = inputs.shape[1]
    cut = min(256, n_rows)

    def step(i, _):
        at = pl.ds(pl.multiple_of(i * tile, tile), tile)
        weights = first[:, at].T
        for c in range(0, n_rows, cut):
            pre = dot(weights, inputs[:, c : c + cut], 1, 0)
            out[at, c : c + cut] = gelu_slope(pre).astype(bf16)
        return 0

    lax.fori_loop(0, first.shape[1] // tile, step, 0)


def two_forward(act_one, near, far, near_too, far_too, act, act_t, pre_two):
    n_rows = act_one.shape[1]
    cut = min(256, n_rows)
    first, cols = near.shape
    for side, (left, right) in enumerate(((near, far), (near_too, far_too))):
        to = slice(side * cols, (side + 1) * cols)
        left, right = left[...].T, right[...].T
        for c in range(0, n_rows, cut):
            at = slice(c, c + cut)
            pre = dot(left, act_one[:first, at], 1, 0) + dot(right, act_one[first:, at], 1, 0)
            value = gelu_act(pre)
            act_t[to, at] = value.astype(bf16)
            act[at, to] = value.T.astype(bf16)
            pre_two[to, at] = pre


def two_slope(pre, out):
    cut = min(128, pre.shape[0])
    for c in range(0, pre.shape[0], cut):
        out[c : c + cut] = gelu_slope(pre[c : c + cut])


def divided(kept, bit):
    return [k for k in kept if not k & bit]


def three_home(act, *refs, n_third, orders, kept):
    thirds, own, outs = refs[:n_third], refs[n_third], refs[n_third + 1 :]
    rows = own.shape[0]
    mid, span = thirds[0].shape
    blocks = {k: slice(i * rows, (i + 1) * rows) for i, k in enumerate(kept)}
    half = own.shape[1] // 2
    step = math.gcd(span, half)
    for at in range(0, own.shape[1], step):
        left, right = thirds[at // span], thirds[n_third // 2 + at // span]
        cut = slice(at % span, at % span + step)
        total = dot(act[:, :mid], left[:, cut], 1, 0) + dot(act[:, mid:], right[:, cut], 1, 0)
        own[:, at : at + step] = total[blocks[0]]
        part = at // half
        keep, send = outs[2 * part], outs[2 * part + 1]
        put = slice(at - part * half, at - part * half + step)
        bit = orders[part][0]
        for i, k in enumerate(divided(kept, bit)):
            if k:
                keep[(i - 1) * rows : i * rows, put] = total[blocks[k]]
            send[i * rows : (i + 1) * rows, put] = total[blocks[k | bit]].astype(bf16)


def three_pass(own, *refs, stage, orders, kept):
    ins, new_own, outs = refs[:4], refs[4], refs[5:]
    rows = own.shape[0]
    half = own.shape[1] // 2
    for part, order in enumerate(orders):
        here = list(kept)
        for bit in order[:stage]:
            here = divided(here, bit)
        keep, got = ins[2 * part], ins[2 * part + 1]
        at = slice(part * half, (part + 1) * half)
        total = {}
        for i, k in enumerate(here):
            value = own[:, at] if k == 0 else keep[(i - 1) * rows : i * rows]
            total[k] = value + got[i * rows : (i + 1) * rows].astype(f32)
        new_own[:, at] = total[0]
        bit = order[stage]
        send = outs[2 * part + 1] if len(outs) == 4 else outs[part]
        for i, k in enumerate(divided(here, bit)):
            if k:
                outs[2 * part][(i - 1) * rows : i * rows] = total[k]
            send[i * rows : (i + 1) * rows] = total[k | bit].astype(bf16)


def error_step(number, wanted, wanted_too, fourth, *refs, widths, half, block, n_out):
    groups = len(widths)
    terms = refs[: 3 * groups]
    act, pre = refs[-2:]
    deltas, grad_four = refs[3 * groups : 5 * groups], refs[-3]
    start = 0
    spots = []
    for g, width in enumerate(widths):
        for part in range(2):
            at = slice(start, start + width)
            start += width
            spots.append(at)
            total = terms[3 * g][:, part * width : (part + 1) * width]
            total = total + terms[3 * g + 1 + part][...].astype(f32)
            pre[:, at] = total
            act[:, at] = gelu_act(total).astype(bf16)
    predicted = dot(fourth[...], act[...], 1, 1)
    mine = jnp.where(lax.axis_index("dp") >= half, 1, 0)
    wanted = wanted[mine] + wanted_too[mine]
    live = wanted[n_out : n_out + 1, :].astype(f32)
    error = (2.0 / (number[:, :1] * block) * (predicted - wanted.astype(f32)) * live).astype(bf16)
    row = lax.broadcasted_iota(jnp.int32, error.shape, 0)
    error = jnp.where(row < n_out, error, jnp.zeros_like(error))
    grad_four[...] = dot(error, act[...], 1, 0)
    turned = error.astype(f32).T.astype(bf16)
    for at, delta in zip(spots, deltas):
        value = dot(turned, fourth[:, at], 1, 0) * gelu_slope(pre[:, at])
        delta[...] = value.astype(bf16)


def join(own, got, out):
    rows = own.shape[0]
    out[:rows] = own[...]
    filled = rows + got.shape[0]
    out[rows:filled] = got[...]
    if filled < out.shape[0]:
        out[filled:] = jnp.zeros((out.shape[0] - filled, out.shape[1]), out.dtype)


def lay(*refs, axis):
    out, at = refs[-1], 0
    for value in refs[:-1]:
        to = at + value.shape[axis]
        if axis:
            out[:, at:to] = value[...]
        else:
            out[at:to] = value[...]
        at = to


def join_all(*refs, held, evens, rows):
    out = refs[-1]
    half = out.shape[1] // 2
    for i, blocks in enumerate(held):
        for j, k in enumerate(blocks):
            to = evens.index(k) * rows
            at = slice(i // 2 * half, (i // 2 + 1) * half)
            out[to : to + rows, at] = refs[i][j * rows : (j + 1) * rows]


def three_away(act_t, whole, away):
    mid = act_t.shape[0] // 2
    away[...] = dot(act_t[mid:], whole[...], 1, 0).astype(bf16)


def three_own(act_t, whole, got, *grads):
    mid = act_t.shape[0] // 2
    span = grads[0].shape[1]
    for i, grad in enumerate(grads):
        at = slice(i * span, (i + 1) * span)
        value = dot(act_t[:mid], whole[:, at], 1, 0) + got[:, at].astype(f32)
        grad[...] = value.astype(grad.dtype)


def three_back(whole, *refs, n_third):
    thirds, before, sum_two = refs[:n_third], refs[n_third:-1], refs[-1]
    mid, span = thirds[0].shape
    for side in range(2):
        to = slice(side * mid, (side + 1) * mid)
        total = before[0][to] if before else None
        for i, third in enumerate(thirds[side * n_third // 2 : (side + 1) * n_third // 2]):
            term = dot(third[...], whole[:, i * span : (i + 1) * span], 1, 1)
            total = term if total is None else total + term
        sum_two[to] = total


def two_first(sum_two, slope, act_one, delta, away_far, away):
    value = (sum_two[...] * slope[...]).astype(bf16)
    delta[...] = value
    mid, near = delta.shape[0] // 2, away.shape[0]
    away_far[...] = dot(act_one[near:], value[mid:], 1, 1).astype(bf16)
    away[...] = dot(act_one[:near], value[mid:], 1, 1).astype(bf16)


def two_own(delta, act_one, got, *grads, start):
    mid, span = delta.shape[0] // 2, grads[0].shape[0]
    for i, grad in enumerate(grads):
        at = slice(i * span, (i + 1) * span)
        rows = slice(start + i * span, start + (i + 1) * span)
        value = dot(act_one[rows], delta[:mid], 1, 1) + got[at].astype(f32)
        grad[...] = value.astype(grad.dtype)


def split_dp(parts, step, keep, send):
    bit = (lax.axis_index("dp") & step) != 0
    for i in range(len(parts) // 2):
        even, odd = parts[2 * i], parts[2 * i + 1]
        keep[i] = jnp.where(bit, odd, even)
        send[i] = jnp.where(bit, even, odd).astype(bf16)


def one_back(
    inputs, delta, slope, grad_four, near, far, near_too, far_too, keep, send, *, n_dp, places, n_in, n_out
):
    span = far.shape[0]
    n_mp = near.shape[0] // span + 1
    wide = span // n_dp
    mid = delta.shape[0] // 2
    whole = []
    for k in range(n_mp):
        at = slice(k * span, (k + 1) * span)
        left, right = (near[at], near_too[at]) if k + 1 < n_mp else (far[...], far_too[...])
        value = dot(left, delta[:mid], 1, 0) + dot(right, delta[mid:], 1, 0)
        value = (value * slope[k * span : (k + 1) * span].astype(f32)).astype(bf16)
        grad_one = dot(inputs[...], value, 1, 1)
        at = places.index(k) * span
        pieces = [grad_one[:n_in], grad_four[:n_out, at : at + span]]
        spare = keep.shape[1] - n_in - n_out
        if spare:
            pieces.append(jnp.zeros((spare, span), f32))
        whole.append(jnp.concatenate(pieces, 0))
    parts = [
        jnp.concatenate([value[:, d * wide : (d + 1) * wide] for value in whole], 1)
        for d in range(n_dp)
    ]
    split_dp(parts, 1, keep, send)


def halve(own, got, keep, send, *, step):
    split_dp([own[i] + got[i].astype(f32) for i in range(own.shape[0])], step, keep, send)


def last_half(own, got, keep, send):
    total = own[0] + got[0].astype(f32)
    wide = keep.shape[1]
    keep[...] = total[:, :wide]
    send[...] = total[:, wide:].astype(bf16)


def last_half_mp(own, got, keep, send):
    total = own[...] + got[...].astype(f32)
    wide = keep.shape[1]
    keep[...] = total[:, :wide]
    send[...] = total[:, wide:].astype(bf16)


def add_up(own, got, out):
    out[...] = (own[...].astype(f32) + got[...].astype(f32)).astype(out.dtype)


def update_small(own, *refs):
    gots, (w_in, w_out, m_in, m_out), outs = refs[:-8], refs[-8:-4], refs[-4:]
    nw_in, nw_out, nm_in, nm_out = outs
    total = own[...]
    for got in gots:
        total = total + got[...].astype(f32)
    n_in, n_out = w_in.shape[0], w_out.shape[0]
    mom = momentum_decay * m_in[...] + total[:n_in]
    nm_in[...] = mom
    nw_in[...] = w_in[...] - learn_rate * mom
    mom = momentum_decay * m_out[...] + total[n_in : n_in + n_out]
    nm_out[...] = mom
    nw_out[...] = w_out[...] - learn_rate * mom


def update_big(weight, moment, own, *refs):
    gots, (new_weight, new_moment) = refs[:-2], refs[-2:]
    total = own[...]
    for got in gots:
        total = total + got[...].astype(f32)
    mom = momentum_decay * moment[...] + total
    new_moment[...] = mom
    new_weight[...] = weight[...] - learn_rate * mom


def after(first, *values):
    return lax.optimization_barrier((first, *values))[1:]


def laid(values, axis):
    shape = list(values[0].shape)
    shape[axis] *= len(values)
    return on_core(functools.partial(lay, axis=axis), shaped(tuple(shape), bf16), values, "lay")


def gathered(own, n_mp):
    held = {0: own}
    for k in [k for k in range(1, n_mp) if parent(k) == 0][::-1]:
        held[k] = swap(own, "mp", k)
    return held


def passed_on(held, n_mp, ready):
    for k in sorted((k for k in range(1, n_mp) if parent(k) and k not in held), key=lambda k: -low_bit(k)):
        held[k] = swap(after(ready, held[parent(k)])[0], "mp", low_bit(k))


def summed(held, ks):
    gots = []
    for k in sorted((k for k in ks if k), key=lambda k: (low_bit(k), -k)):
        got = swap(held[k], "mp", low_bit(k))
        to = parent(k)
        if to:
            held[to] = on_core(add_up, shaped(got.shape, bf16), [held[to], got], "add_up")
        else:
            gots.append(got)
    return gots


def on_device(
    samples,
    targets,
    counts,
    weight_in,
    weight_mid,
    weight_top,
    weight_out,
    moment_in,
    moment_mid,
    moment_top,
    moment_out,
):
    slots, n_in, block = samples.shape
    n_out = targets.shape[1]
    n_dp, n_mp = lax.axis_size("dp"), lax.axis_size("mp")
    half = n_dp // 2
    per = slots // n_mp
    rows = per * block // 2
    n_rows = half * rows
    wide = weight_in.shape[1]
    lanes = max(rows, 2 * wide)
    tall = up_to(max(n_in, n_out) + 1, 16)
    hidden = wide * n_dp
    width = hidden * n_mp
    n_mid, n_top = weight_mid.shape[1], weight_top.shape[1]
    planes = range(n_mp)
    groups = [list(planes[:-1]), [n_mp - 1]]
    places = [k for ks in groups for k in ks]
    part = functools.partial

    piece = on_core(
        part(pack_small, tall=tall), shaped((tall, lanes), bf16), [weight_in, weight_out.T], "pack_small"
    )
    second = gathered(weight_mid.astype(bf16), n_mp)
    picked, wanted = on_core(
        part(pick_rows, tall=tall, rows=rows, per=per),
        [shaped((2 * tall, lanes), bf16), shaped((2, tall, rows), bf16)],
        [samples, targets],
        "pick_rows",
        scalars=[counts],
    )
    pieces = [piece] + [swap(piece, "mp", k) for k in planes[1:]]
    top = after((picked, pieces), weight_top.astype(bf16))[0]
    third = gathered(top, n_mp)
    early = [second[k] for k in planes if k and not parent(k)]
    passed_on(second, n_mp, (picked, pieces))

    packed = on_core(
        pack_all,
        shaped(((2 + n_mp) * tall, lanes), bf16),
        [picked, *after(early, *pieces)],
        "pack_all",
    )
    wanted = [wanted, swap(wanted, "dp", half)]
    held = lax.all_gather(packed, "dp")
    inputs, first, fourth, number = on_core(
        part(place_small, n_in=n_in, tall=tall, rows=rows, wide=wide, places=places),
        [
            shaped((tall, n_rows), bf16),
            shaped((tall, width), bf16),
            shaped((tall, width), bf16),
            shaped((1, lanes), f32),
        ],
        [held],
        "place_small",
    )

    act_one = on_core(
        part(one_forward, tile=256), shaped((width, n_rows), bf16), [inputs, first], "one_forward"
    )
    wide_mid = 2 * n_mid
    near = laid(after((picked, pieces), *[second[k] for k in planes[:-1]]), 0)
    third_early = [third[k] for k in planes if k and not parent(k)]
    far = after((act_one, third_early, wanted[1]), second[n_mp - 1])[0]
    second_all = [near, far, swap(near, "dp", 1), swap(far, "dp", 1)]
    act_two, act_two_t, pre_two = on_core(
        two_forward,
        [shaped((n_rows, wide_mid), bf16), shaped((wide_mid, n_rows), bf16), shaped((wide_mid, n_rows), f32)],
        [act_one, *second_all],
        "two_forward",
    )
    passed_on(third, n_mp - 1, act_two)
    third_all = []
    evens = list(range(0, n_dp, 2))
    bits = [1 << i for i in range(1, n_dp.bit_length() - 1)]
    orders = [bits, bits[::-1]]
    slope_one = on_core(
        part(one_slope, tile=256), shaped((width, n_rows), bf16), [inputs, first], "one_slope",
        flops=12_000_000_000,
    )
    slope_two = on_core(two_slope, shaped((wide_mid, n_rows), f32), [pre_two], "two_slope")
    terms = []
    ahead = [third[k] for k in planes if k and not parent(k)]
    for ks in groups:
        cols = len(ks) * n_top
        third_too = [swap(after(act_one, third[k])[0] if k else top, "dp", 1) for k in ks]
        third_all.append([third[k] for k in ks] + third_too)
        weights = after(ahead, *third_all[-1])
        left = half // 2
        kinds = [shaped(((left - 1) * rows, cols // 2), f32), shaped((left * rows, cols // 2), bf16)]
        own, *halves = on_core(
            part(three_home, n_third=len(weights), orders=orders, kept=evens),
            [shaped((rows, cols), f32)] + kinds * 2,
            [act_two, *weights],
            "three_home",
        )
        passed_on(third, n_mp, halves)
        ahead = []
        for stage in range(len(bits)):
            sends = halves[1::2] if len(halves) == 4 else halves
            gots = [swap(send, "dp", order[stage]) for send, order in zip(sends, orders)]
            ahead = ahead or [slope_one, slope_two, *gots]
            if stage + 1 == len(bits):
                break
            keeps, left = halves[::2], left // 2
            kinds = [shaped((left * rows, cols // 2), bf16)]
            if left > 1:
                kinds = [shaped(((left - 1) * rows, cols // 2), f32)] + kinds
            own, *halves = on_core(
                part(three_pass, stage=stage + 1, orders=orders, kept=evens),
                [shaped((rows, cols), f32)] + kinds * 2,
                [own, keeps[0], gots[0], keeps[1], gots[1]],
                "three_pass",
            )
        terms += [own, *gots]
    *deltas, grad_four = on_core(
        part(error_step, widths=[len(ks) * n_top // 2 for ks in groups], half=half, block=block, n_out=n_out),
        [shaped((rows, len(ks) * n_top // 2), bf16) for ks in groups for _ in range(2)]
        + [shaped((tall, width), f32)],
        [number, *wanted, fourth, *terms],
        "error_step",
        scratch=[pltpu.VMEM((rows, width), bf16), pltpu.VMEM((rows, width), f32)],
    )

    sum_two, grad_three = None, {}
    gathers = {}
    for g in reversed(range(len(groups))):
        held, kinds = [[0], [0]], []
        arrays = list(deltas[2 * g : 2 * g + 2])
        cols = arrays[0].shape[1]
        for stage in range(len(bits)):
            last = stage + 1 == len(bits)
            gots = [swap(value, "dp", order[stage]) for value, order in zip(arrays, orders)]
            more = [[k | order[stage] for k in blocks] for blocks, order in zip(held, orders)]
            if last:
                break
            held = [a + b for a, b in zip(held, more)]
            spare = 16 * (g == 0 and stage + 2 == len(bits))
            arrays = [
                on_core(join, shaped((len(blocks) * rows + spare, cols), bf16), [own, got], "join")
                for blocks, own, got in zip(held, arrays, gots)
            ]
            gathers[g, stage] = gots
        gathers[g] = (arrays, gots, [held[0], more[0], held[1], more[1]])
    for g in reversed(range(len(groups))):
        ks, carried = groups[g], sum_two is not None
        arrays, gots, blocks = gathers[g]
        if carried:
            gots = after((sum_two, got_far), *gots)
        elif (0, 0) in gathers:
            gots = after(gathers[0, 0], *gots)
        whole = on_core(
            part(join_all, held=blocks, evens=evens, rows=rows),
            shaped((n_rows, len(ks) * n_top), bf16),
            [arrays[0], gots[0], arrays[1], gots[1]],
            "join_all",
        )
        away = on_core(
            three_away, shaped((n_mid, len(ks) * n_top), bf16), [act_two_t, whole], "three_away"
        )
        away = swap(away, "dp", 1)
        sum_two = on_core(
            part(three_back, n_third=2 * len(ks)),
            shaped((wide_mid, n_rows), f32),
            [whole, *third_all[g]] + ([sum_two] if carried else []),
            "three_back",
        )
        grads = on_core(
            three_own,
            [shaped((n_mid, n_top), bf16 if k else f32) for k in ks],
            [act_two_t, whole, away],
            "three_own",
        )
        grad_three.update(zip(ks, grads))
        if not carried:
            got_far = swap(grads[0], "mp", 1)
    far = n_mp - 1
    grad_three[far - 1] = on_core(
        add_up, shaped(got_far.shape, bf16), [grad_three[far - 1], got_far], "add_up"
    )
    delta_two, away_far, away = on_core(
        two_first,
        [
            shaped((wide_mid, n_rows), bf16),
            shaped((hidden, n_mid), bf16),
            shaped((far * hidden, n_mid), bf16),
        ],
        [sum_two, slope_two, act_one],
        "two_first",
        flops=LONG,
    )
    (farthest,) = on_core(
        part(two_own, start=far * hidden),
        [shaped((hidden, n_mid), bf16)],
        [delta_two, act_one, swap(away_far, "dp", 1)],
        "two_own",
    )
    grads = on_core(
        part(two_own, start=0),
        [shaped((hidden, n_mid), bf16 if k else f32) for k in planes[:-1]],
        [delta_two, act_one, swap(away, "dp", 1)],
        "two_own",
    )
    grad_two = dict(zip(planes, [*grads, farthest]))
    got = swap(grad_two[far], "mp", 1)
    grad_two[far - 1] = on_core(add_up, shaped(got.shape, bf16), [grad_two[far - 1], got], "add_up")
    grad_two[1], grad_three[1] = after(grad_two[far - 1], grad_two[1], grad_three[1])
    gots_two = summed(grad_two, planes[:far])
    gots_three = summed(grad_three, planes[:far])[::-1]
    like = lambda value: shaped(value.shape, f32)
    new_top, mom_top = on_core(
        update_big, [like(weight_top)] * 2, [weight_top, moment_top, grad_three[0], *gots_three], "update_top",
        flops=2_000_000_000,
    )
    n_small = up_to(n_in + n_out, 16)
    shape = (half, n_small, n_mp * wide)
    keep, send = on_core(
        part(one_back, n_dp=n_dp, places=places, n_in=n_in, n_out=n_out),
        [shaped(shape, f32), shaped(shape, bf16)],
        [inputs, delta_two, slope_one, grad_four, *second_all],
        "one_back",
        flops=LONG,
    )
    step = 1
    while step < half:
        got = swap(send, "dp", step)
        if step == 2:
            got = after(gots_three[0], got)[0]
        step *= 2
        shape = (shape[0] // 2, *shape[1:])
        keep, send = on_core(
            part(halve, step=step), [shaped(shape, f32), shaped(shape, bf16)], [keep, got], "halve"
        )
    got = swap(send, "dp", step)
    half_mp = n_mp // 2 * wide
    keep, send = on_core(
        last_half,
        [shaped((n_small, half_mp), f32), shaped((n_small, half_mp), bf16)],
        [keep, got],
        "last_half",
    )
    step = n_mp // 2
    while step:
        got = swap(send, "mp", step)
        step //= 2
        if step:
            got = after((gots_two, mom_top), got)[0]
        if step:
            half_mp = step * wide
            keep, send = on_core(
                last_half_mp,
                [shaped((n_small, half_mp), f32), shaped((n_small, half_mp), bf16)],
                [keep, got],
                "last_half_mp",
            )
    gots_small = [got]

    flat = (weight_in, weight_out.T, moment_in, moment_out.T)
    new_in, new_out, mom_in, mom_out = on_core(
        update_small, [like(value) for value in flat], [keep, *gots_small, *flat], "update_small"
    )
    new_mid, mom_mid = on_core(
        update_big, [like(weight_mid)] * 2, [weight_mid, moment_mid, grad_two[0], *gots_two], "update_mid"
    )
    return (new_in, new_mid, new_top, new_out.T, mom_in, mom_mid, mom_top, mom_out.T)


def solution(mesh):
    in_specs = (
        P("dp", None, None),
        P("dp", None, None),
        P("dp"),
        P(None, ("mp", "dp")),
        P("mp", "dp"),
        P("dp", "mp"),
        P(("mp", "dp"), None),
        P(None, ("mp", "dp")),
        P("mp", "dp"),
        P("dp", "mp"),
        P(("mp", "dp"), None),
    )
    out_specs = (
        P(None, ("mp", "dp")),
        P("mp", "dp"),
        P("dp", "mp"),
        P(("mp", "dp"), None),
        P(None, ("mp", "dp")),
        P("mp", "dp"),
        P("dp", "mp"),
        P(("mp", "dp"), None),
    )
    return jax.shard_map(
        on_device, mesh=mesh, in_specs=in_specs, out_specs=out_specs, check_vma=False
    )
```

```python
import functools
import math

import jax
import jax.numpy as jnp
from jax import lax
from jax.experimental import pallas as pl
from jax.experimental.pallas import tpu as pltpu
from jax.sharding import PartitionSpec as P

momentum_decay = 0.9
learn_rate = 0.05
bf16 = jnp.bfloat16
f32 = jnp.float32
VMEM_BYTES = 24 << 20
LONG = 100_000_000_000


def swap(value, axis, step):
    count = lax.axis_size(axis)
    return lax.ppermute(value, axis, [(at, at ^ step) for at in range(count)])


def parent(k):
    return k & (k - 1)


def low_bit(k):
    return k & -k


def up_to(value, unit):
    return -(-value // unit) * unit


def gelu_act(value):
    return 0.5 * value * (1.0 + lax.erf(value * math.sqrt(0.5)))


def gelu_slope(value):
    return 0.5 * (1.0 + lax.erf(value * math.sqrt(0.5))) + value * jnp.exp(
        -0.5 * value * value
    ) * (1.0 / math.sqrt(2.0 * math.pi))


def dot(left, right, at_left, at_right):
    dims = (((at_left,), (at_right,)), ((), ()))
    return lax.dot_general(left, right, dims, preferred_element_type=f32)


def shaped(dims, kind):
    return jax.ShapeDtypeStruct(dims, kind)


def on_core(body, outs, args, name, flops=0, scratch=(), scalars=()):
    at = pl.BlockSpec(memory_space=pltpu.VMEM)
    return pl.pallas_call(
        body,
        out_shape=outs,
        in_specs=[pl.BlockSpec(memory_space=pltpu.SMEM)] * len(scalars) + [at] * len(args),
        out_specs=jax.tree.map(lambda _: at, outs),
        scratch_shapes=list(scratch),
        compiler_params=pltpu.CompilerParams(vmem_limit_bytes=VMEM_BYTES),
        cost_estimate=pl.CostEstimate(flops=flops, bytes_accessed=0, transcendentals=0),
        name=name,
    )(*scalars, *args)


def pack_small(w_in, w_out, out, *, tall):
    n_in, wide = w_in.shape
    n_out = w_out.shape[0]
    left = jnp.concatenate([w_in[...], jnp.zeros((tall - n_in, wide), f32)], 0)
    right = jnp.concatenate([w_out[...], jnp.zeros((tall - n_out, wide), f32)], 0)
    parts = [left, right]
    spare = out.shape[1] - 2 * wide
    if spare:
        parts.append(jnp.zeros((tall, spare), f32))
    out[...] = jnp.concatenate(parts, 1).astype(bf16)


def pick_rows(count, samples, targets, out, wanted, *, tall, rows, per):
    slots, n_in, block = samples.shape
    n_out = targets.shape[1]
    half = lax.axis_size("dp") // 2
    high = lax.axis_index("dp") >= half
    xs, ys = [], []
    for j in range(per):
        at = per * lax.axis_index("mp") + j
        slot = jnp.where(high, slots - 1 - at, at)
        keep = slot < count[0]
        for source, last, all_of in (
            (samples, jnp.full((1, block), count[0].astype(f32)), xs),
            (targets, jnp.full((1, block), keep.astype(f32)), ys),
        ):
            value = source[slot].astype(f32)
            parts = [jnp.where(keep, value, jnp.zeros_like(value)), last]
            spare = tall - value.shape[0] - 1
            if spare:
                parts.append(jnp.zeros((spare, block), f32))
            all_of.append(jnp.concatenate(parts, 0).astype(bf16))
    x = jnp.concatenate(xs, 1) if per > 1 else xs[0]
    y = jnp.concatenate(ys, 1) if per > 1 else ys[0]
    spare = out.shape[1] - rows
    for t in range(2):
        at = slice(t * rows, (t + 1) * rows)
        half_x = x[:, at]
        if spare:
            half_x = jnp.concatenate([half_x, jnp.zeros((tall, spare), bf16)], 1)
        out[tall * t : tall * (t + 1)] = half_x
        wanted[t] = y[:, at]


def pack_all(*refs):
    out, at = refs[-1], 0
    for part in refs[:-1]:
        out[at : at + part.shape[0]] = part[...]
        at += part.shape[0]


def place_small(held, inputs, first, fourth, number, *, n_in, tall, rows, wide, places):
    n_dp, n_mp = lax.axis_size("dp"), lax.axis_size("mp")
    half = n_dp // 2
    total = held[0, n_in : n_in + 1].astype(f32)
    for d in range(1, n_dp):
        total = total + held[d, n_in : n_in + 1].astype(f32)
    number[...] = total
    for place, k in enumerate(range(0, n_dp, 2)):
        at = lax.axis_index("dp") ^ k
        high = at >= half
        pair = jnp.where(high, at - half, at)
        both = held[pair, : 2 * tall] + held[pair + half, : 2 * tall]
        value = jnp.where(high, both[tall:], both[:tall])
        inputs[:, place * rows : (place + 1) * rows] = value[:, :rows]
    hidden = n_dp * wide
    for k in range(n_mp):
        row = slice((2 + k) * tall, (3 + k) * tall)
        pieces = [held[d, row] for d in range(n_dp)]
        at = slice(k * hidden, (k + 1) * hidden)
        first[:, at] = jnp.concatenate([piece[:, :wide] for piece in pieces], 1)
        at = slice(places.index(k) * hidden, (places.index(k) + 1) * hidden)
        fourth[:, at] = jnp.concatenate([piece[:, wide : 2 * wide] for piece in pieces], 1)


def one_forward(inputs, first, out, *, tile):
    n_rows = inputs.shape[1]
    cut = min(256, n_rows)

    def step(i, _):
        at = pl.ds(pl.multiple_of(i * tile, tile), tile)
        weights = first[:, at].T
        for c in range(0, n_rows, cut):
            pre = dot(weights, inputs[:, c : c + cut], 1, 0)
            out[at, c : c + cut] = gelu_act(pre).astype(bf16)
        return 0

    lax.fori_loop(0, first.shape[1] // tile, step, 0)


def one_slope(inputs, first, out, *, tile, start):
    n_rows = inputs.shape[1]
    cut = min(256, n_rows)

    def step(i, _):
        at = pl.ds(pl.multiple_of(i * tile, tile), tile)
        weights = first[:, pl.ds(pl.multiple_of(start + i * tile, tile), tile)].T
        for c in range(0, n_rows, cut):
            pre = dot(weights, inputs[:, c : c + cut], 1, 0)
            out[at, c : c + cut] = gelu_slope(pre).astype(bf16)
        return 0

    lax.fori_loop(0, out.shape[0] // tile, step, 0)


def two_forward(act_one, near, far, near_too, far_too, act, act_t, pre_two):
    n_rows = act_one.shape[1]
    cut = min(256, n_rows)
    first, cols = near.shape
    for side, (left, right) in enumerate(((near, far), (near_too, far_too))):
        to = slice(side * cols, (side + 1) * cols)
        left, right = left[...].T, right[...].T
        for c in range(0, n_rows, cut):
            at = slice(c, c + cut)
            pre = dot(left, act_one[:first, at], 1, 0) + dot(right, act_one[first:, at], 1, 0)
            value = gelu_act(pre)
            act_t[to, at] = value.astype(bf16)
            act[at, to] = value.T.astype(bf16)
            pre_two[to, at] = pre


def two_slope(pre, out):
    cut = min(128, pre.shape[0])
    for c in range(0, pre.shape[0], cut):
        out[c : c + cut] = gelu_slope(pre[c : c + cut])


def divided(kept, bit):
    return [k for k in kept if not k & bit]


def three_home(act, *refs, n_third, orders, kept):
    thirds, own, outs = refs[:n_third], refs[n_third], refs[n_third + 1 :]
    rows = own.shape[0]
    mid, span = thirds[0].shape
    blocks = {k: slice(i * rows, (i + 1) * rows) for i, k in enumerate(kept)}
    half = own.shape[1] // 2
    step = math.gcd(span, half)
    for at in range(0, own.shape[1], step):
        left, right = thirds[at // span], thirds[n_third // 2 + at // span]
        cut = slice(at % span, at % span + step)
        total = dot(act[:, :mid], left[:, cut], 1, 0) + dot(act[:, mid:], right[:, cut], 1, 0)
        own[:, at : at + step] = total[blocks[0]]
        part = at // half
        keep, send = outs[2 * part], outs[2 * part + 1]
        put = slice(at - part * half, at - part * half + step)
        bit = orders[part][0]
        for i, k in enumerate(divided(kept, bit)):
            if k:
                keep[(i - 1) * rows : i * rows, put] = total[blocks[k]]
            send[i * rows : (i + 1) * rows, put] = total[blocks[k | bit]].astype(bf16)


def three_pass(own, *refs, stage, orders, kept):
    ins, new_own, outs = refs[:4], refs[4], refs[5:]
    rows = own.shape[0]
    half = own.shape[1] // 2
    for part, order in enumerate(orders):
        here = list(kept)
        for bit in order[:stage]:
            here = divided(here, bit)
        keep, got = ins[2 * part], ins[2 * part + 1]
        at = slice(part * half, (part + 1) * half)
        total = {}
        for i, k in enumerate(here):
            value = own[:, at] if k == 0 else keep[(i - 1) * rows : i * rows]
            total[k] = value + got[i * rows : (i + 1) * rows].astype(f32)
        new_own[:, at] = total[0]
        bit = order[stage]
        send = outs[2 * part + 1] if len(outs) == 4 else outs[part]
        for i, k in enumerate(divided(here, bit)):
            if k:
                outs[2 * part][(i - 1) * rows : i * rows] = total[k]
            send[i * rows : (i + 1) * rows] = total[k | bit].astype(bf16)


def error_step(number, wanted, wanted_too, fourth, *refs, widths, half, block, n_out):
    groups = len(widths)
    terms = refs[: 3 * groups]
    act, pre = refs[-2:]
    deltas, grad_four = refs[3 * groups : 5 * groups], refs[-3]
    start = 0
    spots = []
    for g, width in enumerate(widths):
        for part in range(2):
            at = slice(start, start + width)
            start += width
            spots.append(at)
            total = terms[3 * g][:, part * width : (part + 1) * width]
            total = total + terms[3 * g + 1 + part][...].astype(f32)
            pre[:, at] = total
            act[:, at] = gelu_act(total).astype(bf16)
    predicted = dot(fourth[...], act[...], 1, 1)
    mine = jnp.where(lax.axis_index("dp") >= half, 1, 0)
    wanted = wanted[mine] + wanted_too[mine]
    live = wanted[n_out : n_out + 1, :].astype(f32)
    error = (2.0 / (number[:, :1] * block) * (predicted - wanted.astype(f32)) * live).astype(bf16)
    row = lax.broadcasted_iota(jnp.int32, error.shape, 0)
    error = jnp.where(row < n_out, error, jnp.zeros_like(error))
    grad_four[...] = dot(error, act[...], 1, 0)
    turned = error.astype(f32).T.astype(bf16)
    for at, delta in zip(spots, deltas):
        value = dot(turned, fourth[:, at], 1, 0) * gelu_slope(pre[:, at])
        delta[...] = value.astype(bf16)


def join(own, got, out):
    rows = own.shape[0]
    out[:rows] = own[...]
    filled = rows + got.shape[0]
    out[rows:filled] = got[...]
    if filled < out.shape[0]:
        out[filled:] = jnp.zeros((out.shape[0] - filled, out.shape[1]), out.dtype)


def lay(*refs, axis):
    out, at = refs[-1], 0
    for value in refs[:-1]:
        to = at + value.shape[axis]
        if axis:
            out[:, at:to] = value[...]
        else:
            out[at:to] = value[...]
        at = to


def join_all(*refs, held, evens, rows):
    out = refs[-1]
    half = out.shape[1] // 2
    for i, blocks in enumerate(held):
        for j, k in enumerate(blocks):
            to = evens.index(k) * rows
            at = slice(i // 2 * half, (i // 2 + 1) * half)
            out[to : to + rows, at] = refs[i][j * rows : (j + 1) * rows]


def three_away(act_t, whole, away):
    mid = act_t.shape[0] // 2
    away[...] = dot(act_t[mid:], whole[...], 1, 0).astype(bf16)


def three_own(act_t, whole, got, *grads):
    mid = act_t.shape[0] // 2
    span = grads[0].shape[1]
    for i, grad in enumerate(grads):
        at = slice(i * span, (i + 1) * span)
        value = dot(act_t[:mid], whole[:, at], 1, 0) + got[:, at].astype(f32)
        grad[...] = value.astype(grad.dtype)


def three_back(whole, *refs, n_third):
    thirds, before, sum_two = refs[:n_third], refs[n_third:-1], refs[-1]
    mid, span = thirds[0].shape
    for side in range(2):
        to = slice(side * mid, (side + 1) * mid)
        total = before[0][to] if before else None
        for i, third in enumerate(thirds[side * n_third // 2 : (side + 1) * n_third // 2]):
            term = dot(third[...], whole[:, i * span : (i + 1) * span], 1, 1)
            total = term if total is None else total + term
        sum_two[to] = total


def two_first(sum_two, slope, act_one, delta, away_far, away):
    value = (sum_two[...] * slope[...]).astype(bf16)
    delta[...] = value
    mid, near = delta.shape[0] // 2, away.shape[0]
    away_far[...] = dot(act_one[near:], value[mid:], 1, 1).astype(bf16)
    away[...] = dot(act_one[:near], value[mid:], 1, 1).astype(bf16)


def two_own(delta, act_one, got, *grads, start):
    mid, span = delta.shape[0] // 2, grads[0].shape[0]
    for i, grad in enumerate(grads):
        at = slice(i * span, (i + 1) * span)
        rows = slice(start + i * span, start + (i + 1) * span)
        value = dot(act_one[rows], delta[:mid], 1, 1) + got[at].astype(f32)
        grad[...] = value.astype(grad.dtype)


def split_dp(parts, step, keep, send):
    bit = (lax.axis_index("dp") & step) != 0
    for i in range(len(parts) // 2):
        even, odd = parts[2 * i], parts[2 * i + 1]
        keep[i] = jnp.where(bit, odd, even)
        send[i] = jnp.where(bit, even, odd).astype(bf16)


def one_back(
    inputs, delta, slope, slope_more, grad_four, near, far, near_too, far_too, keep, send, *, n_dp, places, n_in, n_out
):
    span = far.shape[0]
    n_mp = near.shape[0] // span + 1
    wide = span // n_dp
    mid = delta.shape[0] // 2
    whole = []
    for k in range(n_mp):
        at = slice(k * span, (k + 1) * span)
        left, right = (near[at], near_too[at]) if k + 1 < n_mp else (far[...], far_too[...])
        value = dot(left, delta[:mid], 1, 0) + dot(right, delta[mid:], 1, 0)
        source, row = (slope, k * span) if 2 * k < n_mp else (slope_more, (k - n_mp // 2) * span)
        value = (value * source[row : row + span].astype(f32)).astype(bf16)
        grad_one = dot(inputs[...], value, 1, 1)
        at = places.index(k) * span
        pieces = [grad_one[:n_in], grad_four[:n_out, at : at + span]]
        spare = keep.shape[1] - n_in - n_out
        if spare:
            pieces.append(jnp.zeros((spare, span), f32))
        whole.append(jnp.concatenate(pieces, 0))
    parts = [
        jnp.concatenate([value[:, d * wide : (d + 1) * wide] for value in whole], 1)
        for d in range(n_dp)
    ]
    split_dp(parts, 1, keep, send)


def halve(own, got, keep, send, *, step):
    split_dp([own[i] + got[i].astype(f32) for i in range(own.shape[0])], step, keep, send)


def last_half(own, got, keep, send):
    total = own[0] + got[0].astype(f32)
    wide = keep.shape[1]
    keep[...] = total[:, :wide]
    send[...] = total[:, wide:].astype(bf16)


def last_half_mp(own, got, keep, send):
    total = own[...] + got[...].astype(f32)
    wide = keep.shape[1]
    keep[...] = total[:, :wide]
    send[...] = total[:, wide:].astype(bf16)


def add_up(own, got, out):
    out[...] = (own[...].astype(f32) + got[...].astype(f32)).astype(out.dtype)


def update_small(own, *refs):
    gots, (w_in, w_out, m_in, m_out), outs = refs[:-8], refs[-8:-4], refs[-4:]
    nw_in, nw_out, nm_in, nm_out = outs
    total = own[...]
    for got in gots:
        total = total + got[...].astype(f32)
    n_in, n_out = w_in.shape[0], w_out.shape[0]
    mom = momentum_decay * m_in[...] + total[:n_in]
    nm_in[...] = mom
    nw_in[...] = w_in[...] - learn_rate * mom
    mom = momentum_decay * m_out[...] + total[n_in : n_in + n_out]
    nm_out[...] = mom
    nw_out[...] = w_out[...] - learn_rate * mom


def update_big(weight, moment, own, *refs):
    gots, (new_weight, new_moment) = refs[:-2], refs[-2:]
    total = own[...]
    for got in gots:
        total = total + got[...].astype(f32)
    mom = momentum_decay * moment[...] + total
    new_moment[...] = mom
    new_weight[...] = weight[...] - learn_rate * mom


def after(first, *values):
    return lax.optimization_barrier((first, *values))[1:]


def laid(values, axis):
    shape = list(values[0].shape)
    shape[axis] *= len(values)
    return on_core(functools.partial(lay, axis=axis), shaped(tuple(shape), bf16), values, "lay")


def gathered(own, n_mp):
    held = {0: own}
    for k in [k for k in range(1, n_mp) if parent(k) == 0][::-1]:
        held[k] = swap(own, "mp", k)
    return held


def passed_on(held, n_mp, ready):
    for k in sorted((k for k in range(1, n_mp) if parent(k) and k not in held), key=lambda k: -low_bit(k)):
        held[k] = swap(after(ready, held[parent(k)])[0], "mp", low_bit(k))


def summed(held, ks):
    gots = []
    for k in sorted((k for k in ks if k), key=lambda k: (low_bit(k), -k)):
        got = swap(held[k], "mp", low_bit(k))
        to = parent(k)
        if to:
            held[to] = on_core(add_up, shaped(got.shape, bf16), [held[to], got], "add_up")
        else:
            gots.append(got)
    return gots


def on_device(
    samples,
    targets,
    counts,
    weight_in,
    weight_mid,
    weight_top,
    weight_out,
    moment_in,
    moment_mid,
    moment_top,
    moment_out,
):
    slots, n_in, block = samples.shape
    n_out = targets.shape[1]
    n_dp, n_mp = lax.axis_size("dp"), lax.axis_size("mp")
    half = n_dp // 2
    per = slots // n_mp
    rows = per * block // 2
    n_rows = half * rows
    wide = weight_in.shape[1]
    lanes = max(rows, 2 * wide)
    tall = up_to(max(n_in, n_out) + 1, 16)
    hidden = wide * n_dp
    width = hidden * n_mp
    n_mid, n_top = weight_mid.shape[1], weight_top.shape[1]
    planes = range(n_mp)
    groups = [list(planes[:-1]), [n_mp - 1]]
    places = [k for ks in groups for k in ks]
    part = functools.partial

    piece = on_core(
        part(pack_small, tall=tall), shaped((tall, lanes), bf16), [weight_in, weight_out.T], "pack_small"
    )
    second = gathered(weight_mid.astype(bf16), n_mp)
    picked, wanted = on_core(
        part(pick_rows, tall=tall, rows=rows, per=per),
        [shaped((2 * tall, lanes), bf16), shaped((2, tall, rows), bf16)],
        [samples, targets],
        "pick_rows",
        scalars=[counts],
    )
    pieces = [piece] + [swap(piece, "mp", k) for k in planes[1:]]
    top = after((picked, pieces), weight_top.astype(bf16))[0]
    third = gathered(top, n_mp)
    early = [second[k] for k in planes if k and not parent(k)]
    passed_on(second, n_mp, (picked, pieces))

    packed = on_core(
        pack_all,
        shaped(((2 + n_mp) * tall, lanes), bf16),
        [picked, *after(early, *pieces)],
        "pack_all",
    )
    wanted = [wanted, swap(wanted, "dp", half)]
    held = lax.all_gather(packed, "dp")
    inputs, first, fourth, number = on_core(
        part(place_small, n_in=n_in, tall=tall, rows=rows, wide=wide, places=places),
        [
            shaped((tall, n_rows), bf16),
            shaped((tall, width), bf16),
            shaped((tall, width), bf16),
            shaped((1, lanes), f32),
        ],
        [held],
        "place_small",
    )

    act_one = on_core(
        part(one_forward, tile=256), shaped((width, n_rows), bf16), [inputs, first], "one_forward"
    )
    wide_mid = 2 * n_mid
    near = laid(after((picked, pieces), *[second[k] for k in planes[:-1]]), 0)
    third_early = [third[k] for k in planes if k and not parent(k)]
    far = after((act_one, third_early, wanted[1]), second[n_mp - 1])[0]
    second_all = [near, far, swap(near, "dp", 1), swap(far, "dp", 1)]
    act_two, act_two_t, pre_two = on_core(
        two_forward,
        [shaped((n_rows, wide_mid), bf16), shaped((wide_mid, n_rows), bf16), shaped((wide_mid, n_rows), f32)],
        [act_one, *second_all],
        "two_forward",
    )
    passed_on(third, n_mp - 1, act_two)
    third_all = []
    evens = list(range(0, n_dp, 2))
    bits = [1 << i for i in range(1, n_dp.bit_length() - 1)]
    orders = [bits, bits[::-1]]
    slopes = [
        on_core(
            part(one_slope, tile=256, start=start),
            shaped((width // 2, n_rows), bf16),
            [inputs, first],
            "one_slope",
            flops=6_000_000_000,
        )
        for start in (0, width // 2)
    ]
    slope_two = on_core(two_slope, shaped((wide_mid, n_rows), f32), [pre_two], "two_slope")
    terms = []
    ahead = [third[k] for k in planes if k and not parent(k)]
    for ks in groups:
        cols = len(ks) * n_top
        ready = (act_one, slopes[0]) if n_mp - 1 in ks else act_one
        third_too = [swap(after(ready, third[k])[0] if k else top, "dp", 1) for k in ks]
        third_all.append([third[k] for k in ks] + third_too)
        weights = after(ahead, *third_all[-1])
        left = half // 2
        kinds = [shaped(((left - 1) * rows, cols // 2), f32), shaped((left * rows, cols // 2), bf16)]
        own, *halves = on_core(
            part(three_home, n_third=len(weights), orders=orders, kept=evens),
            [shaped((rows, cols), f32)] + kinds * 2,
            [act_two, *weights],
            "three_home",
        )
        passed_on(third, n_mp, halves)
        ahead = []
        for stage in range(len(bits)):
            sends = halves[1::2] if len(halves) == 4 else halves
            gots = [swap(send, "dp", order[stage]) for send, order in zip(sends, orders)]
            ahead = ahead or [slopes[1], slope_two]
            if stage + 1 == len(bits):
                break
            keeps, left = halves[::2], left // 2
            kinds = [shaped((left * rows, cols // 2), bf16)]
            if left > 1:
                kinds = [shaped(((left - 1) * rows, cols // 2), f32)] + kinds
            own, *halves = on_core(
                part(three_pass, stage=stage + 1, orders=orders, kept=evens),
                [shaped((rows, cols), f32)] + kinds * 2,
                [own, keeps[0], gots[0], keeps[1], gots[1]],
                "three_pass",
            )
        terms += [own, *gots]
    *deltas, grad_four = on_core(
        part(error_step, widths=[len(ks) * n_top // 2 for ks in groups], half=half, block=block, n_out=n_out),
        [shaped((rows, len(ks) * n_top // 2), bf16) for ks in groups for _ in range(2)]
        + [shaped((tall, width), f32)],
        [number, *wanted, fourth, *terms],
        "error_step",
        scratch=[pltpu.VMEM((rows, width), bf16), pltpu.VMEM((rows, width), f32)],
    )

    sum_two, grad_three = None, {}
    gathers = {}
    for g in reversed(range(len(groups))):
        held, kinds = [[0], [0]], []
        arrays = list(deltas[2 * g : 2 * g + 2])
        cols = arrays[0].shape[1]
        for stage in range(len(bits)):
            last = stage + 1 == len(bits)
            gots = [swap(value, "dp", order[stage]) for value, order in zip(arrays, orders)]
            more = [[k | order[stage] for k in blocks] for blocks, order in zip(held, orders)]
            if last:
                break
            held = [a + b for a, b in zip(held, more)]
            spare = 16 * (g == 0 and stage + 2 == len(bits))
            arrays = [
                on_core(join, shaped((len(blocks) * rows + spare, cols), bf16), [own, got], "join")
                for blocks, own, got in zip(held, arrays, gots)
            ]
            gathers[g, stage] = gots
        gathers[g] = (arrays, gots, [held[0], more[0], held[1], more[1]])
    for g in reversed(range(len(groups))):
        ks, carried = groups[g], sum_two is not None
        arrays, gots, blocks = gathers[g]
        if carried:
            gots = after((sum_two, got_far), *gots)
        elif (0, 0) in gathers:
            gots = after(gathers[0, 0], *gots)
        whole = on_core(
            part(join_all, held=blocks, evens=evens, rows=rows),
            shaped((n_rows, len(ks) * n_top), bf16),
            [arrays[0], gots[0], arrays[1], gots[1]],
            "join_all",
        )
        away = on_core(
            three_away, shaped((n_mid, len(ks) * n_top), bf16), [act_two_t, whole], "three_away"
        )
        away = swap(away, "dp", 1)
        sum_two = on_core(
            part(three_back, n_third=2 * len(ks)),
            shaped((wide_mid, n_rows), f32),
            [whole, *third_all[g]] + ([sum_two] if carried else []),
            "three_back",
        )
        grads = on_core(
            three_own,
            [shaped((n_mid, n_top), bf16 if k else f32) for k in ks],
            [act_two_t, whole, away],
            "three_own",
        )
        grad_three.update(zip(ks, grads))
        if not carried:
            got_far = swap(grads[0], "mp", 1)
    far = n_mp - 1
    grad_three[far - 1] = on_core(
        add_up, shaped(got_far.shape, bf16), [grad_three[far - 1], got_far], "add_up"
    )
    delta_two, away_far, away = on_core(
        two_first,
        [
            shaped((wide_mid, n_rows), bf16),
            shaped((hidden, n_mid), bf16),
            shaped((far * hidden, n_mid), bf16),
        ],
        [sum_two, slope_two, act_one],
        "two_first",
        flops=LONG,
    )
    (farthest,) = on_core(
        part(two_own, start=far * hidden),
        [shaped((hidden, n_mid), bf16)],
        [delta_two, act_one, swap(away_far, "dp", 1)],
        "two_own",
    )
    grads = on_core(
        part(two_own, start=0),
        [shaped((hidden, n_mid), bf16 if k else f32) for k in planes[:-1]],
        [delta_two, act_one, swap(away, "dp", 1)],
        "two_own",
    )
    grad_two = dict(zip(planes, [*grads, farthest]))
    got = swap(grad_two[far], "mp", 1)
    grad_two[far - 1] = on_core(add_up, shaped(got.shape, bf16), [grad_two[far - 1], got], "add_up")
    grad_two[1], grad_three[1] = after(grad_two[far - 1], grad_two[1], grad_three[1])
    gots_two = summed(grad_two, planes[:far])
    gots_three = summed(grad_three, planes[:far])[::-1]
    like = lambda value: shaped(value.shape, f32)
    new_top, mom_top = on_core(
        update_big, [like(weight_top)] * 2, [weight_top, moment_top, grad_three[0], *gots_three], "update_top",
        flops=2_000_000_000,
    )
    n_small = up_to(n_in + n_out, 16)
    shape = (half, n_small, n_mp * wide)
    keep, send = on_core(
        part(one_back, n_dp=n_dp, places=places, n_in=n_in, n_out=n_out),
        [shaped(shape, f32), shaped(shape, bf16)],
        [inputs, delta_two, *slopes, grad_four, *second_all],
        "one_back",
        flops=LONG,
    )
    step = 1
    while step < half:
        got = swap(send, "dp", step)
        if step == 2:
            got = after(gots_three[0], got)[0]
        step *= 2
        shape = (shape[0] // 2, *shape[1:])
        keep, send = on_core(
            part(halve, step=step), [shaped(shape, f32), shaped(shape, bf16)], [keep, got], "halve"
        )
    got = swap(send, "dp", step)
    half_mp = n_mp // 2 * wide
    keep, send = on_core(
        last_half,
        [shaped((n_small, half_mp), f32), shaped((n_small, half_mp), bf16)],
        [keep, got],
        "last_half",
    )
    step = n_mp // 2
    while step:
        got = swap(send, "mp", step)
        step //= 2
        if step:
            got = after((gots_two, mom_top), got)[0]
        if step:
            half_mp = step * wide
            keep, send = on_core(
                last_half_mp,
                [shaped((n_small, half_mp), f32), shaped((n_small, half_mp), bf16)],
                [keep, got],
                "last_half_mp",
            )
    gots_small = [got]

    flat = (weight_in, weight_out.T, moment_in, moment_out.T)
    new_in, new_out, mom_in, mom_out = on_core(
        update_small, [like(value) for value in flat], [keep, *gots_small, *flat], "update_small"
    )
    new_mid, mom_mid = on_core(
        update_big, [like(weight_mid)] * 2, [weight_mid, moment_mid, grad_two[0], *gots_two], "update_mid"
    )
    return (new_in, new_mid, new_top, new_out.T, mom_in, mom_mid, mom_top, mom_out.T)


def solution(mesh):
    in_specs = (
        P("dp", None, None),
        P("dp", None, None),
        P("dp"),
        P(None, ("mp", "dp")),
        P("mp", "dp"),
        P("dp", "mp"),
        P(("mp", "dp"), None),
        P(None, ("mp", "dp")),
        P("mp", "dp"),
        P("dp", "mp"),
        P(("mp", "dp"), None),
    )
    out_specs = (
        P(None, ("mp", "dp")),
        P("mp", "dp"),
        P("dp", "mp"),
        P(("mp", "dp"), None),
        P(None, ("mp", "dp")),
        P("mp", "dp"),
        P("dp", "mp"),
        P(("mp", "dp"), None),
    )
    return jax.shard_map(
        on_device, mesh=mesh, in_specs=in_specs, out_specs=out_specs, check_vma=False
    )
```

```python
import functools
import math

import jax
import jax.numpy as jnp
from jax import lax
from jax.experimental import pallas as pl
from jax.experimental.pallas import tpu as pltpu
from jax.sharding import PartitionSpec as P

momentum_decay = 0.9
learn_rate = 0.05
bf16 = jnp.bfloat16
f32 = jnp.float32
VMEM_BYTES = 24 << 20
LONG = 100_000_000_000


def swap(value, axis, step):
    count = lax.axis_size(axis)
    return lax.ppermute(value, axis, [(at, at ^ step) for at in range(count)])


def parent(k):
    return k & (k - 1)


def low_bit(k):
    return k & -k


def up_to(value, unit):
    return -(-value // unit) * unit


def gelu_act(value):
    return 0.5 * value * (1.0 + lax.erf(value * math.sqrt(0.5)))


def gelu_slope(value):
    return 0.5 * (1.0 + lax.erf(value * math.sqrt(0.5))) + value * jnp.exp(
        -0.5 * value * value
    ) * (1.0 / math.sqrt(2.0 * math.pi))


def dot(left, right, at_left, at_right):
    dims = (((at_left,), (at_right,)), ((), ()))
    return lax.dot_general(left, right, dims, preferred_element_type=f32)


def shaped(dims, kind):
    return jax.ShapeDtypeStruct(dims, kind)


def on_core(body, outs, args, name, flops=0, scratch=(), scalars=()):
    at = pl.BlockSpec(memory_space=pltpu.VMEM)
    return pl.pallas_call(
        body,
        out_shape=outs,
        in_specs=[pl.BlockSpec(memory_space=pltpu.SMEM)] * len(scalars) + [at] * len(args),
        out_specs=jax.tree.map(lambda _: at, outs),
        scratch_shapes=list(scratch),
        compiler_params=pltpu.CompilerParams(vmem_limit_bytes=VMEM_BYTES),
        cost_estimate=pl.CostEstimate(flops=flops, bytes_accessed=0, transcendentals=0),
        name=name,
    )(*scalars, *args)


def pack_small(w_in, w_out, out, *, tall):
    n_in, wide = w_in.shape
    n_out = w_out.shape[0]
    left = jnp.concatenate([w_in[...], jnp.zeros((tall - n_in, wide), f32)], 0)
    right = jnp.concatenate([w_out[...], jnp.zeros((tall - n_out, wide), f32)], 0)
    parts = [left, right]
    spare = out.shape[1] - 2 * wide
    if spare:
        parts.append(jnp.zeros((tall, spare), f32))
    out[...] = jnp.concatenate(parts, 1).astype(bf16)


def pick_rows(count, samples, targets, out, wanted, *, tall, rows, per):
    slots, n_in, block = samples.shape
    n_out = targets.shape[1]
    half = lax.axis_size("dp") // 2
    high = lax.axis_index("dp") >= half
    xs, ys = [], []
    for j in range(per):
        at = per * lax.axis_index("mp") + j
        slot = jnp.where(high, slots - 1 - at, at)
        keep = slot < count[0]
        for source, last, all_of in (
            (samples, jnp.full((1, block), count[0].astype(f32)), xs),
            (targets, jnp.full((1, block), keep.astype(f32)), ys),
        ):
            value = source[slot].astype(f32)
            parts = [jnp.where(keep, value, jnp.zeros_like(value)), last]
            spare = tall - value.shape[0] - 1
            if spare:
                parts.append(jnp.zeros((spare, block), f32))
            all_of.append(jnp.concatenate(parts, 0).astype(bf16))
    x = jnp.concatenate(xs, 1) if per > 1 else xs[0]
    y = jnp.concatenate(ys, 1) if per > 1 else ys[0]
    spare = out.shape[1] - rows
    for t in range(2):
        at = slice(t * rows, (t + 1) * rows)
        half_x = x[:, at]
        if spare:
            half_x = jnp.concatenate([half_x, jnp.zeros((tall, spare), bf16)], 1)
        out[tall * t : tall * (t + 1)] = half_x
        wanted[t] = y[:, at]


def pack_all(*refs):
    out, at = refs[-1], 0
    for part in refs[:-1]:
        out[at : at + part.shape[0]] = part[...]
        at += part.shape[0]


def place_small(held, inputs, first, fourth, number, *, n_in, tall, rows, wide, places):
    n_dp, n_mp = lax.axis_size("dp"), lax.axis_size("mp")
    half = n_dp // 2
    total = held[0, n_in : n_in + 1].astype(f32)
    for d in range(1, n_dp):
        total = total + held[d, n_in : n_in + 1].astype(f32)
    number[...] = total
    for place, k in enumerate(range(0, n_dp, 2)):
        at = lax.axis_index("dp") ^ k
        high = at >= half
        pair = jnp.where(high, at - half, at)
        both = held[pair, : 2 * tall] + held[pair + half, : 2 * tall]
        value = jnp.where(high, both[tall:], both[:tall])
        inputs[:, place * rows : (place + 1) * rows] = value[:, :rows]
    hidden = n_dp * wide
    for k in range(n_mp):
        row = slice((2 + k) * tall, (3 + k) * tall)
        pieces = [held[d, row] for d in range(n_dp)]
        at = slice(k * hidden, (k + 1) * hidden)
        first[:, at] = jnp.concatenate([piece[:, :wide] for piece in pieces], 1)
        at = slice(places.index(k) * hidden, (places.index(k) + 1) * hidden)
        fourth[:, at] = jnp.concatenate([piece[:, wide : 2 * wide] for piece in pieces], 1)


def one_forward(inputs, first, out, *, tile):
    n_rows = inputs.shape[1]
    cut = min(256, n_rows)

    def step(i, _):
        at = pl.ds(pl.multiple_of(i * tile, tile), tile)
        weights = first[:, at].T
        for c in range(0, n_rows, cut):
            pre = dot(weights, inputs[:, c : c + cut], 1, 0)
            out[at, c : c + cut] = gelu_act(pre).astype(bf16)
        return 0

    lax.fori_loop(0, first.shape[1] // tile, step, 0)


def one_slope(inputs, first, out, *, tile, start):
    n_rows = inputs.shape[1]
    cut = min(256, n_rows)

    def step(i, _):
        at = pl.ds(pl.multiple_of(i * tile, tile), tile)
        weights = first[:, pl.ds(pl.multiple_of(start + i * tile, tile), tile)].T
        for c in range(0, n_rows, cut):
            pre = dot(weights, inputs[:, c : c + cut], 1, 0)
            out[at, c : c + cut] = gelu_slope(pre).astype(bf16)
        return 0

    lax.fori_loop(0, out.shape[0] // tile, step, 0)


def two_forward(act_one, near, far, near_too, far_too, act, act_t, pre_two):
    n_rows = act_one.shape[1]
    cut = min(256, n_rows)
    first, cols = near.shape
    for side, (left, right) in enumerate(((near, far), (near_too, far_too))):
        to = slice(side * cols, (side + 1) * cols)
        left, right = left[...].T, right[...].T
        for c in range(0, n_rows, cut):
            at = slice(c, c + cut)
            pre = dot(left, act_one[:first, at], 1, 0) + dot(right, act_one[first:, at], 1, 0)
            value = gelu_act(pre)
            act_t[to, at] = value.astype(bf16)
            act[at, to] = value.T.astype(bf16)
            pre_two[to, at] = pre


def two_slope(pre, out):
    cut = min(128, pre.shape[0])
    for c in range(0, pre.shape[0], cut):
        out[c : c + cut] = gelu_slope(pre[c : c + cut])


def divided(kept, bit):
    return [k for k in kept if not k & bit]


def three_home(act, *refs, n_third, orders, kept):
    thirds, own, outs = refs[:n_third], refs[n_third], refs[n_third + 1 :]
    rows = own.shape[0]
    mid, span = thirds[0].shape
    blocks = {k: slice(i * rows, (i + 1) * rows) for i, k in enumerate(kept)}
    half = own.shape[1] // 2
    step = math.gcd(span, half)
    for at in range(0, own.shape[1], step):
        left, right = thirds[at // span], thirds[n_third // 2 + at // span]
        cut = slice(at % span, at % span + step)
        total = dot(act[:, :mid], left[:, cut], 1, 0) + dot(act[:, mid:], right[:, cut], 1, 0)
        own[:, at : at + step] = total[blocks[0]]
        part = at // half
        keep, send = outs[2 * part], outs[2 * part + 1]
        put = slice(at - part * half, at - part * half + step)
        bit = orders[part][0]
        for i, k in enumerate(divided(kept, bit)):
            if k:
                keep[(i - 1) * rows : i * rows, put] = total[blocks[k]]
            send[i * rows : (i + 1) * rows, put] = total[blocks[k | bit]].astype(bf16)


def three_pass(own, *refs, stage, orders, kept):
    ins, new_own, outs = refs[:4], refs[4], refs[5:]
    rows = own.shape[0]
    half = own.shape[1] // 2
    for part, order in enumerate(orders):
        here = list(kept)
        for bit in order[:stage]:
            here = divided(here, bit)
        keep, got = ins[2 * part], ins[2 * part + 1]
        at = slice(part * half, (part + 1) * half)
        total = {}
        for i, k in enumerate(here):
            value = own[:, at] if k == 0 else keep[(i - 1) * rows : i * rows]
            total[k] = value + got[i * rows : (i + 1) * rows].astype(f32)
        new_own[:, at] = total[0]
        bit = order[stage]
        send = outs[2 * part + 1] if len(outs) == 4 else outs[part]
        for i, k in enumerate(divided(here, bit)):
            if k:
                outs[2 * part][(i - 1) * rows : i * rows] = total[k]
            send[i * rows : (i + 1) * rows] = total[k | bit].astype(bf16)


def error_step(number, wanted, wanted_too, fourth, *refs, widths, half, block, n_out):
    groups = len(widths)
    terms = refs[: 3 * groups]
    act, pre = refs[-2:]
    deltas, grad_four = refs[3 * groups : 5 * groups], refs[-3]
    start = 0
    spots = []
    for g, width in enumerate(widths):
        for part in range(2):
            at = slice(start, start + width)
            start += width
            spots.append(at)
            total = terms[3 * g][:, part * width : (part + 1) * width]
            total = total + terms[3 * g + 1 + part][...].astype(f32)
            pre[:, at] = total
            act[:, at] = gelu_act(total).astype(bf16)
    predicted = dot(fourth[...], act[...], 1, 1)
    mine = jnp.where(lax.axis_index("dp") >= half, 1, 0)
    wanted = wanted[mine] + wanted_too[mine]
    live = wanted[n_out : n_out + 1, :].astype(f32)
    error = (2.0 / (number[:, :1] * block) * (predicted - wanted.astype(f32)) * live).astype(bf16)
    row = lax.broadcasted_iota(jnp.int32, error.shape, 0)
    error = jnp.where(row < n_out, error, jnp.zeros_like(error))
    grad_four[...] = dot(error, act[...], 1, 0)
    turned = error.astype(f32).T.astype(bf16)
    for at, delta in zip(spots, deltas):
        value = dot(turned, fourth[:, at], 1, 0) * gelu_slope(pre[:, at])
        delta[...] = value.astype(bf16)


def join(own, got, out):
    rows = own.shape[0]
    out[:rows] = own[...]
    out[rows:] = got[...]


def lay(*refs, axis):
    out, at = refs[-1], 0
    for value in refs[:-1]:
        to = at + value.shape[axis]
        if axis:
            out[:, at:to] = value[...]
        else:
            out[at:to] = value[...]
        at = to


def join_all(*refs, held, evens, rows):
    out = refs[-1]
    half = out.shape[1] // 2
    for i, blocks in enumerate(held):
        for j, k in enumerate(blocks):
            to = evens.index(k) * rows
            at = slice(i // 2 * half, (i // 2 + 1) * half)
            out[to : to + rows, at] = refs[i][j * rows : (j + 1) * rows]


def three_away(act_t, whole, away):
    mid = act_t.shape[0] // 2
    away[...] = dot(act_t[mid:], whole[...], 1, 0).astype(bf16)


def three_own(act_t, whole, got, *grads):
    mid = act_t.shape[0] // 2
    span = grads[0].shape[1]
    for i, grad in enumerate(grads):
        at = slice(i * span, (i + 1) * span)
        value = dot(act_t[:mid], whole[:, at], 1, 0) + got[:, at].astype(f32)
        grad[...] = value.astype(grad.dtype)


def three_back(whole, *refs, n_third):
    thirds, before, sum_two = refs[:n_third], refs[n_third:-1], refs[-1]
    mid, span = thirds[0].shape
    for side in range(2):
        to = slice(side * mid, (side + 1) * mid)
        total = before[0][to] if before else None
        for i, third in enumerate(thirds[side * n_third // 2 : (side + 1) * n_third // 2]):
            term = dot(third[...], whole[:, i * span : (i + 1) * span], 1, 1)
            total = term if total is None else total + term
        sum_two[to] = total


def two_first(sum_two, slope, act_one, delta, away_far, away):
    value = (sum_two[...] * slope[...]).astype(bf16)
    delta[...] = value
    mid, near = delta.shape[0] // 2, away.shape[0]
    away_far[...] = dot(act_one[near:], value[mid:], 1, 1).astype(bf16)
    away[...] = dot(act_one[:near], value[mid:], 1, 1).astype(bf16)


def two_own(delta, act_one, got, *grads, start):
    mid, span = delta.shape[0] // 2, grads[0].shape[0]
    for i, grad in enumerate(grads):
        at = slice(i * span, (i + 1) * span)
        rows = slice(start + i * span, start + (i + 1) * span)
        value = dot(act_one[rows], delta[:mid], 1, 1) + got[at].astype(f32)
        grad[...] = value.astype(grad.dtype)


def split_dp(parts, step, keep, send):
    bit = (lax.axis_index("dp") & step) != 0
    for i in range(len(parts) // 2):
        even, odd = parts[2 * i], parts[2 * i + 1]
        keep[i] = jnp.where(bit, odd, even)
        send[i] = jnp.where(bit, even, odd).astype(bf16)


def one_back(
    inputs, delta, slope, slope_more, grad_four, near, far, near_too, far_too, keep, send, *, n_dp, places, n_in, n_out
):
    span = far.shape[0]
    n_mp = near.shape[0] // span + 1
    wide = span // n_dp
    mid = delta.shape[0] // 2
    whole = []
    for k in range(n_mp):
        at = slice(k * span, (k + 1) * span)
        left, right = (near[at], near_too[at]) if k + 1 < n_mp else (far[...], far_too[...])
        value = dot(left, delta[:mid], 1, 0) + dot(right, delta[mid:], 1, 0)
        source, row = (slope, k * span) if 2 * k < n_mp else (slope_more, (k - n_mp // 2) * span)
        value = (value * source[row : row + span].astype(f32)).astype(bf16)
        grad_one = dot(inputs[...], value, 1, 1)
        at = places.index(k) * span
        pieces = [grad_one[:n_in], grad_four[:n_out, at : at + span]]
        spare = keep.shape[1] - n_in - n_out
        if spare:
            pieces.append(jnp.zeros((spare, span), f32))
        whole.append(jnp.concatenate(pieces, 0))
    parts = [
        jnp.concatenate([value[:, d * wide : (d + 1) * wide] for value in whole], 1)
        for d in range(n_dp)
    ]
    split_dp(parts, 1, keep, send)


def halve(own, got, keep, send, *, step):
    split_dp([own[i] + got[i].astype(f32) for i in range(own.shape[0])], step, keep, send)


def last_half(own, got, keep, send):
    total = own[0] + got[0].astype(f32)
    wide = keep.shape[1]
    keep[...] = total[:, :wide]
    send[...] = total[:, wide:].astype(bf16)


def last_half_mp(own, got, keep, send):
    total = own[...] + got[...].astype(f32)
    wide = keep.shape[1]
    keep[...] = total[:, :wide]
    send[...] = total[:, wide:].astype(bf16)


def add_up(own, got, out):
    out[...] = (own[...].astype(f32) + got[...].astype(f32)).astype(out.dtype)


def update_small(own, *refs):
    gots, (w_in, w_out, m_in, m_out), outs = refs[:-8], refs[-8:-4], refs[-4:]
    nw_in, nw_out, nm_in, nm_out = outs
    total = own[...]
    for got in gots:
        total = total + got[...].astype(f32)
    n_in, n_out = w_in.shape[0], w_out.shape[0]
    mom = momentum_decay * m_in[...] + total[:n_in]
    nm_in[...] = mom
    nw_in[...] = w_in[...] - learn_rate * mom
    mom = momentum_decay * m_out[...] + total[n_in : n_in + n_out]
    nm_out[...] = mom
    nw_out[...] = w_out[...] - learn_rate * mom


def update_big(weight, moment, own, *refs):
    gots, (new_weight, new_moment) = refs[:-2], refs[-2:]
    total = own[...]
    for got in gots:
        total = total + got[...].astype(f32)
    mom = momentum_decay * moment[...] + total
    new_moment[...] = mom
    new_weight[...] = weight[...] - learn_rate * mom


def after(first, *values):
    return lax.optimization_barrier((first, *values))[1:]


def laid(values, axis):
    shape = list(values[0].shape)
    shape[axis] *= len(values)
    return on_core(functools.partial(lay, axis=axis), shaped(tuple(shape), bf16), values, "lay")


def gathered(own, n_mp):
    held = {0: own}
    for k in [k for k in range(1, n_mp) if parent(k) == 0][::-1]:
        held[k] = swap(own, "mp", k)
    return held


def passed_on(held, n_mp, ready):
    for k in sorted((k for k in range(1, n_mp) if parent(k) and k not in held), key=lambda k: -low_bit(k)):
        held[k] = swap(after(ready, held[parent(k)])[0], "mp", low_bit(k))


def summed(held, ks):
    gots = []
    for k in sorted((k for k in ks if k), key=lambda k: (low_bit(k), -k)):
        got = swap(held[k], "mp", low_bit(k))
        to = parent(k)
        if to:
            held[to] = on_core(add_up, shaped(got.shape, bf16), [held[to], got], "add_up")
        else:
            gots.append(got)
    return gots


def on_device(
    samples,
    targets,
    counts,
    weight_in,
    weight_mid,
    weight_top,
    weight_out,
    moment_in,
    moment_mid,
    moment_top,
    moment_out,
):
    slots, n_in, block = samples.shape
    n_out = targets.shape[1]
    n_dp, n_mp = lax.axis_size("dp"), lax.axis_size("mp")
    half = n_dp // 2
    per = slots // n_mp
    rows = per * block // 2
    n_rows = half * rows
    wide = weight_in.shape[1]
    lanes = max(rows, 2 * wide)
    tall = up_to(max(n_in, n_out) + 1, 16)
    hidden = wide * n_dp
    width = hidden * n_mp
    n_mid, n_top = weight_mid.shape[1], weight_top.shape[1]
    planes = range(n_mp)
    groups = [list(planes[:-1]), [n_mp - 1]]
    places = [k for ks in groups for k in ks]
    part = functools.partial

    piece = on_core(
        part(pack_small, tall=tall), shaped((tall, lanes), bf16), [weight_in, weight_out.T], "pack_small"
    )
    second = gathered(weight_mid.astype(bf16), n_mp)
    picked, wanted = on_core(
        part(pick_rows, tall=tall, rows=rows, per=per),
        [shaped((2 * tall, lanes), bf16), shaped((2, tall, rows), bf16)],
        [samples, targets],
        "pick_rows",
        scalars=[counts],
    )
    pieces = [piece] + [swap(piece, "mp", k) for k in planes[1:]]
    top = after((picked, pieces), weight_top.astype(bf16))[0]
    third = gathered(top, n_mp)
    early = [second[k] for k in planes if k and not parent(k)]
    passed_on(second, n_mp, (picked, pieces))

    packed = on_core(
        pack_all,
        shaped(((2 + n_mp) * tall, lanes), bf16),
        [picked, *after(early, *pieces)],
        "pack_all",
    )
    wanted = [wanted, swap(wanted, "dp", half)]
    held = lax.all_gather(packed, "dp")
    inputs, first, fourth, number = on_core(
        part(place_small, n_in=n_in, tall=tall, rows=rows, wide=wide, places=places),
        [
            shaped((tall, n_rows), bf16),
            shaped((tall, width), bf16),
            shaped((tall, width), bf16),
            shaped((1, lanes), f32),
        ],
        [held],
        "place_small",
    )

    act_one = on_core(
        part(one_forward, tile=256), shaped((width, n_rows), bf16), [inputs, first], "one_forward"
    )
    wide_mid = 2 * n_mid
    near = laid(after((picked, pieces), *[second[k] for k in planes[:-1]]), 0)
    third_early = [third[k] for k in planes if k and not parent(k)]
    far = after((act_one, third_early, wanted[1]), second[n_mp - 1])[0]
    second_all = [near, far, swap(near, "dp", 1), swap(far, "dp", 1)]
    act_two, act_two_t, pre_two = on_core(
        two_forward,
        [shaped((n_rows, wide_mid), bf16), shaped((wide_mid, n_rows), bf16), shaped((wide_mid, n_rows), f32)],
        [act_one, *second_all],
        "two_forward",
    )
    passed_on(third, n_mp - 1, act_two)
    third_all = []
    evens = list(range(0, n_dp, 2))
    bits = [1 << i for i in range(1, n_dp.bit_length() - 1)]
    orders = [bits, bits[::-1]]
    slopes = [
        on_core(
            part(one_slope, tile=256, start=start),
            shaped((width // 2, n_rows), bf16),
            [inputs, first],
            "one_slope",
            flops=6_000_000_000,
        )
        for start in (0, width // 2)
    ]
    slope_two = on_core(two_slope, shaped((wide_mid, n_rows), f32), [pre_two], "two_slope")
    terms = []
    ahead = [third[k] for k in planes if k and not parent(k)]
    for ks in groups:
        cols = len(ks) * n_top
        ready = (act_one, slopes[0]) if n_mp - 1 in ks else act_one
        third_too = [swap(after(ready, third[k])[0] if k else top, "dp", 1) for k in ks]
        third_all.append([third[k] for k in ks] + third_too)
        weights = after(ahead, *third_all[-1])
        left = half // 2
        kinds = [shaped(((left - 1) * rows, cols // 2), f32), shaped((left * rows, cols // 2), bf16)]
        own, *halves = on_core(
            part(three_home, n_third=len(weights), orders=orders, kept=evens),
            [shaped((rows, cols), f32)] + kinds * 2,
            [act_two, *weights],
            "three_home",
        )
        passed_on(third, n_mp, halves)
        ahead = []
        for stage in range(len(bits)):
            sends = halves[1::2] if len(halves) == 4 else halves
            gots = [swap(send, "dp", order[stage]) for send, order in zip(sends, orders)]
            ahead = ahead or [slopes[1], slope_two]
            if stage + 1 == len(bits):
                break
            keeps, left = halves[::2], left // 2
            kinds = [shaped((left * rows, cols // 2), bf16)]
            if left > 1:
                kinds = [shaped(((left - 1) * rows, cols // 2), f32)] + kinds
            own, *halves = on_core(
                part(three_pass, stage=stage + 1, orders=orders, kept=evens),
                [shaped((rows, cols), f32)] + kinds * 2,
                [own, keeps[0], gots[0], keeps[1], gots[1]],
                "three_pass",
            )
        terms += [own, *gots]
    *deltas, grad_four = on_core(
        part(error_step, widths=[len(ks) * n_top // 2 for ks in groups], half=half, block=block, n_out=n_out),
        [shaped((rows, len(ks) * n_top // 2), bf16) for ks in groups for _ in range(2)]
        + [shaped((tall, width), f32)],
        [number, *wanted, fourth, *terms],
        "error_step",
        scratch=[pltpu.VMEM((rows, width), bf16), pltpu.VMEM((rows, width), f32)],
    )

    sum_two, grad_three = None, {}
    gathers = {}
    for g in reversed(range(len(groups))):
        held, kinds = [[0], [0]], []
        arrays = list(deltas[2 * g : 2 * g + 2])
        cols = arrays[0].shape[1]
        for stage in range(len(bits)):
            last = stage + 1 == len(bits)
            gots = [swap(value, "dp", order[stage]) for value, order in zip(arrays, orders)]
            more = [[k | order[stage] for k in blocks] for blocks, order in zip(held, orders)]
            if last:
                break
            held = [a + b for a, b in zip(held, more)]
            arrays = [
                on_core(join, shaped((len(blocks) * rows, cols), bf16), [own, got], "join")
                for blocks, own, got in zip(held, arrays, gots)
            ]
            gathers[g, stage] = gots
        gathers[g] = (arrays, gots, [held[0], more[0], held[1], more[1]])
    for g in reversed(range(len(groups))):
        ks, carried = groups[g], sum_two is not None
        arrays, gots, blocks = gathers[g]
        if carried:
            gots = after((sum_two, got_far), *gots)
        elif (0, 0) in gathers:
            gots = after(gathers[0, 0], *gots)
        whole = on_core(
            part(join_all, held=blocks, evens=evens, rows=rows),
            shaped((n_rows, len(ks) * n_top), bf16),
            [arrays[0], gots[0], arrays[1], gots[1]],
            "join_all",
        )
        away = on_core(
            three_away, shaped((n_mid, len(ks) * n_top), bf16), [act_two_t, whole], "three_away"
        )
        away = swap(away, "dp", 1)
        sum_two = on_core(
            part(three_back, n_third=2 * len(ks)),
            shaped((wide_mid, n_rows), f32),
            [whole, *third_all[g]] + ([sum_two] if carried else []),
            "three_back",
        )
        grads = on_core(
            three_own,
            [shaped((n_mid, n_top), bf16 if k else f32) for k in ks],
            [act_two_t, whole, away],
            "three_own",
        )
        grad_three.update(zip(ks, grads))
        if not carried:
            got_far = swap(grads[0], "mp", 1)
    far = n_mp - 1
    grad_three[far - 1] = on_core(
        add_up, shaped(got_far.shape, bf16), [grad_three[far - 1], got_far], "add_up"
    )
    delta_two, away_far, away = on_core(
        two_first,
        [
            shaped((wide_mid, n_rows), bf16),
            shaped((hidden, n_mid), bf16),
            shaped((far * hidden, n_mid), bf16),
        ],
        [sum_two, slope_two, act_one],
        "two_first",
        flops=LONG,
    )
    (farthest,) = on_core(
        part(two_own, start=far * hidden),
        [shaped((hidden, n_mid), bf16)],
        [delta_two, act_one, swap(away_far, "dp", 1)],
        "two_own",
    )
    grads = on_core(
        part(two_own, start=0),
        [shaped((hidden, n_mid), bf16 if k else f32) for k in planes[:-1]],
        [delta_two, act_one, swap(away, "dp", 1)],
        "two_own",
    )
    grad_two = dict(zip(planes, [*grads, farthest]))
    got = swap(grad_two[far], "mp", 1)
    grad_two[far - 1] = on_core(add_up, shaped(got.shape, bf16), [grad_two[far - 1], got], "add_up")
    grad_two[1], grad_three[1] = after(grad_two[far - 1], grad_two[1], grad_three[1])
    gots_two = summed(grad_two, planes[:far])
    gots_three = summed(grad_three, planes[:far])[::-1]
    like = lambda value: shaped(value.shape, f32)
    new_top, mom_top = on_core(
        update_big, [like(weight_top)] * 2, [weight_top, moment_top, grad_three[0], *gots_three], "update_top",
        flops=2_000_000_000,
    )
    n_small = up_to(n_in + n_out, 16)
    shape = (half, n_small, n_mp * wide)
    keep, send = on_core(
        part(one_back, n_dp=n_dp, places=places, n_in=n_in, n_out=n_out),
        [shaped(shape, f32), shaped(shape, bf16)],
        [inputs, delta_two, *slopes, grad_four, *second_all],
        "one_back",
        flops=LONG,
    )
    step = 1
    while step < half:
        got = swap(send, "dp", step)
        if step == 2:
            got = after(gots_three[0], got)[0]
        step *= 2
        shape = (shape[0] // 2, *shape[1:])
        keep, send = on_core(
            part(halve, step=step), [shaped(shape, f32), shaped(shape, bf16)], [keep, got], "halve"
        )
    got = swap(send, "dp", step)
    half_mp = n_mp // 2 * wide
    keep, send = on_core(
        last_half,
        [shaped((n_small, half_mp), f32), shaped((n_small, half_mp), bf16)],
        [keep, got],
        "last_half",
    )
    step = n_mp // 2
    while step:
        got = swap(send, "mp", step)
        step //= 2
        if step:
            got = after((gots_two, mom_top), got)[0]
        if step:
            half_mp = step * wide
            keep, send = on_core(
                last_half_mp,
                [shaped((n_small, half_mp), f32), shaped((n_small, half_mp), bf16)],
                [keep, got],
                "last_half_mp",
            )
    gots_small = [got]

    flat = (weight_in, weight_out.T, moment_in, moment_out.T)
    new_in, new_out, mom_in, mom_out = on_core(
        update_small, [like(value) for value in flat], [keep, *gots_small, *flat], "update_small"
    )
    new_mid, mom_mid = on_core(
        update_big, [like(weight_mid)] * 2, [weight_mid, moment_mid, grad_two[0], *gots_two], "update_mid"
    )
    return (new_in, new_mid, new_top, new_out.T, mom_in, mom_mid, mom_top, mom_out.T)


def solution(mesh):
    in_specs = (
        P("dp", None, None),
        P("dp", None, None),
        P("dp"),
        P(None, ("mp", "dp")),
        P("mp", "dp"),
        P("dp", "mp"),
        P(("mp", "dp"), None),
        P(None, ("mp", "dp")),
        P("mp", "dp"),
        P("dp", "mp"),
        P(("mp", "dp"), None),
    )
    out_specs = (
        P(None, ("mp", "dp")),
        P("mp", "dp"),
        P("dp", "mp"),
        P(("mp", "dp"), None),
        P(None, ("mp", "dp")),
        P("mp", "dp"),
        P("dp", "mp"),
        P(("mp", "dp"), None),
    )
    return jax.shard_map(
        on_device, mesh=mesh, in_specs=in_specs, out_specs=out_specs, check_vma=False
    )
```

```python
import functools
import math

import jax
import jax.numpy as jnp
from jax import lax
from jax.experimental import pallas as pl
from jax.experimental.pallas import tpu as pltpu
from jax.sharding import PartitionSpec as P

momentum_decay = 0.9
learn_rate = 0.05
bf16 = jnp.bfloat16
f32 = jnp.float32
VMEM_BYTES = 24 << 20
LONG = 100_000_000_000


def swap(value, axis, step):
    count = lax.axis_size(axis)
    return lax.ppermute(value, axis, [(at, at ^ step) for at in range(count)])


def parent(k):
    return k & (k - 1)


def low_bit(k):
    return k & -k


def up_to(value, unit):
    return -(-value // unit) * unit


def gelu_act(value):
    return 0.5 * value * (1.0 + lax.erf(value * math.sqrt(0.5)))


def gelu_slope(value):
    return 0.5 * (1.0 + lax.erf(value * math.sqrt(0.5))) + value * jnp.exp(
        -0.5 * value * value
    ) * (1.0 / math.sqrt(2.0 * math.pi))


def dot(left, right, at_left, at_right):
    dims = (((at_left,), (at_right,)), ((), ()))
    return lax.dot_general(left, right, dims, preferred_element_type=f32)


def shaped(dims, kind):
    return jax.ShapeDtypeStruct(dims, kind)


def on_core(body, outs, args, name, flops=0, scratch=(), scalars=()):
    at = pl.BlockSpec(memory_space=pltpu.VMEM)
    return pl.pallas_call(
        body,
        out_shape=outs,
        in_specs=[pl.BlockSpec(memory_space=pltpu.SMEM)] * len(scalars) + [at] * len(args),
        out_specs=jax.tree.map(lambda _: at, outs),
        scratch_shapes=list(scratch),
        compiler_params=pltpu.CompilerParams(vmem_limit_bytes=VMEM_BYTES),
        cost_estimate=pl.CostEstimate(flops=flops, bytes_accessed=0, transcendentals=0),
        name=name,
    )(*scalars, *args)


def pack_small(w_in, w_out, out, *, tall):
    n_in, wide = w_in.shape
    n_out = w_out.shape[0]
    left = jnp.concatenate([w_in[...], jnp.zeros((tall - n_in, wide), f32)], 0)
    right = jnp.concatenate([w_out[...], jnp.zeros((tall - n_out, wide), f32)], 0)
    parts = [left, right]
    spare = out.shape[1] - 2 * wide
    if spare:
        parts.append(jnp.zeros((tall, spare), f32))
    out[...] = jnp.concatenate(parts, 1).astype(bf16)


def pick_rows(count, samples, targets, out, wanted, *, tall, rows, per):
    slots, n_in, block = samples.shape
    n_out = targets.shape[1]
    half = lax.axis_size("dp") // 2
    high = lax.axis_index("dp") >= half
    xs, ys = [], []
    for j in range(per):
        at = per * lax.axis_index("mp") + j
        slot = jnp.where(high, slots - 1 - at, at)
        keep = slot < count[0]
        for source, last, all_of in (
            (samples, jnp.full((1, block), count[0].astype(f32)), xs),
            (targets, jnp.full((1, block), keep.astype(f32)), ys),
        ):
            value = source[slot].astype(f32)
            parts = [jnp.where(keep, value, jnp.zeros_like(value)), last]
            spare = tall - value.shape[0] - 1
            if spare:
                parts.append(jnp.zeros((spare, block), f32))
            all_of.append(jnp.concatenate(parts, 0).astype(bf16))
    x = jnp.concatenate(xs, 1) if per > 1 else xs[0]
    y = jnp.concatenate(ys, 1) if per > 1 else ys[0]
    spare = out.shape[1] - rows
    for t in range(2):
        at = slice(t * rows, (t + 1) * rows)
        half_x = x[:, at]
        if spare:
            half_x = jnp.concatenate([half_x, jnp.zeros((tall, spare), bf16)], 1)
        out[tall * t : tall * (t + 1)] = half_x
        wanted[t] = y[:, at]


def pack_all(*refs):
    out, at = refs[-1], 0
    for part in refs[:-1]:
        out[at : at + part.shape[0]] = part[...]
        at += part.shape[0]


def place_small(held, inputs, first, fourth, number, *, n_in, tall, rows, wide, places):
    n_dp, n_mp = lax.axis_size("dp"), lax.axis_size("mp")
    half = n_dp // 2
    total = held[0, n_in : n_in + 1].astype(f32)
    for d in range(1, n_dp):
        total = total + held[d, n_in : n_in + 1].astype(f32)
    number[...] = total
    for place, k in enumerate(range(0, n_dp, 2)):
        at = lax.axis_index("dp") ^ k
        high = at >= half
        pair = jnp.where(high, at - half, at)
        both = held[pair, : 2 * tall] + held[pair + half, : 2 * tall]
        value = jnp.where(high, both[tall:], both[:tall])
        inputs[:, place * rows : (place + 1) * rows] = value[:, :rows]
    hidden = n_dp * wide
    for k in range(n_mp):
        row = slice((2 + k) * tall, (3 + k) * tall)
        pieces = [held[d, row] for d in range(n_dp)]
        at = slice(k * hidden, (k + 1) * hidden)
        first[:, at] = jnp.concatenate([piece[:, :wide] for piece in pieces], 1)
        at = slice(places.index(k) * hidden, (places.index(k) + 1) * hidden)
        fourth[:, at] = jnp.concatenate([piece[:, wide : 2 * wide] for piece in pieces], 1)


def one_forward(inputs, first, out, *, tile):
    n_rows = inputs.shape[1]
    cut = min(256, n_rows)

    def step(i, _):
        at = pl.ds(pl.multiple_of(i * tile, tile), tile)
        weights = first[:, at].T
        for c in range(0, n_rows, cut):
            pre = dot(weights, inputs[:, c : c + cut], 1, 0)
            out[at, c : c + cut] = gelu_act(pre).astype(bf16)
        return 0

    lax.fori_loop(0, first.shape[1] // tile, step, 0)


def one_slope(inputs, first, out, *, tile, start):
    n_rows = inputs.shape[1]
    cut = min(256, n_rows)

    def step(i, _):
        at = pl.ds(pl.multiple_of(i * tile, tile), tile)
        weights = first[:, pl.ds(pl.multiple_of(start + i * tile, tile), tile)].T
        for c in range(0, n_rows, cut):
            pre = dot(weights, inputs[:, c : c + cut], 1, 0)
            out[at, c : c + cut] = gelu_slope(pre).astype(bf16)
        return 0

    lax.fori_loop(0, out.shape[0] // tile, step, 0)


def two_forward(act_one, near, far, near_too, far_too, act, act_t, pre_two):
    n_rows = act_one.shape[1]
    cut = min(256, n_rows)
    first, cols = near.shape
    for side, (left, right) in enumerate(((near, far), (near_too, far_too))):
        to = slice(side * cols, (side + 1) * cols)
        left, right = left[...].T, right[...].T
        for c in range(0, n_rows, cut):
            at = slice(c, c + cut)
            pre = dot(left, act_one[:first, at], 1, 0) + dot(right, act_one[first:, at], 1, 0)
            value = gelu_act(pre)
            act_t[to, at] = value.astype(bf16)
            act[at, to] = value.T.astype(bf16)
            pre_two[to, at] = pre


def two_slope(pre, out):
    cut = min(128, pre.shape[0])
    for c in range(0, pre.shape[0], cut):
        out[c : c + cut] = gelu_slope(pre[c : c + cut])


def divided(kept, bit):
    return [k for k in kept if not k & bit]


def three_home(act, *refs, n_third, orders, kept):
    thirds, own, outs = refs[:n_third], refs[n_third], refs[n_third + 1 :]
    rows = own.shape[0]
    mid, span = thirds[0].shape
    blocks = {k: slice(i * rows, (i + 1) * rows) for i, k in enumerate(kept)}
    half = own.shape[1] // 2
    step = math.gcd(span, half)
    for at in range(0, own.shape[1], step):
        left, right = thirds[at // span], thirds[n_third // 2 + at // span]
        cut = slice(at % span, at % span + step)
        total = dot(act[:, :mid], left[:, cut], 1, 0) + dot(act[:, mid:], right[:, cut], 1, 0)
        own[:, at : at + step] = total[blocks[0]]
        part = at // half
        keep, send = outs[2 * part], outs[2 * part + 1]
        put = slice(at - part * half, at - part * half + step)
        bit = orders[part][0]
        for i, k in enumerate(divided(kept, bit)):
            if k:
                keep[(i - 1) * rows : i * rows, put] = total[blocks[k]]
            send[i * rows : (i + 1) * rows, put] = total[blocks[k | bit]].astype(bf16)


def three_pass(own, *refs, stage, orders, kept):
    ins, new_own, outs = refs[:4], refs[4], refs[5:]
    rows = own.shape[0]
    half = own.shape[1] // 2
    for part, order in enumerate(orders):
        here = list(kept)
        for bit in order[:stage]:
            here = divided(here, bit)
        keep, got = ins[2 * part], ins[2 * part + 1]
        at = slice(part * half, (part + 1) * half)
        total = {}
        for i, k in enumerate(here):
            value = own[:, at] if k == 0 else keep[(i - 1) * rows : i * rows]
            total[k] = value + got[i * rows : (i + 1) * rows].astype(f32)
        new_own[:, at] = total[0]
        bit = order[stage]
        send = outs[2 * part + 1] if len(outs) == 4 else outs[part]
        for i, k in enumerate(divided(here, bit)):
            if k:
                outs[2 * part][(i - 1) * rows : i * rows] = total[k]
            send[i * rows : (i + 1) * rows] = total[k | bit].astype(bf16)


def error_step(number, wanted, wanted_too, fourth, *refs, widths, half, block, n_out):
    groups = len(widths)
    terms = refs[: 3 * groups]
    act, pre = refs[-2:]
    deltas, grad_four = refs[3 * groups : 5 * groups], refs[-3]
    start = 0
    spots = []
    for g, width in enumerate(widths):
        for part in range(2):
            at = slice(start, start + width)
            start += width
            spots.append(at)
            total = terms[3 * g][:, part * width : (part + 1) * width]
            total = total + terms[3 * g + 1 + part][...].astype(f32)
            pre[:, at] = total
            act[:, at] = gelu_act(total).astype(bf16)
    predicted = dot(fourth[...], act[...], 1, 1)
    mine = jnp.where(lax.axis_index("dp") >= half, 1, 0)
    wanted = wanted[mine] + wanted_too[mine]
    live = wanted[n_out : n_out + 1, :].astype(f32)
    error = (2.0 / (number[:, :1] * block) * (predicted - wanted.astype(f32)) * live).astype(bf16)
    row = lax.broadcasted_iota(jnp.int32, error.shape, 0)
    error = jnp.where(row < n_out, error, jnp.zeros_like(error))
    grad_four[...] = dot(error, act[...], 1, 0)
    turned = error.astype(f32).T.astype(bf16)
    for at, delta in zip(spots, deltas):
        value = dot(turned, fourth[:, at], 1, 0) * gelu_slope(pre[:, at])
        delta[...] = value.astype(bf16)


def join(own, got, out):
    rows = own.shape[0]
    out[:rows] = own[...]
    out[rows:] = got[...]


def lay(*refs, axis):
    out, at = refs[-1], 0
    for value in refs[:-1]:
        to = at + value.shape[axis]
        if axis:
            out[:, at:to] = value[...]
        else:
            out[at:to] = value[...]
        at = to


def join_all(*refs, held, evens, rows):
    out = refs[-1]
    half = out.shape[1] // 2
    for i, blocks in enumerate(held):
        for j, k in enumerate(blocks):
            to = evens.index(k) * rows
            at = slice(i // 2 * half, (i // 2 + 1) * half)
            out[to : to + rows, at] = refs[i][j * rows : (j + 1) * rows]


def three_away(act_t, whole, away):
    mid = act_t.shape[0] // 2
    away[...] = dot(act_t[mid:], whole[...], 1, 0).astype(bf16)


def three_own(act_t, whole, got, *grads):
    mid = act_t.shape[0] // 2
    span = grads[0].shape[1]
    for i, grad in enumerate(grads):
        at = slice(i * span, (i + 1) * span)
        value = dot(act_t[:mid], whole[:, at], 1, 0) + got[:, at].astype(f32)
        grad[...] = value.astype(grad.dtype)


def three_back(whole, *refs, n_third):
    thirds, before, sum_two = refs[:n_third], refs[n_third:-1], refs[-1]
    mid, span = thirds[0].shape
    for side in range(2):
        to = slice(side * mid, (side + 1) * mid)
        total = before[0][to] if before else None
        for i, third in enumerate(thirds[side * n_third // 2 : (side + 1) * n_third // 2]):
            term = dot(third[...], whole[:, i * span : (i + 1) * span], 1, 1)
            total = term if total is None else total + term
        sum_two[to] = total


def two_first(sum_two, slope, act_one, delta, away):
    value = (sum_two[...] * slope[...]).astype(bf16)
    delta[...] = value
    mid = delta.shape[0] // 2
    away[...] = dot(act_one[act_one.shape[0] - away.shape[0] :], value[mid:], 1, 1).astype(bf16)


def two_away(delta, act_one, away):
    mid = delta.shape[0] // 2
    away[...] = dot(act_one[: away.shape[0]], delta[mid:], 1, 1).astype(bf16)


def two_own(delta, act_one, got, *grads, start):
    mid, span = delta.shape[0] // 2, grads[0].shape[0]
    for i, grad in enumerate(grads):
        at = slice(i * span, (i + 1) * span)
        rows = slice(start + i * span, start + (i + 1) * span)
        value = dot(act_one[rows], delta[:mid], 1, 1) + got[at].astype(f32)
        grad[...] = value.astype(grad.dtype)


def split_dp(parts, step, keep, send):
    bit = (lax.axis_index("dp") & step) != 0
    for i in range(len(parts) // 2):
        even, odd = parts[2 * i], parts[2 * i + 1]
        keep[i] = jnp.where(bit, odd, even)
        send[i] = jnp.where(bit, even, odd).astype(bf16)


def one_back(
    inputs, delta, slope, slope_more, grad_four, near, far, near_too, far_too, keep, send, *, n_dp, places, n_in, n_out
):
    span = far.shape[0]
    n_mp = near.shape[0] // span + 1
    wide = span // n_dp
    mid = delta.shape[0] // 2
    whole = []
    for k in range(n_mp):
        at = slice(k * span, (k + 1) * span)
        left, right = (near[at], near_too[at]) if k + 1 < n_mp else (far[...], far_too[...])
        value = dot(left, delta[:mid], 1, 0) + dot(right, delta[mid:], 1, 0)
        source, row = (slope, k * span) if 2 * k < n_mp else (slope_more, (k - n_mp // 2) * span)
        value = (value * source[row : row + span].astype(f32)).astype(bf16)
        grad_one = dot(inputs[...], value, 1, 1)
        at = places.index(k) * span
        pieces = [grad_one[:n_in], grad_four[:n_out, at : at + span]]
        spare = keep.shape[1] - n_in - n_out
        if spare:
            pieces.append(jnp.zeros((spare, span), f32))
        whole.append(jnp.concatenate(pieces, 0))
    parts = [
        jnp.concatenate([value[:, d * wide : (d + 1) * wide] for value in whole], 1)
        for d in range(n_dp)
    ]
    split_dp(parts, 1, keep, send)


def halve(own, got, keep, send, *, step):
    split_dp([own[i] + got[i].astype(f32) for i in range(own.shape[0])], step, keep, send)


def last_half(own, got, keep, send):
    total = own[0] + got[0].astype(f32)
    wide = keep.shape[1]
    keep[...] = total[:, :wide]
    send[...] = total[:, wide:].astype(bf16)


def last_half_mp(own, got, keep, send):
    total = own[...] + got[...].astype(f32)
    wide = keep.shape[1]
    keep[...] = total[:, :wide]
    send[...] = total[:, wide:].astype(bf16)


def add_up(own, got, out):
    out[...] = (own[...].astype(f32) + got[...].astype(f32)).astype(out.dtype)


def update_small(own, *refs):
    gots, (w_in, w_out, m_in, m_out), outs = refs[:-8], refs[-8:-4], refs[-4:]
    nw_in, nw_out, nm_in, nm_out = outs
    total = own[...]
    for got in gots:
        total = total + got[...].astype(f32)
    n_in, n_out = w_in.shape[0], w_out.shape[0]
    mom = momentum_decay * m_in[...] + total[:n_in]
    nm_in[...] = mom
    nw_in[...] = w_in[...] - learn_rate * mom
    mom = momentum_decay * m_out[...] + total[n_in : n_in + n_out]
    nm_out[...] = mom
    nw_out[...] = w_out[...] - learn_rate * mom


def update_big(weight, moment, own, *refs):
    gots, (new_weight, new_moment) = refs[:-2], refs[-2:]
    total = own[...]
    for got in gots:
        total = total + got[...].astype(f32)
    mom = momentum_decay * moment[...] + total
    new_moment[...] = mom
    new_weight[...] = weight[...] - learn_rate * mom


def after(first, *values):
    return lax.optimization_barrier((first, *values))[1:]


def laid(values, axis):
    shape = list(values[0].shape)
    shape[axis] *= len(values)
    return on_core(functools.partial(lay, axis=axis), shaped(tuple(shape), bf16), values, "lay")


def gathered(own, n_mp):
    held = {0: own}
    for k in [k for k in range(1, n_mp) if parent(k) == 0][::-1]:
        held[k] = swap(own, "mp", k)
    return held


def passed_on(held, n_mp, ready):
    for k in sorted((k for k in range(1, n_mp) if parent(k) and k not in held), key=lambda k: -low_bit(k)):
        held[k] = swap(after(ready, held[parent(k)])[0], "mp", low_bit(k))


def summed(held, ks):
    gots = []
    for k in sorted((k for k in ks if k), key=lambda k: (low_bit(k), -k)):
        got = swap(held[k], "mp", low_bit(k))
        to = parent(k)
        if to:
            held[to] = on_core(add_up, shaped(got.shape, bf16), [held[to], got], "add_up")
        else:
            gots.append(got)
    return gots


def on_device(
    samples,
    targets,
    counts,
    weight_in,
    weight_mid,
    weight_top,
    weight_out,
    moment_in,
    moment_mid,
    moment_top,
    moment_out,
):
    slots, n_in, block = samples.shape
    n_out = targets.shape[1]
    n_dp, n_mp = lax.axis_size("dp"), lax.axis_size("mp")
    half = n_dp // 2
    per = slots // n_mp
    rows = per * block // 2
    n_rows = half * rows
    wide = weight_in.shape[1]
    lanes = max(rows, 2 * wide)
    tall = up_to(max(n_in, n_out) + 1, 16)
    hidden = wide * n_dp
    width = hidden * n_mp
    n_mid, n_top = weight_mid.shape[1], weight_top.shape[1]
    planes = range(n_mp)
    groups = [list(planes[:-1]), [n_mp - 1]]
    places = [k for ks in groups for k in ks]
    part = functools.partial

    piece = on_core(
        part(pack_small, tall=tall), shaped((tall, lanes), bf16), [weight_in, weight_out.T], "pack_small"
    )
    second = gathered(weight_mid.astype(bf16), n_mp)
    picked, wanted = on_core(
        part(pick_rows, tall=tall, rows=rows, per=per),
        [shaped((2 * tall, lanes), bf16), shaped((2, tall, rows), bf16)],
        [samples, targets],
        "pick_rows",
        scalars=[counts],
    )
    pieces = [piece] + [swap(piece, "mp", k) for k in planes[1:]]
    top = after((picked, pieces), weight_top.astype(bf16))[0]
    third = gathered(top, n_mp)
    early = [second[k] for k in planes if k and not parent(k)]
    passed_on(second, n_mp, (picked, pieces))

    packed = on_core(
        pack_all,
        shaped(((2 + n_mp) * tall, lanes), bf16),
        [picked, *after(early, *pieces)],
        "pack_all",
    )
    wanted = [wanted, swap(wanted, "dp", half)]
    held = lax.all_gather(packed, "dp")
    inputs, first, fourth, number = on_core(
        part(place_small, n_in=n_in, tall=tall, rows=rows, wide=wide, places=places),
        [
            shaped((tall, n_rows), bf16),
            shaped((tall, width), bf16),
            shaped((tall, width), bf16),
            shaped((1, lanes), f32),
        ],
        [held],
        "place_small",
    )

    act_one = on_core(
        part(one_forward, tile=256), shaped((width, n_rows), bf16), [inputs, first], "one_forward"
    )
    wide_mid = 2 * n_mid
    near = laid(after((picked, pieces), *[second[k] for k in planes[:-1]]), 0)
    third_early = [third[k] for k in planes if k and not parent(k)]
    far = after((act_one, third_early, wanted[1]), second[n_mp - 1])[0]
    second_all = [near, far, swap(near, "dp", 1), swap(far, "dp", 1)]
    act_two, act_two_t, pre_two = on_core(
        two_forward,
        [shaped((n_rows, wide_mid), bf16), shaped((wide_mid, n_rows), bf16), shaped((wide_mid, n_rows), f32)],
        [act_one, *second_all],
        "two_forward",
    )
    passed_on(third, n_mp - 1, act_two)
    third_all = []
    evens = list(range(0, n_dp, 2))
    bits = [1 << i for i in range(1, n_dp.bit_length() - 1)]
    orders = [bits, bits[::-1]]
    slopes = [
        on_core(
            part(one_slope, tile=256, start=start),
            shaped((width // 2, n_rows), bf16),
            [inputs, first],
            "one_slope",
            flops=6_000_000_000,
        )
        for start in (0, width // 2)
    ]
    slope_two = on_core(two_slope, shaped((wide_mid, n_rows), f32), [pre_two], "two_slope")
    terms = []
    ahead = [third[k] for k in planes if k and not parent(k)]
    for ks in groups:
        cols = len(ks) * n_top
        ready = (act_one, slopes[0]) if n_mp - 1 in ks else act_one
        third_too = [swap(after(ready, third[k])[0] if k else top, "dp", 1) for k in ks]
        third_all.append([third[k] for k in ks] + third_too)
        weights = after(ahead, *third_all[-1])
        left = half // 2
        kinds = [shaped(((left - 1) * rows, cols // 2), f32), shaped((left * rows, cols // 2), bf16)]
        own, *halves = on_core(
            part(three_home, n_third=len(weights), orders=orders, kept=evens),
            [shaped((rows, cols), f32)] + kinds * 2,
            [act_two, *weights],
            "three_home",
        )
        passed_on(third, n_mp, halves)
        ahead = []
        for stage in range(len(bits)):
            sends = halves[1::2] if len(halves) == 4 else halves
            gots = [swap(send, "dp", order[stage]) for send, order in zip(sends, orders)]
            ahead = ahead or [slopes[1], slope_two]
            if stage + 1 == len(bits):
                break
            keeps, left = halves[::2], left // 2
            kinds = [shaped((left * rows, cols // 2), bf16)]
            if left > 1:
                kinds = [shaped(((left - 1) * rows, cols // 2), f32)] + kinds
            own, *halves = on_core(
                part(three_pass, stage=stage + 1, orders=orders, kept=evens),
                [shaped((rows, cols), f32)] + kinds * 2,
                [own, keeps[0], gots[0], keeps[1], gots[1]],
                "three_pass",
            )
        terms += [own, *gots]
    *deltas, grad_four = on_core(
        part(error_step, widths=[len(ks) * n_top // 2 for ks in groups], half=half, block=block, n_out=n_out),
        [shaped((rows, len(ks) * n_top // 2), bf16) for ks in groups for _ in range(2)]
        + [shaped((tall, width), f32)],
        [number, *wanted, fourth, *terms],
        "error_step",
        scratch=[pltpu.VMEM((rows, width), bf16), pltpu.VMEM((rows, width), f32)],
    )

    sum_two, grad_three = None, {}
    gathers = {}
    for g in reversed(range(len(groups))):
        held, kinds = [[0], [0]], []
        arrays = list(deltas[2 * g : 2 * g + 2])
        cols = arrays[0].shape[1]
        for stage in range(len(bits)):
            last = stage + 1 == len(bits)
            gots = [swap(value, "dp", order[stage]) for value, order in zip(arrays, orders)]
            more = [[k | order[stage] for k in blocks] for blocks, order in zip(held, orders)]
            if last:
                break
            held = [a + b for a, b in zip(held, more)]
            arrays = [
                on_core(join, shaped((len(blocks) * rows, cols), bf16), [own, got], "join")
                for blocks, own, got in zip(held, arrays, gots)
            ]
            gathers[g, stage] = gots
        gathers[g] = (arrays, gots, [held[0], more[0], held[1], more[1]])
    for g in reversed(range(len(groups))):
        ks, carried = groups[g], sum_two is not None
        arrays, gots, blocks = gathers[g]
        if carried:
            gots = after((sum_two, got_far), *gots)
        elif (0, 0) in gathers:
            gots = after(gathers[0, 0], *gots)
        whole = on_core(
            part(join_all, held=blocks, evens=evens, rows=rows),
            shaped((n_rows, len(ks) * n_top), bf16),
            [arrays[0], gots[0], arrays[1], gots[1]],
            "join_all",
        )
        away = on_core(
            three_away, shaped((n_mid, len(ks) * n_top), bf16), [act_two_t, whole], "three_away"
        )
        away = swap(away, "dp", 1)
        sum_two = on_core(
            part(three_back, n_third=2 * len(ks)),
            shaped((wide_mid, n_rows), f32),
            [whole, *third_all[g]] + ([sum_two] if carried else []),
            "three_back",
        )
        grads = on_core(
            three_own,
            [shaped((n_mid, n_top), bf16 if k else f32) for k in ks],
            [act_two_t, whole, away],
            "three_own",
        )
        grad_three.update(zip(ks, grads))
        if not carried:
            got_far = swap(grads[0], "mp", 1)
    far = n_mp - 1
    grad_three[far - 1] = on_core(
        add_up, shaped(got_far.shape, bf16), [grad_three[far - 1], got_far], "add_up"
    )
    delta_two, away_far = on_core(
        two_first,
        [shaped((wide_mid, n_rows), bf16), shaped((hidden, n_mid), bf16)],
        [sum_two, slope_two, act_one],
        "two_first",
        flops=LONG,
    )
    (farthest,) = on_core(
        part(two_own, start=far * hidden),
        [shaped((hidden, n_mid), bf16)],
        [delta_two, act_one, swap(away_far, "dp", 1)],
        "two_own",
    )
    away = on_core(
        two_away,
        shaped((far * hidden, n_mid), bf16),
        [after(farthest, delta_two)[0], act_one],
        "two_away",
    )
    grads = on_core(
        part(two_own, start=0),
        [shaped((hidden, n_mid), bf16 if k else f32) for k in planes[:-1]],
        [delta_two, act_one, swap(away, "dp", 1)],
        "two_own",
    )
    grad_two = dict(zip(planes, [*grads, farthest]))
    got = swap(grad_two[far], "mp", 1)
    grad_two[far - 1] = on_core(add_up, shaped(got.shape, bf16), [grad_two[far - 1], got], "add_up")
    grad_two[1], grad_three[1] = after(grad_two[far - 1], grad_two[1], grad_three[1])
    gots_two = summed(grad_two, planes[:far])
    gots_three = summed(grad_three, planes[:far])[::-1]
    like = lambda value: shaped(value.shape, f32)
    new_top, mom_top = on_core(
        update_big, [like(weight_top)] * 2, [weight_top, moment_top, grad_three[0], *gots_three], "update_top",
        flops=2_000_000_000,
    )
    n_small = up_to(n_in + n_out, 16)
    shape = (half, n_small, n_mp * wide)
    keep, send = on_core(
        part(one_back, n_dp=n_dp, places=places, n_in=n_in, n_out=n_out),
        [shaped(shape, f32), shaped(shape, bf16)],
        [inputs, delta_two, *slopes, grad_four, *second_all],
        "one_back",
        flops=LONG,
    )
    step = 1
    while step < half:
        got = swap(send, "dp", step)
        if step == 2:
            got = after(gots_three[0], got)[0]
        step *= 2
        shape = (shape[0] // 2, *shape[1:])
        keep, send = on_core(
            part(halve, step=step), [shaped(shape, f32), shaped(shape, bf16)], [keep, got], "halve"
        )
    got = swap(send, "dp", step)
    half_mp = n_mp // 2 * wide
    keep, send = on_core(
        last_half,
        [shaped((n_small, half_mp), f32), shaped((n_small, half_mp), bf16)],
        [keep, got],
        "last_half",
    )
    step = n_mp // 2
    while step:
        got = swap(send, "mp", step)
        step //= 2
        if step:
            got = after((gots_two, mom_top), got)[0]
        if step:
            half_mp = step * wide
            keep, send = on_core(
                last_half_mp,
                [shaped((n_small, half_mp), f32), shaped((n_small, half_mp), bf16)],
                [keep, got],
                "last_half_mp",
            )
    gots_small = [got]

    flat = (weight_in, weight_out.T, moment_in, moment_out.T)
    new_in, new_out, mom_in, mom_out = on_core(
        update_small, [like(value) for value in flat], [keep, *gots_small, *flat], "update_small"
    )
    new_mid, mom_mid = on_core(
        update_big, [like(weight_mid)] * 2, [weight_mid, moment_mid, grad_two[0], *gots_two], "update_mid"
    )
    return (new_in, new_mid, new_top, new_out.T, mom_in, mom_mid, mom_top, mom_out.T)


def solution(mesh):
    in_specs = (
        P("dp", None, None),
        P("dp", None, None),
        P("dp"),
        P(None, ("mp", "dp")),
        P("mp", "dp"),
        P("dp", "mp"),
        P(("mp", "dp"), None),
        P(None, ("mp", "dp")),
        P("mp", "dp"),
        P("dp", "mp"),
        P(("mp", "dp"), None),
    )
    out_specs = (
        P(None, ("mp", "dp")),
        P("mp", "dp"),
        P("dp", "mp"),
        P(("mp", "dp"), None),
        P(None, ("mp", "dp")),
        P("mp", "dp"),
        P("dp", "mp"),
        P(("mp", "dp"), None),
    )
    return jax.shard_map(
        on_device, mesh=mesh, in_specs=in_specs, out_specs=out_specs, check_vma=False
    )
```
